128 devices in a mesh: op: 16 (over z, x), sec: 8 (over y, core).
Axes of the slice: x: 4, y: 4, z: 4, core: 2. Of those that a mesh axis runs over, the one named last changes fastest.
Arguments:
- psi: bfloat16 [256, 128, 256], P('sec', 'op'), may hold values from -6 to 6
- left_env: bfloat16 [128, 256, 128, 128], P('op', 'sec'), may hold values from -0.5 to 0.5
- right_env: bfloat16 [128, 8, 256, 256], P('op', 'sec'), may hold values from -0.375 to 0.375
- source: int32 [128, 256], P('op', 'sec'), may hold values from 0 to 255, as said below
- coupling: int32 [128, 256], P('op', 'sec'), may hold values from 0 to 3
Outputs:
- sigma: bfloat16 [256, 128, 256], P('sec', 'op')
- renorm: float32 [128, 8, 256, 256], P(('op', 'sec'))
The draws below stay inside these ranges and needn't reach their ends.
Inputs may be any that keep to these rules, and one draw needn't show every extreme that they name: source[k, s] lies in the same aligned block of 32 sectors as s.
All inputs are finite; a program needn't handle non-finite values.
Results may differ from the reference program's by a relative error of at most 0.011.
Values may be sent and summed in bfloat16 or wider, within the bound.
A program may use at most 128 MiB of HBM per device.

```python
import jax
import jax.numpy as jnp
from jax import lax

B = 128
M = 256
S_DEV = 32
SECTORS = 256
GROUPS = 8
KOPS = 128


def draw_source(key, part):
    key = jax.random.fold_in(key, 7)
    offset = jax.random.randint(key, (KOPS, SECTORS), 0, S_DEV)
    column = jnp.arange(SECTORS, dtype=jnp.int32)
    return (column // S_DEV * S_DEV)[None, :] + offset


def plant(drawn, rng, least, high):
    spot = [jax.random.randint(jax.random.fold_in(rng, axis), (), 0, length) for axis, length in enumerate(drawn.shape)]
    main_axis = drawn.shape.index(max(drawn.shape))
    next_to = spot[:main_axis] + [(spot[main_axis] + 1) % drawn.shape[main_axis]] + spot[main_axis + 1:]
    return drawn.at[tuple(spot)].set(least).at[tuple(next_to)].set(high)


def steps_of(key, dims, split, low, high):
    gain = 1.0
    for axis_at, parts in split:
        steps = jax.random.uniform(jax.random.fold_in(jax.random.fold_in(key, 6), axis_at), (parts,), jnp.float32, low / len(split), high / len(split))
        gain = gain * jnp.repeat(jnp.exp(steps), dims[axis_at] // parts).reshape((-1,) + (1,) * (len(dims) - 1 - axis_at))
    return gain


def normal_values(own_key, extent, spread, limit, cuts=(), kind=jnp.bfloat16):
    entries = jax.random.normal(own_key, extent, jnp.float32) * spread
    if len(cuts) > 0:
        entries = steps_of(own_key, extent, cuts, -0.22, 0.18) * entries
    return jnp.clip(entries, min=-limit, max=limit).astype(kind)


def setup_inputs(seed: int = 0) -> dict:
    key_of = jax.random.split(jax.random.key(seed), 6)
    psi = normal_values(key_of[0], (SECTORS, B, M), 1.0, 6.0, ((0, 8), (1, 16)))
    left_env = normal_values(key_of[1], (KOPS, SECTORS, B, B), B ** -0.5, 0.5, ((0, 16), (1, 8)))
    right_env = normal_values(key_of[2], (KOPS, GROUPS, M, M), M ** -0.5, 0.375, ((0, 16), (1, 8)))
    source = draw_source(jax.random.fold_in(key_of[5], 71), 0)
    coupling = plant(jax.random.randint(key_of[4], (KOPS, SECTORS), 0, 4), jax.random.fold_in(key_of[4], 1), 0, 3).astype(jnp.int32)
    return {"psi": psi, "left_env": left_env, "right_env": right_env, "source": source, "coupling": coupling}


COEFS = (1.0, -0.5773503, 0.8164966, -0.7071068)


def reference(psi, left_env, right_env, source, coupling):
    table = jnp.array(COEFS, jnp.float32)
    coef = table[coupling]
    psi_wide = psi.astype(jnp.float32)
    psi_groups = psi_wide.reshape(GROUPS, S_DEV, B, M)

    def step(carry, inputs):
        env_k, src_k, coef_k, right_k = inputs
        picked = psi_wide[src_k]
        mixed = jnp.einsum("sab,sbm->sam", env_k.astype(jnp.float32), picked).astype(jnp.bfloat16)
        mixed_wide = mixed.astype(jnp.float32).reshape(GROUPS, S_DEV, B, M)
        image = jnp.einsum("gsam,gmn->gsan", mixed_wide, right_k.astype(jnp.float32)).reshape(SECTORS, B, M)
        carry = carry + coef_k[:, None, None] * image
        part = jnp.einsum("gsbm,gsbn->gmn", psi_groups, mixed_wide)
        return carry, part

    start = jnp.zeros((SECTORS, B, M), jnp.float32)
    total, renorm = lax.scan(step, start, (left_env, source, coef, right_env))
    sigma = (total * (KOPS ** -0.5)).astype(jnp.bfloat16)
    return sigma, renorm * ((S_DEV * B) ** -0.5)
```

```python
import functools

import jax
import jax.numpy as jnp
from jax import lax
from jax.experimental import pallas as pl
from jax.experimental.pallas import tpu as pltpu
from jax.sharding import PartitionSpec as P

COEFS = (1.0, -0.5773503, 0.8164966, -0.7071068)
MESH = pl.DeviceIdType.MESH
F32 = jnp.float32
BF16 = jnp.bfloat16
CHUNKS = 4


def turn(a, step):
    return lax.rem(a + step, 4)


def kernel(
    psi_ref, left_ref, right_ref, src_ref, cpl_ref,
    sig_ref, ren_ref,
    left, scaled, right, got, full, full_t, image, zed, parts, block,
    hop1, hop2, kept, hop3, hop4, relay,
    load_sem, send_sem, gather_sem, sum_sem, swap_sem, relay_sem, far_sem, own_sem,
    acc00, acc01, acc02, acc03, acc10, acc11, acc12, acc13,
):
    acc = ((acc00, acc01, acc02, acc03), (acc10, acc11, acc12, acc13))
    op, sec = lax.axis_index("op"), lax.axis_index("sec")
    z, x = op // 4, op % 4
    y, core = sec // 2, sec % 2
    coords = ((x, z), (z, x))

    loads = [
        pltpu.make_async_copy(psi_ref.at[pl.ds(h * 128, 128)], got.at[h, op], load_sem.at[h]) for h in range(2)
    ]
    loads.append(pltpu.make_async_copy(left_ref, left, load_sem.at[2]))
    loads.append(pltpu.make_async_copy(right_ref, right, load_sem.at[3]))
    for copy in loads:
        copy.start()

    barrier = pltpu.get_barrier_semaphore()
    peers = [(z * 4 + turn(x, 1), sec), (z * 4 + turn(x, 3), sec), (turn(z, 1) * 4 + x, sec), (turn(z, 3) * 4 + x, sec)]
    peers += [(op, lax.rem(sec + i, 8)) for i in range(1, 8)]
    for peer in peers:
        pl.semaphore_signal(barrier, inc=1, device_id=peer, device_id_type=MESH)
    pl.semaphore_wait(barrier, len(peers))

    sent = []

    def place(h, p, q):
        return q * 4 + p if h == 0 else p * 4 + q

    def at(h, dp, dq):
        p, q = coords[h]
        return place(h, turn(p, dp), turn(q, dq))

    def start(src, dst, recv_sem, target):
        copy = pltpu.make_async_remote_copy(
            src_ref=src, dst_ref=dst, send_sem=send_sem.at[len(sent)], recv_sem=recv_sem,
            device_id=(target, sec), device_id_type=MESH,
        )
        copy.start()
        sent.append(copy)

    def arrived(dst, recv_sem):
        pltpu.make_async_remote_copy(
            src_ref=dst, dst_ref=dst, send_sem=send_sem.at[0], recv_sem=recv_sem,
            device_id=(op, sec), device_id_type=MESH,
        ).wait_recv()

    def piece(h, dp, dq, half):
        ref = got.at[h, at(h, dp, dq)]
        return ref if half is None else ref.at[pl.ds(half * 64, 64)]

    def pass_on(h, dp, dq, half, sp, sq):
        ref = piece(h, dp, dq, half)
        rel = (dp - sp) % 4 * 4 + (dq - sq) % 4
        start(ref, ref, gather_sem.at[h, rel, 0 if half is None else half], at(h, sp % 4, sq % 4))

    def await_piece(h, dp, dq, half):
        arrived(piece(h, dp, dq, half), gather_sem.at[h, dp * 4 + dq, 0 if half is None else half])

    for h in range(2):
        loads[h].wait()
        for sp in (1, -1):
            pass_on(h, 0, 0, None, sp, 0)
    for h in range(2):
        for sq in (1, -1):
            pass_on(h, 0, 0, None, 0, sq)

    def scale(part):
        @pl.loop(2 * part, 2 * part + 2)
        def _(k):
            @pl.loop(0, 32, unroll=8)
            def _(s):
                level = cpl_ref[k, s]
                coef = jnp.where(
                    level == 0, COEFS[0], jnp.where(level == 1, COEFS[1], jnp.where(level == 2, COEFS[2], COEFS[3]))
                )
                scaled[k, s] = (left[k, s].astype(F32) * coef).astype(BF16)

    def pair_image(h, zz, j):
        to = pl.ds(pl.multiple_of(zz * 32 + j * 16, 16), 16)

        def put(ref, first, second):
            for s in range(16):
                two = jnp.concatenate([first[s * 8 : s * 8 + 8], second[s * 8 : s * 8 + 8]], axis=0)
                ref[h * 16 + s, to, :] = two.astype(BF16)

        def rows_in(o):
            return got[h, zz * 4 + 2 * j + o]

        put(full, rows_in(0).astype(F32), rows_in(1).astype(F32))
        for k in range(8):
            unit, reg = k % 2, k // 2 % 2
            pltpu.matmul_push_rhs(right[k], reg, unit)
            for o in range(2):
                pltpu.matmul_acc_lhs(acc[unit][2 * reg + o], rows_in(o), reg if o == 0 else None)
            put(image.at[k], pltpu.matmul_pop(acc[unit][2 * reg]), pltpu.matmul_pop(acc[unit][2 * reg + 1]))

    def images(count, which):
        @pl.loop(0, count)
        def _(i):
            h, dz, other = which(i)
            j = x // 2
            pair_image(h, lax.rem(z + dz, 4), j + other * (1 - 2 * j))

    loads[2].wait()
    scale(0)
    for h in range(2):
        for dp, half, sp in ((3, 0, 1), (1, 1, -1)):
            await_piece(h, dp, 0, None)
            pass_on(h, dp, 0, half, sp, 0)
            for sq in (1, -1):
                pass_on(h, dp, 0, None, 0, sq)
    for h in range(2):
        for dq, half, sq in ((3, 0, 1), (1, 1, -1)):
            await_piece(h, 0, dq, None)
            pass_on(h, 0, dq, half, 0, sq)
    loads[3].wait()
    images(2, lambda i: (i, 0, 0))
    for h in range(2):
        await_piece(h, 2, 0, 0)
        await_piece(h, 2, 0, 1)
        for sq in (1, -1):
            pass_on(h, 2, 0, None, 0, sq)
    scale(1)
    for h in range(2):
        await_piece(h, 0, 2, 0)
        await_piece(h, 0, 2, 1)
    images(2, lambda i: (i, 0, 1))
    scale(2)
    for h in range(2):
        for dp in (3, 1):
            for dq, half, sq in ((3, 0, 1), (1, 1, -1)):
                await_piece(h, dp, dq, None)
                pass_on(h, dp, dq, half, 0, sq)
    images(4, lambda i: (i // 2, 3 + 2 * (i % 2), 0))
    for h in range(2):
        for dq, half, sq in ((3, 0, 1), (1, 1, -1)):
            await_piece(h, 2, dq, None)
            pass_on(h, 2, dq, half, 0, sq)
    scale(3)
    images(3, lambda i: (i // 2, 3 + 2 * i + 3 * (i // 2), 1 - i // 2))
    for h in range(2):
        for dp in (3, 1):
            for half in range(2):
                await_piece(h, dp, 2, half)
    images(3, lambda i: (1 - i // 2, 3 + 2 * i + 3 * (i // 2), 1 - i // 2))
    for h in range(2):
        for half in range(2):
            await_piece(h, 2, 2, half)
    images(2, lambda i: (i, 2, 1))

    span = 32 // CHUNKS * 8

    def source(k, s):
        return lax.rem(src_ref[k, s], 32)

    def sigma_of(s, unit, buf):
        for t in range(4):
            rhs = jnp.concatenate([image[k, source(k, s)] for k in (2 * t, 2 * t + 1)], axis=0)
            lhs = jnp.concatenate([scaled[2 * t, s], scaled[2 * t + 1, s]], axis=1)
            pltpu.matmul_push_rhs(rhs, t % 2, unit)
            pltpu.matmul_acc_lhs(acc[unit][buf], lhs, t % 2)

    def sigma_chunk(c):
        @pl.loop(c * (8 // CHUNKS), (c + 1) * (8 // CHUNKS))
        def _(i):
            for pair in range(2):
                at_pair = 2 * i + pair
                for e in range(2):
                    sigma_of(2 * at_pair + e, e, pair)
                    full_t[at_pair, :, e * 128 : e * 128 + 128] = full[2 * at_pair + e].T
                first, second = pltpu.matmul_pop(acc[0][pair]), pltpu.matmul_pop(acc[1][pair])
                rows = pl.ds(pl.multiple_of(at_pair * 16, 16), 16)
                for o in range(16):
                    two = jnp.concatenate([first[o * 8 : o * 8 + 8], second[o * 8 : o * 8 + 8]], axis=0).astype(BF16)
                    parts[0, o // 4, o % 4, rows, :] = two[:, :128]
                    parts[1, o % 4, o // 4, rows, :] = two[:, 128:]

    steps = ((0, 1), (1, 3))

    def rows_of(c, half):
        return pl.ds(c * span + half * (span // 2), span // 2)

    def sum1(c):
        for h in range(2):
            p, q = coords[h]
            for d, step in steps:
                start(parts.at[h, turn(q, 2), :, rows_of(c, d), :], hop1.at[h, d, c], sum_sem.at[0, h, d, c], at(h, 0, step))

    def sum2(c):
        for h in range(2):
            p, q = coords[h]
            for d, step in steps:
                arrived(hop1.at[h, d, c], sum_sem.at[0, h, d, c])
                near = turn(q, step)
                old = parts[h, near, :, rows_of(c, d), :].astype(F32)
                parts[h, near, :, rows_of(c, d), :] = (old + hop1[h, d, c].astype(F32)).astype(BF16)
                start(parts.at[h, near, :, pl.ds(c * span, span), :], hop2.at[h, d, c], sum_sem.at[1, h, d, c], at(h, 0, step))

    def sum3(c):
        for h in range(2):
            p, q = coords[h]
            for d, step in steps:
                arrived(hop2.at[h, d, c], sum_sem.at[1, h, d, c])
            rows = pl.ds(c * span, span)
            total = parts[h, q, :, rows, :].astype(F32) + hop2[h, 0, c].astype(F32) + hop2[h, 1, c].astype(F32)
            kept[h, :, rows, :] = total.astype(BF16)
            for d, step in steps:
                start(kept.at[h, turn(p, 2), rows_of(c, d), :], hop3.at[h, d, c], sum_sem.at[2, h, d, c], at(h, step, 0))

    def sum4(c):
        for h in range(2):
            p, q = coords[h]
            for d, step in steps:
                arrived(hop3.at[h, d, c], sum_sem.at[2, h, d, c])
                near = turn(p, step)
                old = kept[h, near, rows_of(c, d), :].astype(F32)
                kept[h, near, rows_of(c, d), :] = (old + hop3[h, d, c].astype(F32)).astype(BF16)
                start(kept.at[h, near, pl.ds(c * span, span), :], hop4.at[h, d, c], sum_sem.at[3, h, d, c], at(h, step, 0))

    def sum5(c):
        for h in range(2):
            p, q = coords[h]
            for d, step in steps:
                arrived(hop4.at[h, d, c], sum_sem.at[3, h, d, c])
            rows = pl.ds(c * span, span)
            total = kept[h, p, rows, :].astype(F32) + hop4[h, 0, c].astype(F32) + hop4[h, 1, c].astype(F32)
            sig_ref[rows, pl.ds(h * 128, 128)] = total * (128 ** -0.5)

    def half_product(ks):
        @pl.loop(0, 4)
        def _(i):
            for e in range(4):
                for j in range(2):
                    none = jnp.zeros((128, 128), BF16)
                    one, two = left[ks[j], 8 * i + 2 * e], left[ks[j], 8 * i + 2 * e + 1]
                    rhs = jnp.concatenate(
                        [jnp.concatenate([one, none], axis=1), jnp.concatenate([none, two], axis=1)], axis=0
                    )
                    pltpu.matmul_push_rhs(rhs, e % 2, j)
                    for half in range(2):
                        buf = acc[j][e % 2 * 2 + half]
                        pltpu.matmul_acc_lhs(
                            buf, full_t[4 * i + e, half * 128 : half * 128 + 128, :], e % 2 if half == 0 else None
                        )
                for j in range(2):
                    for half in range(2):
                        zed[j, 4 * i + e, half * 128 : half * 128 + 128, :] = pltpu.matmul_pop(
                            acc[j][e % 2 * 2 + half]
                        ).astype(BF16)

    def renorm(ks, slot):
        @pl.loop(0, 4)
        def _(i):
            for e in range(4):
                for j in range(2):
                    rhs = jnp.concatenate([full[source(ks[j], 8 * i + 2 * e + n)] for n in range(2)], axis=0)
                    pltpu.matmul_push_rhs(rhs, e % 2, j)
                    for half in range(2):
                        pltpu.matmul_acc_lhs(
                            acc[j][half], zed[j, 4 * i + e, half * 128 : half * 128 + 128, :], e % 2 if half == 0 else None
                        )

        for j in range(2):
            for half in range(2):
                block[slot + j, half * 128 : half * 128 + 128, :] = (
                    pltpu.matmul_pop(acc[j][half]) * (4096 ** -0.5)
                ).astype(BF16)

    def push(src, dst, recv_sem, target):
        copy = pltpu.make_async_remote_copy(
            src_ref=src, dst_ref=dst, send_sem=send_sem.at[len(sent)], recv_sem=recv_sem,
            device_id=(op, target), device_id_type=MESH,
        )
        copy.start()
        sent.append(copy)

    def ship(slot, dy, target):
        push(block.at[slot], ren_ref.at[sec], swap_sem.at[dy, core], target)

    def half_rows(d):
        return pl.ds(d * 128, 128)

    def ship_far():
        for j in range(2):
            for d, step in steps:
                push(block.at[j, half_rows(d)], relay.at[d, j], relay_sem.at[d, j], turn(y, step) * 2 + core)

    def relay_far():
        for j in range(2):
            for d, step in steps:
                arrived(relay.at[d, j], relay_sem.at[d, j])
                sender = turn(y, 4 - step) * 2 + core
                push(relay.at[d, j], ren_ref.at[sender, half_rows(d)], far_sem.at[d, core], turn(y, step) * 2 + j)

    def swapped(dy, sender_core):
        sender = turn(y, 4 - dy) * 2 + sender_core
        arrived(ren_ref.at[sender], swap_sem.at[dy, sender_core])

    far = [turn(y, 2) * 2 + j for j in range(2)]
    near = [[turn(y, dy) * 2 + j for dy in (1, 3)] for j in range(2)]
    here = [2 * y + j for j in range(2)]

    sigma_chunk(0)
    sum1(0)
    sigma_chunk(1)
    sum1(1)
    sigma_chunk(2)
    sum1(2)
    sum2(0)
    sigma_chunk(3)
    sum1(3)
    sum2(1)
    half_product(far)
    sum2(2)
    renorm(far, 0)
    ship_far()
    sum2(3)
    sum3(0)
    half_product(near[0])
    sum3(1)
    renorm(near[0], 2)
    ship(2, 1, near[0][0])
    ship(3, 3, near[0][1])
    sum3(2)
    relay_far()
    half_product(near[1])
    sum3(3)
    sum4(0)
    renorm(near[1], 4)
    ship(4, 1, near[1][0])
    ship(5, 3, near[1][1])
    sum4(1)
    sum4(2)
    sum5(0)
    half_product(here)
    sum4(3)
    sum5(1)
    renorm(here, 6)
    ship(7 - core, 0, 2 * y + 1 - core)
    own = pltpu.make_async_copy(block.at[6 + core], ren_ref.at[sec], own_sem)
    own.start()
    sum5(2)
    sum5(3)
    for dy in (1, 3):
        for c in range(2):
            swapped(dy, c)
    for c in range(2):
        for d in range(2):
            arrived(ren_ref.at[turn(y, 2) * 2 + c, half_rows(d)], far_sem.at[d, c])
    swapped(0, 1 - core)
    own.wait()
    for copy in sent:
        copy.wait_send()


def with_totals(*refs):
    totals = [pltpu.ACC(unit)((128, 256), F32) for unit in (0, 0, 0, 0, 1, 1, 1, 1)]
    pl.run_scoped(functools.partial(kernel, *refs), *totals)


def finish(sig_ref, ren_ref, sigma_ref, renorm_ref, sig, sigma, narrow, wide, in_sem, out_sem):
    come = [pltpu.make_async_copy(ren_ref.at[i], narrow.at[i], in_sem.at[i]) for i in range(8)]
    come.append(pltpu.make_async_copy(sig_ref, sig, in_sem.at[8]))
    go = [pltpu.make_async_copy(wide.at[i], renorm_ref.at[i], out_sem.at[i]) for i in range(8)]
    go.append(pltpu.make_async_copy(sigma, sigma_ref, out_sem.at[8]))
    for copy in come:
        copy.start()
    for i in range(8):
        come[i].wait()
        wide[i] = narrow[i].astype(F32)
        go[i].start()
    come[8].wait()
    sigma[...] = sig[...].astype(BF16)
    go[8].start()
    for copy in go:
        copy.wait()


def body(psi, left_env, right_env, source, coupling):
    vm = pltpu.VMEM
    rows = 256 // CHUNKS
    sig, ren = pl.pallas_call(
        with_totals,
        out_shape=(jax.ShapeDtypeStruct((256, 256), F32), jax.ShapeDtypeStruct((8, 256, 256), BF16)),
        in_specs=[pl.BlockSpec(memory_space=pl.ANY)] * 3 + [pl.BlockSpec(memory_space=pltpu.SMEM)] * 2,
        out_specs=(pl.BlockSpec(memory_space=pltpu.VMEM), pl.BlockSpec(memory_space=pl.ANY)),
        scratch_shapes=[
            vm((8, 32, 128, 128), BF16),
            vm((8, 32, 128, 128), BF16),
            vm((8, 256, 256), BF16),
            vm((2, 16, 128, 256), BF16),
            vm((32, 128, 256), BF16),
            vm((16, 256, 256), BF16),
            vm((8, 32, 128, 256), BF16),
            vm((2, 16, 256, 256), BF16),
            vm((2, 4, 4, 256, 128), BF16),
            vm((8, 256, 256), BF16),
            vm((2, 2, CHUNKS, 4, rows // 2, 128), BF16),
            vm((2, 2, CHUNKS, 4, rows, 128), BF16),
            vm((2, 4, 256, 128), BF16),
            vm((2, 2, CHUNKS, rows // 2, 128), BF16),
            vm((2, 2, CHUNKS, rows, 128), BF16),
            vm((2, 2, 128, 256), BF16),
            pltpu.SemaphoreType.DMA((4,)),
            pltpu.SemaphoreType.DMA((128,)),
            pltpu.SemaphoreType.DMA((2, 16, 2)),
            pltpu.SemaphoreType.DMA((4, 2, 2, CHUNKS)),
            pltpu.SemaphoreType.DMA((4, 2)),
            pltpu.SemaphoreType.DMA((2, 2)),
            pltpu.SemaphoreType.DMA((2, 2)),
            pltpu.SemaphoreType.DMA,
        ],
        compiler_params=pltpu.CompilerParams(
            collective_id=0, has_side_effects=True, vmem_limit_bytes=60 * 1024 * 1024
        ),
        cost_estimate=pl.CostEstimate(flops=13 * 10**9, bytes_accessed=12 * 2**20, transcendentals=0),
        name="dmrg_step",
    )(psi.reshape(256, 256), left_env, right_env.reshape(8, 256, 256), source, coupling)
    sigma, renorm = pl.pallas_call(
        finish,
        out_shape=(jax.ShapeDtypeStruct((256, 256), BF16), jax.ShapeDtypeStruct((8, 256, 256), F32)),
        in_specs=[pl.BlockSpec(memory_space=pl.ANY)] * 2,
        out_specs=(pl.BlockSpec(memory_space=pl.ANY), pl.BlockSpec(memory_space=pl.ANY)),
        scratch_shapes=[
            vm((256, 256), F32),
            vm((256, 256), BF16),
            vm((8, 256, 256), BF16),
            vm((8, 256, 256), F32),
            pltpu.SemaphoreType.DMA((9,)),
            pltpu.SemaphoreType.DMA((9,)),
        ],
        compiler_params=pltpu.CompilerParams(vmem_limit_bytes=60 * 1024 * 1024),
        name="finish",
    )(sig, ren)
    return sigma.reshape(32, 8, 256), renorm[None]


def solution(mesh):
    placed = (
        P("sec", "op", None),
        P("op", "sec", None, None),
        P("op", "sec", None, None),
        P("op", "sec"),
        P("op", "sec"),
    )
    return jax.shard_map(
        body,
        mesh=mesh,
        in_specs=placed,
        out_specs=(P("sec", "op", None), P(("op", "sec"), None, None, None)),
        check_vma=False,
    )
```

```python
import functools

import jax
import jax.numpy as jnp
from jax import lax
from jax.experimental import pallas as pl
from jax.experimental.pallas import tpu as pltpu
from jax.sharding import PartitionSpec as P

COEFS = (1.0, -0.5773503, 0.8164966, -0.7071068)
MESH = pl.DeviceIdType.MESH
F32 = jnp.float32
BF16 = jnp.bfloat16
CHUNKS = 4


def turn(a, step):
    return lax.rem(a + step, 4)


def kernel(
    psi_ref, left_ref, right_ref, src_ref, cpl_ref,
    sig_ref, ren_ref,
    left, scaled, right, got, full, full_t, image, zed, parts, block,
    hop1, hop2, kept, hop3, hop4, relay,
    load_sem, send_sem, gather_sem, sum_sem, swap_sem, relay_sem, far_sem, own_sem,
    acc00, acc01, acc02, acc03, acc10, acc11, acc12, acc13,
):
    acc = ((acc00, acc01, acc02, acc03), (acc10, acc11, acc12, acc13))
    op, sec = lax.axis_index("op"), lax.axis_index("sec")
    z, x = op // 4, op % 4
    y, core = sec // 2, sec % 2
    coords = ((x, z), (z, x))

    loads = [
        pltpu.make_async_copy(psi_ref.at[pl.ds(h * 128, 128)], got.at[h, op], load_sem.at[h]) for h in range(2)
    ]
    loads.append(pltpu.make_async_copy(right_ref, right, load_sem.at[2]))
    loads += [pltpu.make_async_copy(left_ref.at[k], left.at[k], load_sem.at[3 + k]) for k in range(8)]
    for copy in loads:
        copy.start()

    barrier = pltpu.get_barrier_semaphore()
    peers = [(z * 4 + turn(x, 1), sec), (z * 4 + turn(x, 3), sec), (turn(z, 1) * 4 + x, sec), (turn(z, 3) * 4 + x, sec)]
    peers += [(op, lax.rem(sec + i, 8)) for i in range(1, 8)]
    for peer in peers:
        pl.semaphore_signal(barrier, inc=1, device_id=peer, device_id_type=MESH)
    pl.semaphore_wait(barrier, len(peers))

    sent = []

    def place(h, p, q):
        return q * 4 + p if h == 0 else p * 4 + q

    def at(h, dp, dq):
        p, q = coords[h]
        return place(h, turn(p, dp), turn(q, dq))

    def start(src, dst, recv_sem, target):
        copy = pltpu.make_async_remote_copy(
            src_ref=src, dst_ref=dst, send_sem=send_sem.at[len(sent)], recv_sem=recv_sem,
            device_id=(target, sec), device_id_type=MESH,
        )
        copy.start()
        sent.append(copy)

    def arrived(dst, recv_sem):
        pltpu.make_async_remote_copy(
            src_ref=dst, dst_ref=dst, send_sem=send_sem.at[0], recv_sem=recv_sem,
            device_id=(op, sec), device_id_type=MESH,
        ).wait_recv()

    def piece(h, dp, dq, half):
        ref = got.at[h, at(h, dp, dq)]
        return ref if half is None else ref.at[pl.ds(half * 64, 64)]

    def pass_on(h, dp, dq, half, sp, sq):
        ref = piece(h, dp, dq, half)
        rel = (dp - sp) % 4 * 4 + (dq - sq) % 4
        start(ref, ref, gather_sem.at[h, rel, 0 if half is None else half], at(h, sp % 4, sq % 4))

    def await_piece(h, dp, dq, half):
        arrived(piece(h, dp, dq, half), gather_sem.at[h, dp * 4 + dq, 0 if half is None else half])

    for h in range(2):
        loads[h].wait()
        for sp in (1, -1):
            pass_on(h, 0, 0, None, sp, 0)
    for h in range(2):
        for sq in (1, -1):
            pass_on(h, 0, 0, None, 0, sq)

    def scale(part):
        for k in (2 * part, 2 * part + 1):
            loads[3 + k].wait()

        @pl.loop(2 * part, 2 * part + 2)
        def _(k):
            @pl.loop(0, 32, unroll=8)
            def _(s):
                level = cpl_ref[k, s]
                coef = jnp.where(
                    level == 0, COEFS[0], jnp.where(level == 1, COEFS[1], jnp.where(level == 2, COEFS[2], COEFS[3]))
                )
                scaled[k, s] = (left[k, s].astype(F32) * coef).astype(BF16)

    def pair_image(h, zz, j):
        to = pl.ds(pl.multiple_of(zz * 32 + j * 16, 16), 16)

        def put(ref, first, second):
            for s in range(16):
                two = jnp.concatenate([first[s * 8 : s * 8 + 8], second[s * 8 : s * 8 + 8]], axis=0)
                ref[h * 16 + s, to, :] = two.astype(BF16)

        def rows_in(o):
            return got[h, zz * 4 + 2 * j + o]

        put(full, rows_in(0).astype(F32), rows_in(1).astype(F32))
        for k in range(8):
            unit, reg = k % 2, k // 2 % 2
            pltpu.matmul_push_rhs(right[k], reg, unit)
            for o in range(2):
                pltpu.matmul_acc_lhs(acc[unit][2 * reg + o], rows_in(o), reg if o == 0 else None)
            put(image.at[k], pltpu.matmul_pop(acc[unit][2 * reg]), pltpu.matmul_pop(acc[unit][2 * reg + 1]))

    def images(count, which):
        @pl.loop(0, count)
        def _(i):
            h, dz, other = which(i)
            j = x // 2
            pair_image(h, lax.rem(z + dz, 4), j + other * (1 - 2 * j))

    for h in range(2):
        for dp, half, sp in ((3, 0, 1), (1, 1, -1)):
            await_piece(h, dp, 0, None)
            pass_on(h, dp, 0, half, sp, 0)
            for sq in (1, -1):
                pass_on(h, dp, 0, None, 0, sq)
    for h in range(2):
        for dq, half, sq in ((3, 0, 1), (1, 1, -1)):
            await_piece(h, 0, dq, None)
            pass_on(h, 0, dq, half, 0, sq)
    loads[2].wait()
    images(2, lambda i: (i, 0, 0))
    scale(0)
    for h in range(2):
        await_piece(h, 2, 0, 0)
        await_piece(h, 2, 0, 1)
        for sq in (1, -1):
            pass_on(h, 2, 0, None, 0, sq)
    scale(1)
    for h in range(2):
        await_piece(h, 0, 2, 0)
        await_piece(h, 0, 2, 1)
    images(2, lambda i: (i, 0, 1))
    scale(2)
    for h in range(2):
        for dp in (3, 1):
            for dq, half, sq in ((3, 0, 1), (1, 1, -1)):
                await_piece(h, dp, dq, None)
                pass_on(h, dp, dq, half, 0, sq)
    images(4, lambda i: (i // 2, 3 + 2 * (i % 2), 0))
    for h in range(2):
        for dq, half, sq in ((3, 0, 1), (1, 1, -1)):
            await_piece(h, 2, dq, None)
            pass_on(h, 2, dq, half, 0, sq)
    scale(3)
    images(3, lambda i: (i // 2, 3 + 2 * i + 3 * (i // 2), 1 - i // 2))
    for h in range(2):
        for dp in (3, 1):
            for half in range(2):
                await_piece(h, dp, 2, half)
    images(3, lambda i: (1 - i // 2, 3 + 2 * i + 3 * (i // 2), 1 - i // 2))
    for h in range(2):
        for half in range(2):
            await_piece(h, 2, 2, half)
    images(2, lambda i: (i, 2, 1))

    span = 32 // CHUNKS * 8

    def source(k, s):
        return lax.rem(src_ref[k, s], 32)

    def sigma_of(s, unit, buf):
        for t in range(4):
            rhs = jnp.concatenate([image[k, source(k, s)] for k in (2 * t, 2 * t + 1)], axis=0)
            lhs = jnp.concatenate([scaled[2 * t, s], scaled[2 * t + 1, s]], axis=1)
            pltpu.matmul_push_rhs(rhs, t % 2, unit)
            pltpu.matmul_acc_lhs(acc[unit][buf], lhs, t % 2)

    def sigma_chunk(c):
        @pl.loop(c * (8 // CHUNKS), (c + 1) * (8 // CHUNKS))
        def _(i):
            for pair in range(2):
                at_pair = 2 * i + pair
                for e in range(2):
                    sigma_of(2 * at_pair + e, e, pair)
                first, second = pltpu.matmul_pop(acc[0][pair]), pltpu.matmul_pop(acc[1][pair])
                rows = pl.ds(pl.multiple_of(at_pair * 16, 16), 16)
                for o in range(16):
                    two = jnp.concatenate([first[o * 8 : o * 8 + 8], second[o * 8 : o * 8 + 8]], axis=0).astype(BF16)
                    parts[0, o // 4, o % 4, rows, :] = two[:, :128]
                    parts[1, o % 4, o // 4, rows, :] = two[:, 128:]

    steps = ((0, 1), (1, 3))

    def rows_of(c, half):
        return pl.ds(c * span + half * (span // 2), span // 2)

    def sum1(c):
        for h in range(2):
            p, q = coords[h]
            for d, step in steps:
                start(parts.at[h, turn(q, 2), :, rows_of(c, d), :], hop1.at[h, d, c], sum_sem.at[0, h, d, c], at(h, 0, step))

    def sum2(c):
        for h in range(2):
            p, q = coords[h]
            for d, step in steps:
                arrived(hop1.at[h, d, c], sum_sem.at[0, h, d, c])
                near = turn(q, step)
                old = parts[h, near, :, rows_of(c, d), :].astype(F32)
                parts[h, near, :, rows_of(c, d), :] = (old + hop1[h, d, c].astype(F32)).astype(BF16)
                start(parts.at[h, near, :, pl.ds(c * span, span), :], hop2.at[h, d, c], sum_sem.at[1, h, d, c], at(h, 0, step))

    def sum3(c):
        for h in range(2):
            p, q = coords[h]
            for d, step in steps:
                arrived(hop2.at[h, d, c], sum_sem.at[1, h, d, c])
            rows = pl.ds(c * span, span)
            total = parts[h, q, :, rows, :].astype(F32) + hop2[h, 0, c].astype(F32) + hop2[h, 1, c].astype(F32)
            kept[h, :, rows, :] = total.astype(BF16)
            for d, step in steps:
                start(kept.at[h, turn(p, 2), rows_of(c, d), :], hop3.at[h, d, c], sum_sem.at[2, h, d, c], at(h, step, 0))

    def sum4(c):
        for h in range(2):
            p, q = coords[h]
            for d, step in steps:
                arrived(hop3.at[h, d, c], sum_sem.at[2, h, d, c])
                near = turn(p, step)
                old = kept[h, near, rows_of(c, d), :].astype(F32)
                kept[h, near, rows_of(c, d), :] = (old + hop3[h, d, c].astype(F32)).astype(BF16)
                start(kept.at[h, near, pl.ds(c * span, span), :], hop4.at[h, d, c], sum_sem.at[3, h, d, c], at(h, step, 0))

    def sum5(c):
        for h in range(2):
            p, q = coords[h]
            for d, step in steps:
                arrived(hop4.at[h, d, c], sum_sem.at[3, h, d, c])
            rows = pl.ds(c * span, span)
            total = kept[h, p, rows, :].astype(F32) + hop4[h, 0, c].astype(F32) + hop4[h, 1, c].astype(F32)
            sig_ref[rows, pl.ds(h * 128, 128)] = total * (128 ** -0.5)

    def mix(ks, turning=False):
        @pl.loop(0, 4)
        def _(i):
            none = jnp.zeros((128, 128), BF16)
            for e in range(4):
                at_pair = 4 * i + e
                if turning:
                    for n in range(2):
                        full_t[at_pair, :, n * 128 : n * 128 + 128] = full[2 * at_pair + n].T
                for j in range(2):
                    rhs = jnp.concatenate([full[source(ks[j], 2 * at_pair + n)] for n in range(2)], axis=0)
                    pltpu.matmul_push_rhs(rhs, e % 2, j)
                    for n in range(2):
                        one = left[ks[j], 2 * at_pair + n]
                        lhs = jnp.concatenate([one, none] if n == 0 else [none, one], axis=1)
                        pltpu.matmul_acc_lhs(acc[j][e % 2 * 2 + n], lhs, e % 2 if n == 0 else None)
                for j in range(2):
                    for n in range(2):
                        zed[j, at_pair, n * 128 : n * 128 + 128, :] = pltpu.matmul_pop(acc[j][e % 2 * 2 + n]).astype(BF16)

    def renorm(slot):
        @pl.loop(0, 4)
        def _(i):
            for e in range(4):
                for j in range(2):
                    pltpu.matmul_push_rhs(zed[j, 4 * i + e], e % 2, j)
                    for half in range(2):
                        pltpu.matmul_acc_lhs(
                            acc[j][half], full_t[4 * i + e, half * 128 : half * 128 + 128, :], e % 2 if half == 0 else None
                        )

        for j in range(2):
            for half in range(2):
                block[slot + j, half * 128 : half * 128 + 128, :] = (
                    pltpu.matmul_pop(acc[j][half]) * (4096 ** -0.5)
                ).astype(BF16)

    def push(src, dst, recv_sem, target):
        copy = pltpu.make_async_remote_copy(
            src_ref=src, dst_ref=dst, send_sem=send_sem.at[len(sent)], recv_sem=recv_sem,
            device_id=(op, target), device_id_type=MESH,
        )
        copy.start()
        sent.append(copy)

    def ship(slot, dy, target):
        push(block.at[slot], ren_ref.at[sec], swap_sem.at[dy, core], target)

    def half_rows(d):
        return pl.ds(d * 128, 128)

    def ship_far():
        for j in range(2):
            for d, step in steps:
                push(block.at[j, half_rows(d)], relay.at[d, j], relay_sem.at[d, j], turn(y, step) * 2 + core)

    def relay_far():
        for j in range(2):
            for d, step in steps:
                arrived(relay.at[d, j], relay_sem.at[d, j])
                sender = turn(y, 4 - step) * 2 + core
                push(relay.at[d, j], ren_ref.at[sender, half_rows(d)], far_sem.at[d, core], turn(y, step) * 2 + j)

    def swapped(dy, sender_core):
        sender = turn(y, 4 - dy) * 2 + sender_core
        arrived(ren_ref.at[sender], swap_sem.at[dy, sender_core])

    far = [turn(y, 2) * 2 + j for j in range(2)]
    near = [[turn(y, dy) * 2 + j for dy in (1, 3)] for j in range(2)]
    here = [2 * y + j for j in range(2)]

    sigma_chunk(0)
    sum1(0)
    sigma_chunk(1)
    sum1(1)
    mix(far, turning=True)
    sum2(0)
    renorm(0)
    ship_far()
    sum2(1)
    sigma_chunk(2)
    sum1(2)
    sigma_chunk(3)
    sum1(3)
    sum3(0)
    mix(near[0])
    sum2(2)
    sum3(1)
    renorm(2)
    ship(2, 1, near[0][0])
    ship(3, 3, near[0][1])
    sum2(3)
    sum4(0)
    relay_far()
    mix(near[1])
    sum3(2)
    sum4(1)
    renorm(4)
    ship(4, 1, near[1][0])
    ship(5, 3, near[1][1])
    sum3(3)
    sum5(0)
    mix(here)
    sum4(2)
    sum5(1)
    renorm(6)
    ship(7 - core, 0, 2 * y + 1 - core)
    own = pltpu.make_async_copy(block.at[6 + core], ren_ref.at[sec], own_sem)
    own.start()
    sum4(3)
    sum5(2)
    sum5(3)
    for dy in (1, 3):
        for c in range(2):
            swapped(dy, c)
    for c in range(2):
        for d in range(2):
            arrived(ren_ref.at[turn(y, 2) * 2 + c, half_rows(d)], far_sem.at[d, c])
    swapped(0, 1 - core)
    own.wait()
    for copy in sent:
        copy.wait_send()


def with_totals(*refs):
    totals = [pltpu.ACC(unit)((128, 256), F32) for unit in (0, 0, 0, 0, 1, 1, 1, 1)]
    pl.run_scoped(functools.partial(kernel, *refs), *totals)


def finish(sig_ref, ren_ref, sigma_ref, renorm_ref, sig, sigma, narrow, wide, in_sem, out_sem):
    come = [pltpu.make_async_copy(ren_ref.at[i], narrow.at[i], in_sem.at[i]) for i in range(8)]
    come.append(pltpu.make_async_copy(sig_ref, sig, in_sem.at[8]))
    go = [pltpu.make_async_copy(wide.at[i], renorm_ref.at[i], out_sem.at[i]) for i in range(8)]
    go.append(pltpu.make_async_copy(sigma, sigma_ref, out_sem.at[8]))
    for copy in come:
        copy.start()
    for i in range(8):
        come[i].wait()
        wide[i] = narrow[i].astype(F32)
        go[i].start()
    come[8].wait()
    sigma[...] = sig[...].astype(BF16)
    go[8].start()
    for copy in go:
        copy.wait()


def body(psi, left_env, right_env, source, coupling):
    vm = pltpu.VMEM
    rows = 256 // CHUNKS
    sig, ren = pl.pallas_call(
        with_totals,
        out_shape=(jax.ShapeDtypeStruct((256, 256), F32), jax.ShapeDtypeStruct((8, 256, 256), BF16)),
        in_specs=[pl.BlockSpec(memory_space=pl.ANY)] * 3 + [pl.BlockSpec(memory_space=pltpu.SMEM)] * 2,
        out_specs=(pl.BlockSpec(memory_space=pltpu.VMEM), pl.BlockSpec(memory_space=pl.ANY)),
        scratch_shapes=[
            vm((8, 32, 128, 128), BF16),
            vm((8, 32, 128, 128), BF16),
            vm((8, 256, 256), BF16),
            vm((2, 16, 128, 256), BF16),
            vm((32, 128, 256), BF16),
            vm((16, 256, 256), BF16),
            vm((8, 32, 128, 256), BF16),
            vm((2, 16, 256, 256), BF16),
            vm((2, 4, 4, 256, 128), BF16),
            vm((8, 256, 256), BF16),
            vm((2, 2, CHUNKS, 4, rows // 2, 128), BF16),
            vm((2, 2, CHUNKS, 4, rows, 128), BF16),
            vm((2, 4, 256, 128), BF16),
            vm((2, 2, CHUNKS, rows // 2, 128), BF16),
            vm((2, 2, CHUNKS, rows, 128), BF16),
            vm((2, 2, 128, 256), BF16),
            pltpu.SemaphoreType.DMA((11,)),
            pltpu.SemaphoreType.DMA((128,)),
            pltpu.SemaphoreType.DMA((2, 16, 2)),
            pltpu.SemaphoreType.DMA((4, 2, 2, CHUNKS)),
            pltpu.SemaphoreType.DMA((4, 2)),
            pltpu.SemaphoreType.DMA((2, 2)),
            pltpu.SemaphoreType.DMA((2, 2)),
            pltpu.SemaphoreType.DMA,
        ],
        compiler_params=pltpu.CompilerParams(
            collective_id=0, has_side_effects=True, vmem_limit_bytes=60 * 1024 * 1024
        ),
        cost_estimate=pl.CostEstimate(flops=13 * 10**9, bytes_accessed=12 * 2**20, transcendentals=0),
        name="dmrg_step",
    )(psi.reshape(256, 256), left_env, right_env.reshape(8, 256, 256), source, coupling)
    sigma, renorm = pl.pallas_call(
        finish,
        out_shape=(jax.ShapeDtypeStruct((256, 256), BF16), jax.ShapeDtypeStruct((8, 256, 256), F32)),
        in_specs=[pl.BlockSpec(memory_space=pl.ANY)] * 2,
        out_specs=(pl.BlockSpec(memory_space=pl.ANY), pl.BlockSpec(memory_space=pl.ANY)),
        scratch_shapes=[
            vm((256, 256), F32),
            vm((256, 256), BF16),
            vm((8, 256, 256), BF16),
            vm((8, 256, 256), F32),
            pltpu.SemaphoreType.DMA((9,)),
            pltpu.SemaphoreType.DMA((9,)),
        ],
        compiler_params=pltpu.CompilerParams(vmem_limit_bytes=60 * 1024 * 1024),
        name="finish",
    )(sig, ren)
    return sigma.reshape(32, 8, 256), renorm[None]


def solution(mesh):
    placed = (
        P("sec", "op", None),
        P("op", "sec", None, None),
        P("op", "sec", None, None),
        P("op", "sec"),
        P("op", "sec"),
    )
    return jax.shard_map(
        body,
        mesh=mesh,
        in_specs=placed,
        out_specs=(P("sec", "op", None), P(("op", "sec"), None, None, None)),
        check_vma=False,
    )
```

```python
import functools

import jax
import jax.numpy as jnp
from jax import lax
from jax.experimental import pallas as pl
from jax.experimental.pallas import tpu as pltpu
from jax.sharding import PartitionSpec as P

COEFS = (1.0, -0.5773503, 0.8164966, -0.7071068)
MESH = pl.DeviceIdType.MESH
F32 = jnp.float32
BF16 = jnp.bfloat16
CHUNKS = 2


def turn(a, step):
    return lax.rem(a + step, 4)


def kernel(
    psi_ref, left_ref, right_ref, src_ref, cpl_ref,
    sig_ref, ren_ref,
    left, scaled, right, got, full, full_t, image, zed, parts, block,
    hop1, hop2, kept, hop3, hop4, relay,
    load_sem, send_sem, gather_sem, sum_sem, swap_sem, relay_sem, far_sem, own_sem,
    acc00, acc01, acc02, acc03, acc10, acc11, acc12, acc13,
):
    acc = ((acc00, acc01, acc02, acc03), (acc10, acc11, acc12, acc13))
    op, sec = lax.axis_index("op"), lax.axis_index("sec")
    z, x = op // 4, op % 4
    y, core = sec // 2, sec % 2
    coords = ((x, z), (z, x))

    loads = [
        pltpu.make_async_copy(psi_ref.at[pl.ds(h * 128, 128)], got.at[h, op], load_sem.at[h]) for h in range(2)
    ]
    loads.append(pltpu.make_async_copy(right_ref, right, load_sem.at[2]))
    loads += [pltpu.make_async_copy(left_ref.at[k], left.at[k], load_sem.at[3 + k]) for k in range(8)]
    for copy in loads:
        copy.start()

    barrier = pltpu.get_barrier_semaphore()
    peers = [(z * 4 + turn(x, 1), sec), (z * 4 + turn(x, 3), sec), (turn(z, 1) * 4 + x, sec), (turn(z, 3) * 4 + x, sec)]
    peers += [(op, lax.rem(sec + i, 8)) for i in range(1, 8)]
    for peer in peers:
        pl.semaphore_signal(barrier, inc=1, device_id=peer, device_id_type=MESH)
    pl.semaphore_wait(barrier, len(peers))

    def place(h, p, q):
        return q * 4 + p if h == 0 else p * 4 + q

    def at(h, dp, dq):
        p, q = coords[h]
        return place(h, turn(p, dp), turn(q, dq))

    def start(src, dst, kind, recv_sem, target):
        pltpu.make_async_remote_copy(
            src_ref=src, dst_ref=dst, send_sem=send_sem.at[kind], recv_sem=recv_sem,
            device_id=(target, sec), device_id_type=MESH,
        ).start()

    def arrived(dst, recv_sem):
        pltpu.make_async_remote_copy(
            src_ref=dst, dst_ref=dst, send_sem=send_sem.at[0], recv_sem=recv_sem,
            device_id=(op, sec), device_id_type=MESH,
        ).wait_recv()

    def piece(h, dp, dq, half):
        ref = got.at[h, at(h, dp, dq)]
        return ref if half is None else ref.at[pl.ds(half * 64, 64)]

    def pass_on(h, dp, dq, half, sp, sq):
        ref = piece(h, dp, dq, half)
        rel = (dp - sp) % 4 * 4 + (dq - sq) % 4
        start(ref, ref, h, gather_sem.at[h, rel, 0 if half is None else half], at(h, sp % 4, sq % 4))

    def await_piece(h, dp, dq, half):
        arrived(piece(h, dp, dq, half), gather_sem.at[h, dp * 4 + dq, 0 if half is None else half])

    for h in range(2):
        loads[h].wait()
        for sp in (1, -1):
            pass_on(h, 0, 0, None, sp, 0)
    for h in range(2):
        for sq in (1, -1):
            pass_on(h, 0, 0, None, 0, sq)

    def scale(part):
        for k in (2 * part, 2 * part + 1):
            loads[3 + k].wait()

        @pl.loop(2 * part, 2 * part + 2)
        def _(k):
            @pl.loop(0, 32, unroll=8)
            def _(s):
                level = cpl_ref[k, s]
                coef = jnp.where(
                    level == 0, COEFS[0], jnp.where(level == 1, COEFS[1], jnp.where(level == 2, COEFS[2], COEFS[3]))
                )
                scaled[k, s] = (left[k, s].astype(F32) * coef).astype(BF16)

    def pair_image(h, zz, j):
        to = pl.ds(pl.multiple_of(zz * 32 + j * 16, 16), 16)

        def put(ref, first, second):
            for s in range(16):
                two = jnp.concatenate([first[s * 8 : s * 8 + 8], second[s * 8 : s * 8 + 8]], axis=0)
                ref[h * 16 + s, to, :] = two.astype(BF16)

        def rows_in(o):
            return got[h, zz * 4 + 2 * j + o]

        put(full, rows_in(0).astype(F32), rows_in(1).astype(F32))
        for k in range(8):
            unit, reg = k % 2, k // 2 % 2
            pltpu.matmul_push_rhs(right[k], reg, unit)
            for o in range(2):
                pltpu.matmul_acc_lhs(acc[unit][2 * reg + o], rows_in(o), reg if o == 0 else None)
            put(image.at[k], pltpu.matmul_pop(acc[unit][2 * reg]), pltpu.matmul_pop(acc[unit][2 * reg + 1]))

    def images(count, which):
        @pl.loop(0, count)
        def _(i):
            h, dz, other = which(i)
            j = x // 2
            pair_image(h, lax.rem(z + dz, 4), j + other * (1 - 2 * j))

    for h in range(2):
        for dp, half, sp in ((3, 0, 1), (1, 1, -1)):
            await_piece(h, dp, 0, None)
            pass_on(h, dp, 0, half, sp, 0)
            for sq in (1, -1):
                pass_on(h, dp, 0, None, 0, sq)
    for h in range(2):
        for dq, half, sq in ((3, 0, 1), (1, 1, -1)):
            await_piece(h, 0, dq, None)
            pass_on(h, 0, dq, half, 0, sq)
    loads[2].wait()
    images(2, lambda i: (i, 0, 0))
    scale(0)
    for h in range(2):
        await_piece(h, 2, 0, 0)
        await_piece(h, 2, 0, 1)
        for sq in (1, -1):
            pass_on(h, 2, 0, None, 0, sq)
    scale(1)
    for h in range(2):
        await_piece(h, 0, 2, 0)
        await_piece(h, 0, 2, 1)
    images(2, lambda i: (i, 0, 1))
    scale(2)
    for h in range(2):
        for dp in (3, 1):
            for dq, half, sq in ((3, 0, 1), (1, 1, -1)):
                await_piece(h, dp, dq, None)
                pass_on(h, dp, dq, half, 0, sq)
    images(4, lambda i: (i // 2, 3 + 2 * (i % 2), 0))
    for h in range(2):
        for dq, half, sq in ((3, 0, 1), (1, 1, -1)):
            await_piece(h, 2, dq, None)
            pass_on(h, 2, dq, half, 0, sq)
    scale(3)
    images(3, lambda i: (i // 2, 3 + 2 * i + 3 * (i // 2), 1 - i // 2))
    for h in range(2):
        for dp in (3, 1):
            for half in range(2):
                await_piece(h, dp, 2, half)
    images(3, lambda i: (1 - i // 2, 3 + 2 * i + 3 * (i // 2), 1 - i // 2))
    for h in range(2):
        for half in range(2):
            await_piece(h, 2, 2, half)
    images(2, lambda i: (i, 2, 1))

    span = 32 // CHUNKS * 8

    def source(k, s):
        return lax.rem(src_ref[k, s], 32)

    def sigma_of(s, unit, buf):
        for t in range(4):
            rhs = jnp.concatenate([image[k, source(k, s)] for k in (2 * t, 2 * t + 1)], axis=0)
            lhs = jnp.concatenate([scaled[2 * t, s], scaled[2 * t + 1, s]], axis=1)
            pltpu.matmul_push_rhs(rhs, t % 2, unit)
            pltpu.matmul_acc_lhs(acc[unit][buf], lhs, t % 2)

    def sigma_chunk(c):
        @pl.loop(c * (8 // CHUNKS), (c + 1) * (8 // CHUNKS))
        def _(i):
            for pair in range(2):
                at_pair = 2 * i + pair
                for e in range(2):
                    sigma_of(2 * at_pair + e, e, pair)
                first, second = pltpu.matmul_pop(acc[0][pair]), pltpu.matmul_pop(acc[1][pair])
                rows = pl.ds(pl.multiple_of(at_pair * 16, 16), 16)
                for o in range(16):
                    two = jnp.concatenate([first[o * 8 : o * 8 + 8], second[o * 8 : o * 8 + 8]], axis=0).astype(BF16)
                    parts[0, o // 4, o % 4, rows, :] = two[:, :128]
                    parts[1, o % 4, o // 4, rows, :] = two[:, 128:]

    steps = ((0, 1), (1, 3))

    def rows_of(c, half):
        return pl.ds(c * span + half * (span // 2), span // 2)

    def sum1(c):
        for h in range(2):
            p, q = coords[h]
            for d, step in steps:
                start(parts.at[h, turn(q, 2), :, rows_of(c, d), :], hop1.at[h, d, c], 2, sum_sem.at[0, h, d, c], at(h, 0, step))

    def sum2(c):
        for h in range(2):
            p, q = coords[h]
            for d, step in steps:
                arrived(hop1.at[h, d, c], sum_sem.at[0, h, d, c])
                near = turn(q, step)
                old = parts[h, near, :, rows_of(c, d), :].astype(F32)
                parts[h, near, :, rows_of(c, d), :] = (old + hop1[h, d, c].astype(F32)).astype(BF16)
                start(parts.at[h, near, :, pl.ds(c * span, span), :], hop2.at[h, d, c], 3, sum_sem.at[1, h, d, c], at(h, 0, step))

    def sum3(c):
        for h in range(2):
            p, q = coords[h]
            for d, step in steps:
                arrived(hop2.at[h, d, c], sum_sem.at[1, h, d, c])
            rows = pl.ds(c * span, span)
            total = parts[h, q, :, rows, :].astype(F32) + hop2[h, 0, c].astype(F32) + hop2[h, 1, c].astype(F32)
            kept[h, :, rows, :] = total.astype(BF16)
            for d, step in steps:
                start(kept.at[h, turn(p, 2), rows_of(c, d), :], hop3.at[h, d, c], 4, sum_sem.at[2, h, d, c], at(h, step, 0))

    def sum4(c):
        for h in range(2):
            p, q = coords[h]
            for d, step in steps:
                arrived(hop3.at[h, d, c], sum_sem.at[2, h, d, c])
                near = turn(p, step)
                old = kept[h, near, rows_of(c, d), :].astype(F32)
                kept[h, near, rows_of(c, d), :] = (old + hop3[h, d, c].astype(F32)).astype(BF16)
                start(kept.at[h, near, pl.ds(c * span, span), :], hop4.at[h, d, c], 5, sum_sem.at[3, h, d, c], at(h, step, 0))

    def sum5(c):
        for h in range(2):
            p, q = coords[h]
            for d, step in steps:
                arrived(hop4.at[h, d, c], sum_sem.at[3, h, d, c])
            rows = pl.ds(c * span, span)
            total = kept[h, p, rows, :].astype(F32) + hop4[h, 0, c].astype(F32) + hop4[h, 1, c].astype(F32)
            sig_ref[rows, pl.ds(h * 128, 128)] = total * (128 ** -0.5)

    def mix(ks, turning=False):
        @pl.loop(0, 4)
        def _(i):
            none = jnp.zeros((128, 128), BF16)
            for e in range(4):
                at_pair = 4 * i + e
                if turning:
                    for n in range(2):
                        full_t[at_pair, :, n * 128 : n * 128 + 128] = full[2 * at_pair + n].T
                for j in range(2):
                    rhs = jnp.concatenate([full[source(ks[j], 2 * at_pair + n)] for n in range(2)], axis=0)
                    pltpu.matmul_push_rhs(rhs, e % 2, j)
                    for n in range(2):
                        one = left[ks[j], 2 * at_pair + n]
                        lhs = jnp.concatenate([one, none] if n == 0 else [none, one], axis=1)
                        pltpu.matmul_acc_lhs(acc[j][e % 2 * 2 + n], lhs, e % 2 if n == 0 else None)
                for j in range(2):
                    for n in range(2):
                        zed[j, at_pair, n * 128 : n * 128 + 128, :] = pltpu.matmul_pop(acc[j][e % 2 * 2 + n]).astype(BF16)

    def renorm(slot):
        @pl.loop(0, 4)
        def _(i):
            for e in range(4):
                for j in range(2):
                    pltpu.matmul_push_rhs(zed[j, 4 * i + e], e % 2, j)
                    for half in range(2):
                        pltpu.matmul_acc_lhs(
                            acc[j][half], full_t[4 * i + e, half * 128 : half * 128 + 128, :], e % 2 if half == 0 else None
                        )

        for j in range(2):
            for half in range(2):
                block[slot + j, half * 128 : half * 128 + 128, :] = (
                    pltpu.matmul_pop(acc[j][half]) * (4096 ** -0.5)
                ).astype(BF16)

    def push(src, dst, kind, recv_sem, target):
        pltpu.make_async_remote_copy(
            src_ref=src, dst_ref=dst, send_sem=send_sem.at[kind], recv_sem=recv_sem,
            device_id=(op, target), device_id_type=MESH,
        ).start()

    def ship(slot, dy, target):
        push(block.at[slot], ren_ref.at[sec], 6, swap_sem.at[dy, core], target)

    def half_rows(d):
        return pl.ds(d * 128, 128)

    def ship_far():
        for j in range(2):
            for d, step in steps:
                push(block.at[j, half_rows(d)], relay.at[d, j], 6, relay_sem.at[d, j], turn(y, step) * 2 + core)

    def relay_far():
        for j in range(2):
            for d, step in steps:
                arrived(relay.at[d, j], relay_sem.at[d, j])
                sender = turn(y, 4 - step) * 2 + core
                push(relay.at[d, j], ren_ref.at[sender, half_rows(d)], 7, far_sem.at[d, core], turn(y, step) * 2 + j)

    def swapped(dy, sender_core):
        sender = turn(y, 4 - dy) * 2 + sender_core
        arrived(ren_ref.at[sender], swap_sem.at[dy, sender_core])

    far = [turn(y, 2) * 2 + j for j in range(2)]
    near = [[turn(y, dy) * 2 + j for dy in (1, 3)] for j in range(2)]
    here = [2 * y + j for j in range(2)]

    sigma_chunk(0)
    sum1(0)
    sigma_chunk(1)
    sum1(1)
    mix(far, turning=True)
    sum2(0)
    renorm(0)
    ship_far()
    sum2(1)
    mix(near[0])
    sum3(0)
    renorm(2)
    ship(2, 1, near[0][0])
    ship(3, 3, near[0][1])
    relay_far()
    sum4(0)
    mix(near[1])
    sum3(1)
    renorm(4)
    ship(4, 1, near[1][0])
    ship(5, 3, near[1][1])
    sum5(0)
    mix(here)
    sum4(1)
    renorm(6)
    ship(7 - core, 0, 2 * y + 1 - core)
    own = pltpu.make_async_copy(block.at[6 + core], ren_ref.at[sec], own_sem)
    own.start()
    sum5(1)
    for dy in (1, 3):
        for c in range(2):
            swapped(dy, c)
    for c in range(2):
        for d in range(2):
            arrived(ren_ref.at[turn(y, 2) * 2 + c, half_rows(d)], far_sem.at[d, c])
    swapped(0, 1 - core)
    own.wait()
    all_sent = (got.at[0, pl.ds(0, 15)], got.at[1, pl.ds(0, 15)], hop1, hop2, hop3, hop4, block.at[pl.ds(0, 7)], relay)
    for kind, ref in enumerate(all_sent):
        pltpu.make_async_copy(ref, ref, send_sem.at[kind]).wait()


def with_totals(*refs):
    totals = [pltpu.ACC(unit)((128, 256), F32) for unit in (0, 0, 0, 0, 1, 1, 1, 1)]
    pl.run_scoped(functools.partial(kernel, *refs), *totals)


def finish(sig_ref, ren_ref, sigma_ref, renorm_ref, sig, sigma, narrow, wide, in_sem, out_sem):
    come = [pltpu.make_async_copy(ren_ref.at[i], narrow.at[i], in_sem.at[i]) for i in range(8)]
    come.append(pltpu.make_async_copy(sig_ref, sig, in_sem.at[8]))
    go = [pltpu.make_async_copy(wide.at[i], renorm_ref.at[i], out_sem.at[i]) for i in range(8)]
    go.append(pltpu.make_async_copy(sigma, sigma_ref, out_sem.at[8]))
    for copy in come:
        copy.start()
    for i in range(8):
        come[i].wait()
        wide[i] = narrow[i].astype(F32)
        go[i].start()
    come[8].wait()
    sigma[...] = sig[...].astype(BF16)
    go[8].start()
    for copy in go:
        copy.wait()


def body(psi, left_env, right_env, source, coupling):
    vm = pltpu.VMEM
    rows = 256 // CHUNKS
    sig, ren = pl.pallas_call(
        with_totals,
        out_shape=(jax.ShapeDtypeStruct((256, 256), F32), jax.ShapeDtypeStruct((8, 256, 256), BF16)),
        in_specs=[pl.BlockSpec(memory_space=pl.ANY)] * 3 + [pl.BlockSpec(memory_space=pltpu.SMEM)] * 2,
        out_specs=(pl.BlockSpec(memory_space=pltpu.VMEM), pl.BlockSpec(memory_space=pl.ANY)),
        scratch_shapes=[
            vm((8, 32, 128, 128), BF16),
            vm((8, 32, 128, 128), BF16),
            vm((8, 256, 256), BF16),
            vm((2, 16, 128, 256), BF16),
            vm((32, 128, 256), BF16),
            vm((16, 256, 256), BF16),
            vm((8, 32, 128, 256), BF16),
            vm((2, 16, 256, 256), BF16),
            vm((2, 4, 4, 256, 128), BF16),
            vm((8, 256, 256), BF16),
            vm((2, 2, CHUNKS, 4, rows // 2, 128), BF16),
            vm((2, 2, CHUNKS, 4, rows, 128), BF16),
            vm((2, 4, 256, 128), BF16),
            vm((2, 2, CHUNKS, rows // 2, 128), BF16),
            vm((2, 2, CHUNKS, rows, 128), BF16),
            vm((2, 2, 128, 256), BF16),
            pltpu.SemaphoreType.DMA((11,)),
            pltpu.SemaphoreType.DMA((8,)),
            pltpu.SemaphoreType.DMA((2, 16, 2)),
            pltpu.SemaphoreType.DMA((4, 2, 2, CHUNKS)),
            pltpu.SemaphoreType.DMA((4, 2)),
            pltpu.SemaphoreType.DMA((2, 2)),
            pltpu.SemaphoreType.DMA((2, 2)),
            pltpu.SemaphoreType.DMA,
        ],
        compiler_params=pltpu.CompilerParams(
            collective_id=0, has_side_effects=True, vmem_limit_bytes=60 * 1024 * 1024
        ),
        cost_estimate=pl.CostEstimate(flops=13 * 10**9, bytes_accessed=12 * 2**20, transcendentals=0),
        name="dmrg_step",
    )(psi.reshape(256, 256), left_env, right_env.reshape(8, 256, 256), source, coupling)
    sigma, renorm = pl.pallas_call(
        finish,
        out_shape=(jax.ShapeDtypeStruct((256, 256), BF16), jax.ShapeDtypeStruct((8, 256, 256), F32)),
        in_specs=[pl.BlockSpec(memory_space=pl.ANY)] * 2,
        out_specs=(pl.BlockSpec(memory_space=pl.ANY), pl.BlockSpec(memory_space=pl.ANY)),
        scratch_shapes=[
            vm((256, 256), F32),
            vm((256, 256), BF16),
            vm((8, 256, 256), BF16),
            vm((8, 256, 256), F32),
            pltpu.SemaphoreType.DMA((9,)),
            pltpu.SemaphoreType.DMA((9,)),
        ],
        compiler_params=pltpu.CompilerParams(vmem_limit_bytes=60 * 1024 * 1024),
        name="finish",
    )(sig, ren)
    return sigma.reshape(32, 8, 256), renorm[None]


def solution(mesh):
    placed = (
        P("sec", "op", None),
        P("op", "sec", None, None),
        P("op", "sec", None, None),
        P("op", "sec"),
        P("op", "sec"),
    )
    return jax.shard_map(
        body,
        mesh=mesh,
        in_specs=placed,
        out_specs=(P("sec", "op", None), P(("op", "sec"), None, None, None)),
        check_vma=False,
    )
```

```python
import functools

import jax
import jax.numpy as jnp
from jax import lax
from jax.experimental import pallas as pl
from jax.experimental.pallas import tpu as pltpu
from jax.sharding import PartitionSpec as P

COEFS = (1.0, -0.5773503, 0.8164966, -0.7071068)
MESH = pl.DeviceIdType.MESH
F32 = jnp.float32
BF16 = jnp.bfloat16
CHUNKS = 2


def turn(a, step):
    return lax.rem(a + step, 4)


def kernel(
    psi_ref, left_ref, right_ref, src_ref, cpl_ref,
    sig_ref, ren_ref,
    left, scaled, right, got, full, full_t, image, zed, parts, block,
    hop1, hop2, kept, hop3, hop4, relay,
    load_sem, send_sem, gather_sem, sum_sem, swap_sem, relay_sem, far_sem, own_sem,
    *totals,
):
    acc = (totals[:8], totals[8:])
    op, sec = lax.axis_index("op"), lax.axis_index("sec")
    z, x = op // 4, op % 4
    y, core = sec // 2, sec % 2
    coords = ((x, z), (z, x))

    loads = [
        pltpu.make_async_copy(psi_ref.at[pl.ds(h * 128, 128)], got.at[h, op], load_sem.at[h]) for h in range(2)
    ]
    loads.append(pltpu.make_async_copy(right_ref, right, load_sem.at[2]))
    loads += [pltpu.make_async_copy(left_ref.at[k], left.at[k], load_sem.at[3 + k]) for k in range(8)]
    for copy in loads:
        copy.start()

    barrier = pltpu.get_barrier_semaphore()
    peers = [(z * 4 + turn(x, 1), sec), (z * 4 + turn(x, 3), sec), (turn(z, 1) * 4 + x, sec), (turn(z, 3) * 4 + x, sec)]
    peers += [(op, lax.rem(sec + i, 8)) for i in range(1, 8)]
    for peer in peers:
        pl.semaphore_signal(barrier, inc=1, device_id=peer, device_id_type=MESH)
    pl.semaphore_wait(barrier, len(peers))

    def place(h, p, q):
        return q * 4 + p if h == 0 else p * 4 + q

    def at(h, dp, dq):
        p, q = coords[h]
        return place(h, turn(p, dp), turn(q, dq))

    def start(src, dst, kind, recv_sem, target):
        pltpu.make_async_remote_copy(
            src_ref=src, dst_ref=dst, send_sem=send_sem.at[kind], recv_sem=recv_sem,
            device_id=(target, sec), device_id_type=MESH,
        ).start()

    def arrived(dst, recv_sem):
        pltpu.make_async_remote_copy(
            src_ref=dst, dst_ref=dst, send_sem=send_sem.at[0], recv_sem=recv_sem,
            device_id=(op, sec), device_id_type=MESH,
        ).wait_recv()

    def piece(h, dp, dq, half):
        ref = got.at[h, at(h, dp, dq)]
        return ref if half is None else ref.at[pl.ds(half * 64, 64)]

    def pass_on(h, dp, dq, half, sp, sq):
        ref = piece(h, dp, dq, half)
        rel = (dp - sp) % 4 * 4 + (dq - sq) % 4
        start(ref, ref, h, gather_sem.at[h, rel, 0 if half is None else half], at(h, sp % 4, sq % 4))

    def await_piece(h, dp, dq, half):
        arrived(piece(h, dp, dq, half), gather_sem.at[h, dp * 4 + dq, 0 if half is None else half])

    for h in range(2):
        loads[h].wait()
        for sp in (1, -1):
            pass_on(h, 0, 0, None, sp, 0)
    for h in range(2):
        for sq in (1, -1):
            pass_on(h, 0, 0, None, 0, sq)

    def scale(part):
        for k in (2 * part, 2 * part + 1):
            loads[3 + k].wait()

        @pl.loop(2 * part, 2 * part + 2)
        def _(k):
            @pl.loop(0, 32, unroll=8)
            def _(s):
                level = cpl_ref[k, s]
                coef = jnp.where(
                    level == 0, COEFS[0], jnp.where(level == 1, COEFS[1], jnp.where(level == 2, COEFS[2], COEFS[3]))
                )
                scaled[k, s] = (left[k, s].astype(F32) * coef).astype(BF16)

    def feed(unit, base, lhs, reg):
        for n in range(lhs.shape[0] // 64):
            pltpu.matmul_acc_lhs(acc[unit][base + n], lhs[n * 64 : n * 64 + 64], reg if n == 0 else None)

    def in_turns(steps, issue, drain, unroll):
        issue(0, 0)

        @pl.loop(0, steps // unroll - 1)
        def _(i):
            for u in range(unroll):
                issue(i * unroll + u + 1, (u + 1) % unroll)
                drain(i * unroll + u, u)

        for u in range(unroll):
            t = steps - unroll + u
            if u + 1 < unroll:
                issue(t + 1, u + 1)
            drain(t, u)

    def images(count, which):
        def place_of(i):
            h, dz, other = which(i)
            j = x // 2
            j = j + other * (1 - 2 * j)
            zz = lax.rem(z + dz, 4)
            return h, zz * 4 + 2 * j, pl.ds(pl.multiple_of(zz * 32 + j * 16, 16), 16)

        def put(ref, h, to, first, second, at_sector):
            for s in range(8):
                two = jnp.concatenate([first[s * 8 : s * 8 + 8], second[s * 8 : s * 8 + 8]], axis=0)
                ref[h * 16 + at_sector + s, to, :] = two.astype(BF16)

        def issue(t, u):
            h, o, _ = place_of(t // 4)
            for unit in range(2):
                pltpu.matmul_push_rhs(right[2 * u + unit], u % 2, unit)
                for n in range(2):
                    feed(unit, 4 * (u % 2) + 2 * n, got[h, o + n], u % 2 if n == 0 else None)

        def drain(t, u):
            h, o, to = place_of(t // 4)
            if u == 0:
                put(full, h, to, got[h, o, :64].astype(F32), got[h, o + 1, :64].astype(F32), 0)
                put(full, h, to, got[h, o, 64:].astype(F32), got[h, o + 1, 64:].astype(F32), 8)
            for unit in range(2):
                mine = acc[unit][4 * (u % 2) : 4 * (u % 2) + 4]
                for n in range(2):
                    put(image.at[2 * u + unit], h, to, pltpu.matmul_pop(mine[n]), pltpu.matmul_pop(mine[2 + n]), 8 * n)

        in_turns(4 * count, issue, drain, 4)

    for h in range(2):
        for dp, half, sp in ((3, 0, 1), (1, 1, -1)):
            await_piece(h, dp, 0, None)
            pass_on(h, dp, 0, half, sp, 0)
            for sq in (1, -1):
                pass_on(h, dp, 0, None, 0, sq)
    for h in range(2):
        for dq, half, sq in ((3, 0, 1), (1, 1, -1)):
            await_piece(h, 0, dq, None)
            pass_on(h, 0, dq, half, 0, sq)
    loads[2].wait()
    images(2, lambda i: (i, 0, 0))
    scale(0)
    for h in range(2):
        await_piece(h, 2, 0, 0)
        await_piece(h, 2, 0, 1)
        for sq in (1, -1):
            pass_on(h, 2, 0, None, 0, sq)
    scale(1)
    for h in range(2):
        await_piece(h, 0, 2, 0)
        await_piece(h, 0, 2, 1)
    images(2, lambda i: (i, 0, 1))
    scale(2)
    for h in range(2):
        for dp in (3, 1):
            for dq, half, sq in ((3, 0, 1), (1, 1, -1)):
                await_piece(h, dp, dq, None)
                pass_on(h, dp, dq, half, 0, sq)
    images(4, lambda i: (i // 2, 3 + 2 * (i % 2), 0))
    for h in range(2):
        for dq, half, sq in ((3, 0, 1), (1, 1, -1)):
            await_piece(h, 2, dq, None)
            pass_on(h, 2, dq, half, 0, sq)
    scale(3)
    images(3, lambda i: (i // 2, 3 + 2 * i + 3 * (i // 2), 1 - i // 2))
    for h in range(2):
        for dp in (3, 1):
            for half in range(2):
                await_piece(h, dp, 2, half)
    images(3, lambda i: (1 - i // 2, 3 + 2 * i + 3 * (i // 2), 1 - i // 2))
    for h in range(2):
        for half in range(2):
            await_piece(h, 2, 2, half)
    images(2, lambda i: (i, 2, 1))

    span = 32 // CHUNKS * 8

    def source(k, s):
        return lax.rem(src_ref[k, s], 32)

    def sigma_chunk(c):
        def issue(t, u):
            for t2 in range(4):
                for e in range(2):
                    s = 2 * (c * (16 // CHUNKS) + t) + e
                    rhs = jnp.concatenate([image[k, source(k, s)] for k in (2 * t2, 2 * t2 + 1)], axis=0)
                    lhs = jnp.concatenate([scaled[2 * t2, s], scaled[2 * t2 + 1, s]], axis=1)
                    pltpu.matmul_push_rhs(rhs, t2 % 2, e)
                    feed(e, 2 * (u % 2), lhs, t2 % 2)

        def drain(t, u):
            rows = pl.ds(pl.multiple_of((c * (16 // CHUNKS) + t) * 16, 16), 16)
            for n in range(2):
                first, second = pltpu.matmul_pop(acc[0][2 * (u % 2) + n]), pltpu.matmul_pop(acc[1][2 * (u % 2) + n])
                for o in range(8):
                    two = jnp.concatenate([first[o * 8 : o * 8 + 8], second[o * 8 : o * 8 + 8]], axis=0).astype(BF16)
                    parts[0, 2 * n + o // 4, o % 4, rows, :] = two[:, :128]
                    parts[1, o % 4, 2 * n + o // 4, rows, :] = two[:, 128:]

        in_turns(16 // CHUNKS, issue, drain, 4)

    steps = ((0, 1), (1, 3))

    def rows_of(c, half):
        return pl.ds(c * span + half * (span // 2), span // 2)

    def sum1(c):
        for h in range(2):
            p, q = coords[h]
            for d, step in steps:
                start(parts.at[h, turn(q, 2), :, rows_of(c, d), :], hop1.at[h, d, c], 2, sum_sem.at[0, h, d, c], at(h, 0, step))

    def sum2(c):
        for h in range(2):
            p, q = coords[h]
            for d, step in steps:
                arrived(hop1.at[h, d, c], sum_sem.at[0, h, d, c])
                near = turn(q, step)
                old = parts[h, near, :, rows_of(c, d), :].astype(F32)
                parts[h, near, :, rows_of(c, d), :] = (old + hop1[h, d, c].astype(F32)).astype(BF16)
                start(parts.at[h, near, :, pl.ds(c * span, span), :], hop2.at[h, d, c], 3, sum_sem.at[1, h, d, c], at(h, 0, step))

    def sum3(c):
        for h in range(2):
            p, q = coords[h]
            for d, step in steps:
                arrived(hop2.at[h, d, c], sum_sem.at[1, h, d, c])
            rows = pl.ds(c * span, span)
            total = parts[h, q, :, rows, :].astype(F32) + hop2[h, 0, c].astype(F32) + hop2[h, 1, c].astype(F32)
            kept[h, :, rows, :] = total.astype(BF16)
            for d, step in steps:
                start(kept.at[h, turn(p, 2), rows_of(c, d), :], hop3.at[h, d, c], 4, sum_sem.at[2, h, d, c], at(h, step, 0))

    def sum4(c):
        for h in range(2):
            p, q = coords[h]
            for d, step in steps:
                arrived(hop3.at[h, d, c], sum_sem.at[2, h, d, c])
                near = turn(p, step)
                old = kept[h, near, rows_of(c, d), :].astype(F32)
                kept[h, near, rows_of(c, d), :] = (old + hop3[h, d, c].astype(F32)).astype(BF16)
                start(kept.at[h, near, pl.ds(c * span, span), :], hop4.at[h, d, c], 5, sum_sem.at[3, h, d, c], at(h, step, 0))

    def sum5(c):
        for h in range(2):
            p, q = coords[h]
            for d, step in steps:
                arrived(hop4.at[h, d, c], sum_sem.at[3, h, d, c])
            rows = pl.ds(c * span, span)
            total = kept[h, p, rows, :].astype(F32) + hop4[h, 0, c].astype(F32) + hop4[h, 1, c].astype(F32)
            sig_ref[rows, pl.ds(h * 128, 128)] = total * (128 ** -0.5)

    def mix(ks, turning=False):
        none = jnp.zeros((128, 128), BF16)

        def issue(t, u):
            for j in range(2):
                rhs = jnp.concatenate([full[source(ks[j], 2 * t + n)] for n in range(2)], axis=0)
                pltpu.matmul_push_rhs(rhs, u % 2, j)
                for n in range(2):
                    one = left[ks[j], 2 * t + n]
                    lhs = jnp.concatenate([one, none] if n == 0 else [none, one], axis=1)
                    feed(j, 4 * (u % 2) + 2 * n, lhs, u % 2 if n == 0 else None)

        def drain(t, u):
            if turning:
                for n in range(2):
                    full_t[t, :, n * 128 : n * 128 + 128] = full[2 * t + n].T
            for j in range(2):
                for n in range(4):
                    zed[j, t, n * 64 : n * 64 + 64, :] = pltpu.matmul_pop(acc[j][4 * (u % 2) + n]).astype(BF16)

        in_turns(16, issue, drain, 4)

    def renorm(slot):
        @pl.loop(0, 2)
        def _(i):
            for e in range(8):
                for j in range(2):
                    pltpu.matmul_push_rhs(zed[j, 8 * i + e], e % 2, j)
                    feed(j, 0, full_t[8 * i + e], e % 2)

        for j in range(2):
            for n in range(4):
                block[slot + j, n * 64 : n * 64 + 64, :] = (pltpu.matmul_pop(acc[j][n]) * (4096 ** -0.5)).astype(BF16)

    def push(src, dst, kind, recv_sem, target):
        pltpu.make_async_remote_copy(
            src_ref=src, dst_ref=dst, send_sem=send_sem.at[kind], recv_sem=recv_sem,
            device_id=(op, target), device_id_type=MESH,
        ).start()

    def ship(slot, dy, target):
        push(block.at[slot], ren_ref.at[sec], 6, swap_sem.at[dy, core], target)

    def half_rows(d):
        return pl.ds(d * 128, 128)

    def ship_far():
        for j in range(2):
            for d, step in steps:
                push(block.at[j, half_rows(d)], relay.at[d, j], 6, relay_sem.at[d, j], turn(y, step) * 2 + core)

    def relay_far():
        for j in range(2):
            for d, step in steps:
                arrived(relay.at[d, j], relay_sem.at[d, j])
                sender = turn(y, 4 - step) * 2 + core
                push(relay.at[d, j], ren_ref.at[sender, half_rows(d)], 7, far_sem.at[d, core], turn(y, step) * 2 + j)

    def swapped(dy, sender_core):
        sender = turn(y, 4 - dy) * 2 + sender_core
        arrived(ren_ref.at[sender], swap_sem.at[dy, sender_core])

    far = [turn(y, 2) * 2 + j for j in range(2)]
    near = [[turn(y, dy) * 2 + j for dy in (1, 3)] for j in range(2)]
    here = [2 * y + j for j in range(2)]

    sigma_chunk(0)
    sum1(0)
    sigma_chunk(1)
    sum1(1)
    mix(far, turning=True)
    sum2(0)
    renorm(0)
    ship_far()
    sum2(1)
    mix(near[0])
    sum3(0)
    renorm(2)
    ship(2, 1, near[0][0])
    ship(3, 3, near[0][1])
    relay_far()
    sum4(0)
    mix(near[1])
    sum3(1)
    renorm(4)
    ship(4, 1, near[1][0])
    ship(5, 3, near[1][1])
    sum5(0)
    mix(here)
    sum4(1)
    renorm(6)
    ship(7 - core, 0, 2 * y + 1 - core)
    own = pltpu.make_async_copy(block.at[6 + core], ren_ref.at[sec], own_sem)
    own.start()
    sum5(1)
    for dy in (1, 3):
        for c in range(2):
            swapped(dy, c)
    for c in range(2):
        for d in range(2):
            arrived(ren_ref.at[turn(y, 2) * 2 + c, half_rows(d)], far_sem.at[d, c])
    swapped(0, 1 - core)
    own.wait()
    all_sent = (got.at[0, pl.ds(0, 15)], got.at[1, pl.ds(0, 15)], hop1, hop2, hop3, hop4, block.at[pl.ds(0, 7)], relay)
    for kind, ref in enumerate(all_sent):
        pltpu.make_async_copy(ref, ref, send_sem.at[kind]).wait()


def with_totals(*refs):
    totals = [pltpu.ACC(unit)((64, 256), F32) for unit in range(2) for _ in range(8)]
    pl.run_scoped(functools.partial(kernel, *refs), *totals)


def finish(sig_ref, ren_ref, sigma_ref, renorm_ref, sig, sigma, narrow, wide, in_sem, out_sem):
    come = [pltpu.make_async_copy(ren_ref.at[i], narrow.at[i], in_sem.at[i]) for i in range(8)]
    come.append(pltpu.make_async_copy(sig_ref, sig, in_sem.at[8]))
    go = [pltpu.make_async_copy(wide.at[i], renorm_ref.at[i], out_sem.at[i]) for i in range(8)]
    go.append(pltpu.make_async_copy(sigma, sigma_ref, out_sem.at[8]))
    for copy in come:
        copy.start()
    for i in range(8):
        come[i].wait()
        wide[i] = narrow[i].astype(F32)
        go[i].start()
    come[8].wait()
    sigma[...] = sig[...].astype(BF16)
    go[8].start()
    for copy in go:
        copy.wait()


def body(psi, left_env, right_env, source, coupling):
    vm = pltpu.VMEM
    rows = 256 // CHUNKS
    sig, ren = pl.pallas_call(
        with_totals,
        out_shape=(jax.ShapeDtypeStruct((256, 256), F32), jax.ShapeDtypeStruct((8, 256, 256), BF16)),
        in_specs=[pl.BlockSpec(memory_space=pl.ANY)] * 3 + [pl.BlockSpec(memory_space=pltpu.SMEM)] * 2,
        out_specs=(pl.BlockSpec(memory_space=pltpu.VMEM), pl.BlockSpec(memory_space=pl.ANY)),
        scratch_shapes=[
            vm((8, 32, 128, 128), BF16),
            vm((8, 32, 128, 128), BF16),
            vm((8, 256, 256), BF16),
            vm((2, 16, 128, 256), BF16),
            vm((32, 128, 256), BF16),
            vm((16, 256, 256), BF16),
            vm((8, 32, 128, 256), BF16),
            vm((2, 16, 256, 256), BF16),
            vm((2, 4, 4, 256, 128), BF16),
            vm((8, 256, 256), BF16),
            vm((2, 2, CHUNKS, 4, rows // 2, 128), BF16),
            vm((2, 2, CHUNKS, 4, rows, 128), BF16),
            vm((2, 4, 256, 128), BF16),
            vm((2, 2, CHUNKS, rows // 2, 128), BF16),
            vm((2, 2, CHUNKS, rows, 128), BF16),
            vm((2, 2, 128, 256), BF16),
            pltpu.SemaphoreType.DMA((11,)),
            pltpu.SemaphoreType.DMA((8,)),
            pltpu.SemaphoreType.DMA((2, 16, 2)),
            pltpu.SemaphoreType.DMA((4, 2, 2, CHUNKS)),
            pltpu.SemaphoreType.DMA((4, 2)),
            pltpu.SemaphoreType.DMA((2, 2)),
            pltpu.SemaphoreType.DMA((2, 2)),
            pltpu.SemaphoreType.DMA,
        ],
        compiler_params=pltpu.CompilerParams(
            collective_id=0, has_side_effects=True, vmem_limit_bytes=60 * 1024 * 1024
        ),
        cost_estimate=pl.CostEstimate(flops=13 * 10**9, bytes_accessed=12 * 2**20, transcendentals=0),
        name="dmrg_step",
    )(psi.reshape(256, 256), left_env, right_env.reshape(8, 256, 256), source, coupling)
    sigma, renorm = pl.pallas_call(
        finish,
        out_shape=(jax.ShapeDtypeStruct((256, 256), BF16), jax.ShapeDtypeStruct((8, 256, 256), F32)),
        in_specs=[pl.BlockSpec(memory_space=pl.ANY)] * 2,
        out_specs=(pl.BlockSpec(memory_space=pl.ANY), pl.BlockSpec(memory_space=pl.ANY)),
        scratch_shapes=[
            vm((256, 256), F32),
            vm((256, 256), BF16),
            vm((8, 256, 256), BF16),
            vm((8, 256, 256), F32),
            pltpu.SemaphoreType.DMA((9,)),
            pltpu.SemaphoreType.DMA((9,)),
        ],
        compiler_params=pltpu.CompilerParams(vmem_limit_bytes=60 * 1024 * 1024),
        name="finish",
    )(sig, ren)
    return sigma.reshape(32, 8, 256), renorm[None]


def solution(mesh):
    placed = (
        P("sec", "op", None),
        P("op", "sec", None, None),
        P("op", "sec", None, None),
        P("op", "sec"),
        P("op", "sec"),
    )
    return jax.shard_map(
        body,
        mesh=mesh,
        in_specs=placed,
        out_specs=(P("sec", "op", None), P(("op", "sec"), None, None, None)),
        check_vma=False,
    )
```

```python
import functools

import jax
import jax.numpy as jnp
from jax import lax
from jax.experimental import pallas as pl
from jax.experimental.pallas import tpu as pltpu
from jax.sharding import PartitionSpec as P

COEFS = (1.0, -0.5773503, 0.8164966, -0.7071068)
MESH = pl.DeviceIdType.MESH
F32 = jnp.float32
BF16 = jnp.bfloat16
CUTS = (0, 8, 20, 32)
CHUNKS = len(CUTS) - 1


def turn(a, step):
    return lax.rem(a + step, 4)


def kernel(
    psi_ref, left_ref, right_ref, src_hbm, cpl_hbm,
    sig_out, ren_ref,
    src_ref, cpl_ref, sig_ref, left, scaled, right, got, full, full_t, image, zed, parts, block,
    hop1, hop2, kept, hop3, hop4, relay,
    load_sem, send_sem, gather_sem, sum_sem, swap_sem, relay_sem, far_sem, own_sem, leave_sem,
    *totals,
):
    acc = (totals[:8], totals[8:])
    op, sec = lax.axis_index("op"), lax.axis_index("sec")
    z, x = op // 4, op % 4
    y, core = sec // 2, sec % 2
    coords = ((x, z), (z, x))

    barrier = pltpu.get_barrier_semaphore()
    peers = [(z * 4 + turn(x, 1), sec), (z * 4 + turn(x, 3), sec), (turn(z, 1) * 4 + x, sec), (turn(z, 3) * 4 + x, sec)]
    peers += [(op, lax.rem(sec + i, 8)) for i in range(1, 8)]
    for peer in peers:
        pl.semaphore_signal(barrier, inc=1, device_id=peer, device_id_type=MESH)
    loads = [
        pltpu.make_async_copy(psi_ref.at[pl.ds(h * 128, 128)], got.at[h, op], load_sem.at[h]) for h in range(2)
    ]
    loads.append(pltpu.make_async_copy(right_ref, right, load_sem.at[2]))
    loads += [pltpu.make_async_copy(left_ref.at[k], left.at[k], load_sem.at[3 + k]) for k in range(8)]
    loads.append(pltpu.make_async_copy(cpl_hbm, cpl_ref, load_sem.at[11]))
    loads.append(pltpu.make_async_copy(src_hbm, src_ref, load_sem.at[12]))
    for copy in loads[:2] + loads[11:] + loads[2:11]:
        copy.start()
    pl.semaphore_wait(barrier, len(peers))

    def place(h, p, q):
        return q * 4 + p if h == 0 else p * 4 + q

    def at(h, dp, dq):
        p, q = coords[h]
        return place(h, turn(p, dp), turn(q, dq))

    def start(src, dst, kind, recv_sem, target):
        pltpu.make_async_remote_copy(
            src_ref=src, dst_ref=dst, send_sem=send_sem.at[kind], recv_sem=recv_sem,
            device_id=(target, sec), device_id_type=MESH,
        ).start()

    def arrived(dst, recv_sem):
        pltpu.make_async_remote_copy(
            src_ref=dst, dst_ref=dst, send_sem=send_sem.at[0], recv_sem=recv_sem,
            device_id=(op, sec), device_id_type=MESH,
        ).wait_recv()

    def piece(h, dp, dq, half):
        ref = got.at[h, at(h, dp, dq)]
        return ref if half is None else ref.at[pl.ds(half * 64, 64)]

    def pass_on(h, dp, dq, half, sp, sq):
        ref = piece(h, dp, dq, half)
        rel = (dp - sp) % 4 * 4 + (dq - sq) % 4
        start(ref, ref, h, gather_sem.at[h, rel, 0 if half is None else half], at(h, sp % 4, sq % 4))

    def await_piece(h, dp, dq, half):
        arrived(piece(h, dp, dq, half), gather_sem.at[h, dp * 4 + dq, 0 if half is None else half])

    for h in range(2):
        loads[h].wait()
        for sp in (1, -1):
            pass_on(h, 0, 0, None, sp, 0)
    for h in range(2):
        for sq in (1, -1):
            pass_on(h, 0, 0, None, 0, sq)

    def scale(part):
        for k in (2 * part, 2 * part + 1):
            loads[3 + k].wait()

        @pl.loop(2 * part, 2 * part + 2)
        def _(k):
            @pl.loop(0, 32, unroll=8)
            def _(s):
                level = cpl_ref[k, s]
                coef = jnp.where(
                    level == 0, COEFS[0], jnp.where(level == 1, COEFS[1], jnp.where(level == 2, COEFS[2], COEFS[3]))
                )
                scaled[k, s] = (left[k, s].astype(F32) * coef).astype(BF16)

    def feed(unit, base, lhs, reg):
        for n in range(lhs.shape[0] // 64):
            pltpu.matmul_acc_lhs(acc[unit][base + n], lhs[n * 64 : n * 64 + 64], reg if n == 0 else None)

    def in_turns(steps, issue, drain, unroll):
        issue(0, 0)

        @pl.loop(0, steps // unroll - 1)
        def _(i):
            for u in range(unroll):
                issue(i * unroll + u + 1, (u + 1) % unroll)
                drain(i * unroll + u, u)

        for u in range(unroll):
            t = steps - unroll + u
            if u + 1 < unroll:
                issue(t + 1, u + 1)
            drain(t, u)

    waiting = []

    def unit_image(h, dz, other):
        j = x // 2
        if other:
            j = 1 - j
        zz = turn(z, dz)
        o, to = zz * 4 + 2 * j, pl.ds(pl.multiple_of(zz * 32 + j * 16, 16), 16)

        def put(ref, first, second, at_sector):
            for s in range(8):
                two = jnp.concatenate([first[s * 8 : s * 8 + 8], second[s * 8 : s * 8 + 8]], axis=0)
                ref[h * 16 + at_sector + s, to, :] = two.astype(BF16)

        def drain(u):
            if u == 0:
                put(full, got[h, o, :64].astype(F32), got[h, o + 1, :64].astype(F32), 0)
                put(full, got[h, o, 64:].astype(F32), got[h, o + 1, 64:].astype(F32), 8)
            for unit in range(2):
                mine = acc[unit][4 * (u % 2) : 4 * (u % 2) + 4]
                for n in range(2):
                    put(image.at[2 * u + unit], pltpu.matmul_pop(mine[n]), pltpu.matmul_pop(mine[2 + n]), 8 * n)

        for u in range(4):
            for unit in range(2):
                pltpu.matmul_push_rhs(right[2 * u + unit], u % 2, unit)
                for n in range(2):
                    feed(unit, 4 * (u % 2) + 2 * n, got[h, o + n], u % 2 if n == 0 else None)
            if waiting:
                waiting.pop()()
            waiting.append(functools.partial(drain, u))

    both_ways = ((3, 0, 1), (1, 1, -1))

    def from_p(h):
        for dp, half, sp in both_ways:
            await_piece(h, dp, 0, None)
            pass_on(h, dp, 0, half, sp, 0)
            for sq in (1, -1):
                pass_on(h, dp, 0, None, 0, sq)

    def from_p2(h):
        for half in range(2):
            await_piece(h, 2, 0, half)
        for sq in (1, -1):
            pass_on(h, 2, 0, None, 0, sq)

    def from_q(h, dp):
        for dq, half, sq in both_ways:
            await_piece(h, dp, dq, None)
            pass_on(h, dp, dq, half, 0, sq)

    def from_q2(h, dp):
        for half in range(2):
            await_piece(h, dp, 2, half)

    loads[11].wait()
    loads[12].wait()
    scale(0)
    from_p(0)
    from_p(1)
    scale(1)
    from_q(0, 0)
    from_q(1, 0)
    loads[2].wait()
    unit_image(0, 0, 0)
    unit_image(1, 0, 0)
    from_p2(0)
    from_p2(1)
    unit_image(0, 0, 1)
    from_q2(0, 0)
    from_q2(1, 0)
    unit_image(1, 0, 1)
    scale(2)
    from_q(0, 3)
    from_q(1, 3)
    scale(3)
    from_q(0, 1)
    from_q(1, 1)
    unit_image(0, 3, 0)
    unit_image(1, 3, 0)
    unit_image(0, 1, 0)
    unit_image(1, 1, 0)
    from_q(0, 2)
    from_q(1, 2)
    unit_image(0, 3, 1)
    unit_image(0, 1, 1)
    unit_image(1, 2, 0)
    from_q2(0, 3)
    from_q2(0, 1)
    unit_image(0, 2, 0)
    from_q2(1, 3)
    unit_image(1, 3, 1)
    from_q2(1, 1)
    unit_image(1, 1, 1)
    from_q2(0, 2)
    unit_image(0, 2, 1)
    from_q2(1, 2)
    unit_image(1, 2, 1)
    waiting.pop()()

    def source(k, s):
        return lax.rem(src_ref[k, s], 32)

    def sigma_chunk(c):
        def issue(t, u):
            for t2 in range(4):
                for e in range(2):
                    s = CUTS[c] + 2 * t + e
                    rhs = jnp.concatenate([image[k, source(k, s)] for k in (2 * t2, 2 * t2 + 1)], axis=0)
                    lhs = jnp.concatenate([scaled[2 * t2, s], scaled[2 * t2 + 1, s]], axis=1)
                    pltpu.matmul_push_rhs(rhs, t2 % 2, e)
                    feed(e, 2 * (u % 2), lhs, t2 % 2)

        def drain(t, u):
            rows = pl.ds(pl.multiple_of(CUTS[c] * 8 + t * 16, 16), 16)
            for n in range(2):
                first, second = pltpu.matmul_pop(acc[0][2 * (u % 2) + n]), pltpu.matmul_pop(acc[1][2 * (u % 2) + n])
                for o in range(8):
                    two = jnp.concatenate([first[o * 8 : o * 8 + 8], second[o * 8 : o * 8 + 8]], axis=0).astype(BF16)
                    parts[0, 2 * n + o // 4, o % 4, rows, :] = two[:, :128]
                    parts[1, o % 4, 2 * n + o // 4, rows, :] = two[:, 128:]

        in_turns((CUTS[c + 1] - CUTS[c]) // 2, issue, drain, 2)

    steps = ((0, 1), (1, 3))

    def all_rows(c):
        return pl.ds(CUTS[c] * 8, (CUTS[c + 1] - CUTS[c]) * 8)

    def half_of(c, d):
        span = (CUTS[c + 1] - CUTS[c]) * 4
        return pl.ds(CUTS[c] * 8 + d * span, span)

    def small(c):
        return pl.ds(CUTS[c] * 4, (CUTS[c + 1] - CUTS[c]) * 4)

    def sum1(c):
        for h in range(2):
            p, q = coords[h]
            for d, step in steps:
                start(
                    parts.at[h, turn(q, 2), :, half_of(c, d), :], hop1.at[h, d, :, small(c), :],
                    2, sum_sem.at[0, h, d, c], at(h, 0, step),
                )

    def sum2(c):
        for h in range(2):
            p, q = coords[h]
            for d, step in steps:
                arrived(hop1.at[h, d, :, small(c), :], sum_sem.at[0, h, d, c])
                near = turn(q, step)
                old = parts[h, near, :, half_of(c, d), :].astype(F32)
                parts[h, near, :, half_of(c, d), :] = (old + hop1[h, d, :, small(c), :].astype(F32)).astype(BF16)
                start(
                    parts.at[h, near, :, all_rows(c), :], hop2.at[h, d, :, all_rows(c), :],
                    3, sum_sem.at[1, h, d, c], at(h, 0, step),
                )

    def sum3(c):
        for h in range(2):
            p, q = coords[h]
            rows = all_rows(c)
            for d, step in steps:
                arrived(hop2.at[h, d, :, rows, :], sum_sem.at[1, h, d, c])
            total = parts[h, q, :, rows, :].astype(F32)
            total = total + hop2[h, 0, :, rows, :].astype(F32) + hop2[h, 1, :, rows, :].astype(F32)
            kept[h, :, rows, :] = total.astype(BF16)
            for d, step in steps:
                start(
                    kept.at[h, turn(p, 2), half_of(c, d), :], hop3.at[h, d, small(c), :],
                    4, sum_sem.at[2, h, d, c], at(h, step, 0),
                )

    def sum4(c):
        for h in range(2):
            p, q = coords[h]
            for d, step in steps:
                arrived(hop3.at[h, d, small(c), :], sum_sem.at[2, h, d, c])
                near = turn(p, step)
                old = kept[h, near, half_of(c, d), :].astype(F32)
                kept[h, near, half_of(c, d), :] = (old + hop3[h, d, small(c), :].astype(F32)).astype(BF16)
                start(
                    kept.at[h, near, all_rows(c), :], hop4.at[h, d, all_rows(c), :],
                    5, sum_sem.at[3, h, d, c], at(h, step, 0),
                )

    leaves = []

    def sum5(c):
        rows = all_rows(c)
        for h in range(2):
            p, q = coords[h]
            for d, step in steps:
                arrived(hop4.at[h, d, rows, :], sum_sem.at[3, h, d, c])
            total = kept[h, p, rows, :].astype(F32) + hop4[h, 0, rows, :].astype(F32) + hop4[h, 1, rows, :].astype(F32)
            sig_ref[rows, pl.ds(h * 128, 128)] = total * (128 ** -0.5)
        leaves.append(pltpu.make_async_copy(sig_ref.at[rows, :], sig_out.at[rows, :], leave_sem.at[c]))
        leaves[-1].start()

    def mix(ks, turning=False):
        none = jnp.zeros((128, 128), BF16)

        def issue(t, u):
            for j in range(2):
                rhs = jnp.concatenate([full[source(ks[j], 2 * t + n)] for n in range(2)], axis=0)
                pltpu.matmul_push_rhs(rhs, u % 2, j)
                for n in range(2):
                    one = left[ks[j], 2 * t + n]
                    lhs = jnp.concatenate([one, none] if n == 0 else [none, one], axis=1)
                    feed(j, 4 * (u % 2) + 2 * n, lhs, u % 2 if n == 0 else None)

        def drain(t, u):
            if turning:
                for n in range(2):
                    full_t[t, :, n * 128 : n * 128 + 128] = full[2 * t + n].T
            for j in range(2):
                for n in range(4):
                    zed[j, t, n * 64 : n * 64 + 64, :] = pltpu.matmul_pop(acc[j][4 * (u % 2) + n]).astype(BF16)

        in_turns(16, issue, drain, 4)

    def renorm(slot):
        @pl.loop(0, 2)
        def _(i):
            for e in range(8):
                for j in range(2):
                    pltpu.matmul_push_rhs(zed[j, 8 * i + e], e % 2, j)
                    feed(j, 0, full_t[8 * i + e], e % 2)

        for j in range(2):
            for n in range(4):
                block[slot + j, n * 64 : n * 64 + 64, :] = (pltpu.matmul_pop(acc[j][n]) * (4096 ** -0.5)).astype(BF16)

    def push(src, dst, kind, recv_sem, target):
        pltpu.make_async_remote_copy(
            src_ref=src, dst_ref=dst, send_sem=send_sem.at[kind], recv_sem=recv_sem,
            device_id=(op, target), device_id_type=MESH,
        ).start()

    def ship(slot, dy, target):
        push(block.at[slot], ren_ref.at[sec], 6, swap_sem.at[dy, core], target)

    def half_rows(d):
        return pl.ds(d * 128, 128)

    def ship_far():
        for j in range(2):
            for d, step in steps:
                push(block.at[j, half_rows(d)], relay.at[d, j], 6, relay_sem.at[d, j], turn(y, step) * 2 + core)

    def relay_far():
        for j in range(2):
            for d, step in steps:
                arrived(relay.at[d, j], relay_sem.at[d, j])
                sender = turn(y, 4 - step) * 2 + core
                push(relay.at[d, j], ren_ref.at[sender, half_rows(d)], 7, far_sem.at[d, core], turn(y, step) * 2 + j)

    def swapped(dy, sender_core):
        sender = turn(y, 4 - dy) * 2 + sender_core
        arrived(ren_ref.at[sender], swap_sem.at[dy, sender_core])

    far = [turn(y, 2) * 2 + j for j in range(2)]
    near = [[turn(y, dy) * 2 + j for dy in (1, 3)] for j in range(2)]
    here = [2 * y + j for j in range(2)]

    sigma_chunk(0)
    sum1(0)
    mix(far, turning=True)
    renorm(0)
    ship_far()
    sum2(0)
    sigma_chunk(1)
    sum1(1)
    sigma_chunk(2)
    sum1(2)
    sum3(0)
    mix(near[0])
    relay_far()
    sum2(1)
    renorm(2)
    ship(2, 1, near[0][0])
    ship(3, 3, near[0][1])
    sum2(2)
    sum4(0)
    mix(near[1])
    renorm(4)
    ship(4, 1, near[1][0])
    ship(5, 3, near[1][1])
    sum3(1)
    sum5(0)
    mix(here)
    sum3(2)
    sum4(1)
    renorm(6)
    ship(7 - core, 0, 2 * y + 1 - core)
    own = pltpu.make_async_copy(block.at[6 + core], ren_ref.at[sec], own_sem)
    own.start()
    sum4(2)
    sum5(1)
    sum5(2)
    for dy in (1, 3):
        for c in range(2):
            swapped(dy, c)
    for c in range(2):
        for d in range(2):
            arrived(ren_ref.at[turn(y, 2) * 2 + c, half_rows(d)], far_sem.at[d, c])
    swapped(0, 1 - core)
    own.wait()
    for copy in leaves:
        copy.wait()
    all_sent = (got.at[0, pl.ds(0, 15)], got.at[1, pl.ds(0, 15)], hop1, hop2, hop3, hop4, block.at[pl.ds(0, 7)], relay)
    for kind, ref in enumerate(all_sent):
        pltpu.make_async_copy(ref, ref, send_sem.at[kind]).wait()


def with_totals(*refs):
    totals = [pltpu.ACC(unit)((64, 256), F32) for unit in range(2) for _ in range(8)]
    pl.run_scoped(functools.partial(kernel, *refs), *totals)


def finish(sig_ref, ren_ref, sigma_ref, renorm_ref, sig, sigma, narrow, wide, in_sem, out_sem):
    come = [pltpu.make_async_copy(ren_ref.at[i], narrow.at[i], in_sem.at[i]) for i in range(8)]
    come.append(pltpu.make_async_copy(sig_ref, sig, in_sem.at[8]))
    go = [pltpu.make_async_copy(wide.at[i], renorm_ref.at[i], out_sem.at[i]) for i in range(8)]
    go.append(pltpu.make_async_copy(sigma, sigma_ref, out_sem.at[8]))
    for copy in come:
        copy.start()
    for i in range(8):
        come[i].wait()
        wide[i] = narrow[i].astype(F32)
        go[i].start()
    come[8].wait()
    sigma[...] = sig[...].astype(BF16)
    go[8].start()
    for copy in go:
        copy.wait()


def body(psi, left_env, right_env, source, coupling):
    vm = pltpu.VMEM
    sig, ren = pl.pallas_call(
        with_totals,
        out_shape=(jax.ShapeDtypeStruct((256, 256), F32), jax.ShapeDtypeStruct((8, 256, 256), BF16)),
        in_specs=[pl.BlockSpec(memory_space=pl.ANY)] * 5,
        out_specs=(pl.BlockSpec(memory_space=pl.ANY), pl.BlockSpec(memory_space=pl.ANY)),
        scratch_shapes=[
            pltpu.SMEM((8, 32), jnp.int32),
            pltpu.SMEM((8, 32), jnp.int32),
            vm((256, 256), F32),
            vm((8, 32, 128, 128), BF16),
            vm((8, 32, 128, 128), BF16),
            vm((8, 256, 256), BF16),
            vm((2, 16, 128, 256), BF16),
            vm((32, 128, 256), BF16),
            vm((16, 256, 256), BF16),
            vm((8, 32, 128, 256), BF16),
            vm((2, 16, 256, 256), BF16),
            vm((2, 4, 4, 256, 128), BF16),
            vm((8, 256, 256), BF16),
            vm((2, 2, 4, 128, 128), BF16),
            vm((2, 2, 4, 256, 128), BF16),
            vm((2, 4, 256, 128), BF16),
            vm((2, 2, 128, 128), BF16),
            vm((2, 2, 256, 128), BF16),
            vm((2, 2, 128, 256), BF16),
            pltpu.SemaphoreType.DMA((13,)),
            pltpu.SemaphoreType.DMA((8,)),
            pltpu.SemaphoreType.DMA((2, 16, 2)),
            pltpu.SemaphoreType.DMA((4, 2, 2, CHUNKS)),
            pltpu.SemaphoreType.DMA((4, 2)),
            pltpu.SemaphoreType.DMA((2, 2)),
            pltpu.SemaphoreType.DMA((2, 2)),
            pltpu.SemaphoreType.DMA,
            pltpu.SemaphoreType.DMA((CHUNKS,)),
        ],
        compiler_params=pltpu.CompilerParams(
            collective_id=0, has_side_effects=True, vmem_limit_bytes=60 * 1024 * 1024
        ),
        cost_estimate=pl.CostEstimate(flops=13 * 10**9, bytes_accessed=12 * 2**20, transcendentals=0),
        name="dmrg_step",
    )(psi.reshape(256, 256), left_env, right_env.reshape(8, 256, 256), source, coupling)
    sigma, renorm = pl.pallas_call(
        finish,
        out_shape=(jax.ShapeDtypeStruct((256, 256), BF16), jax.ShapeDtypeStruct((8, 256, 256), F32)),
        in_specs=[pl.BlockSpec(memory_space=pl.ANY)] * 2,
        out_specs=(pl.BlockSpec(memory_space=pl.ANY), pl.BlockSpec(memory_space=pl.ANY)),
        scratch_shapes=[
            vm((256, 256), F32),
            vm((256, 256), BF16),
            vm((8, 256, 256), BF16),
            vm((8, 256, 256), F32),
            pltpu.SemaphoreType.DMA((9,)),
            pltpu.SemaphoreType.DMA((9,)),
        ],
        compiler_params=pltpu.CompilerParams(vmem_limit_bytes=60 * 1024 * 1024),
        name="finish",
    )(sig, ren)
    return sigma.reshape(32, 8, 256), renorm[None]


def solution(mesh):
    placed = (
        P("sec", "op", None),
        P("op", "sec", None, None),
        P("op", "sec", None, None),
        P("op", "sec"),
        P("op", "sec"),
    )
    return jax.shard_map(
        body,
        mesh=mesh,
        in_specs=placed,
        out_specs=(P("sec", "op", None), P(("op", "sec"), None, None, None)),
        check_vma=False,
    )
```

```python
import functools

import jax
import jax.numpy as jnp
from jax import lax
from jax.experimental import pallas as pl
from jax.experimental.pallas import tpu as pltpu
from jax.sharding import PartitionSpec as P

COEFS = (1.0, -0.5773503, 0.8164966, -0.7071068)
MESH = pl.DeviceIdType.MESH
F32 = jnp.float32
BF16 = jnp.bfloat16
CUTS = (0, 8, 20, 32)
CHUNKS = len(CUTS) - 1


def turn(a, step):
    return lax.rem(a + step, 4)


def kernel(
    psi_ref, left_ref, right_ref, src_hbm, cpl_hbm,
    sig_out, ren_ref,
    src_ref, cpl_ref, sig_ref, left, scaled, right, got, full, full_t, image, zed, parts, block,
    hop1, hop2, kept, hop3, hop4, relay,
    load_sem, send_sem, gather_sem, sum_sem, swap_sem, relay_sem, far_sem, own_sem, leave_sem,
    *totals,
):
    acc = (totals[:8], totals[8:])
    op, sec = lax.axis_index("op"), lax.axis_index("sec")
    z, x = op // 4, op % 4
    y, core = sec // 2, sec % 2
    flows = (core, 1 - core)
    coords = tuple((x + f * (z - x), z + f * (x - z)) for f in flows)

    def step_of(a, step):
        return lax.rem(a + (1 + 2 * core) * (step % 4), 4)


    barrier = pltpu.get_barrier_semaphore()
    peers = [(z * 4 + turn(x, 1), sec), (z * 4 + turn(x, 3), sec), (turn(z, 1) * 4 + x, sec), (turn(z, 3) * 4 + x, sec)]
    peers += [(op, lax.rem(sec + i, 8)) for i in range(1, 8)]
    for peer in peers:
        pl.semaphore_signal(barrier, inc=1, device_id=peer, device_id_type=MESH)
    loads = [
        pltpu.make_async_copy(psi_ref.at[pl.ds(h * 128, 128)], got.at[h, op], load_sem.at[h]) for h in range(2)
    ]
    loads.append(pltpu.make_async_copy(right_ref, right, load_sem.at[2]))
    loads += [pltpu.make_async_copy(left_ref.at[k], left.at[k], load_sem.at[3 + k]) for k in range(8)]
    loads.append(pltpu.make_async_copy(cpl_hbm, cpl_ref, load_sem.at[11]))
    loads.append(pltpu.make_async_copy(src_hbm, src_ref, load_sem.at[12]))
    for copy in loads[:2] + loads[11:] + loads[2:11]:
        copy.start()
    pl.semaphore_wait(barrier, len(peers))

    def place(h, p, q):
        return q * 4 + p + flows[h] * (3 * p - 3 * q)

    def at(h, dp, dq):
        p, q = coords[h]
        return place(h, step_of(p, dp), step_of(q, dq))

    def start(src, dst, kind, recv_sem, target):
        pltpu.make_async_remote_copy(
            src_ref=src, dst_ref=dst, send_sem=send_sem.at[kind], recv_sem=recv_sem,
            device_id=(target, sec), device_id_type=MESH,
        ).start()

    def arrived(dst, recv_sem):
        pltpu.make_async_remote_copy(
            src_ref=dst, dst_ref=dst, send_sem=send_sem.at[0], recv_sem=recv_sem,
            device_id=(op, sec), device_id_type=MESH,
        ).wait_recv()

    def piece(h, dp, dq, half):
        ref = got.at[flows[h], at(h, dp, dq)]
        return ref if half is None else ref.at[pl.ds(half * 64, 64)]

    def pass_on(h, dp, dq, half, sp, sq):
        ref = piece(h, dp, dq, half)
        rel = (dp - sp) % 4 * 4 + (dq - sq) % 4
        start(ref, ref, h, gather_sem.at[h, rel, 0 if half is None else half], at(h, sp % 4, sq % 4))

    def await_piece(h, dp, dq, half):
        arrived(piece(h, dp, dq, half), gather_sem.at[h, dp * 4 + dq, 0 if half is None else half])

    loads[0].wait()
    loads[1].wait()
    for h in range(2):
        for sp in (1, -1):
            pass_on(h, 0, 0, None, sp, 0)
    for h in range(2):
        for sq in (1, -1):
            pass_on(h, 0, 0, None, 0, sq)

    def scale(part):
        for k in (2 * part, 2 * part + 1):
            loads[3 + k].wait()

        @pl.loop(2 * part, 2 * part + 2)
        def _(k):
            @pl.loop(0, 32, unroll=8)
            def _(s):
                level = cpl_ref[k, s]
                coef = jnp.where(
                    level == 0, COEFS[0], jnp.where(level == 1, COEFS[1], jnp.where(level == 2, COEFS[2], COEFS[3]))
                )
                scaled[k, s] = (left[k, s].astype(F32) * coef).astype(BF16)

    def feed(unit, base, lhs, reg):
        for n in range(lhs.shape[0] // 64):
            pltpu.matmul_acc_lhs(acc[unit][base + n], lhs[n * 64 : n * 64 + 64], reg if n == 0 else None)

    def in_turns(steps, issue, drain, unroll):
        issue(0, 0)

        @pl.loop(0, steps // unroll - 1)
        def _(i):
            for u in range(unroll):
                issue(i * unroll + u + 1, (u + 1) % unroll)
                drain(i * unroll + u, u)

        for u in range(unroll):
            t = steps - unroll + u
            if u + 1 < unroll:
                issue(t + 1, u + 1)
            drain(t, u)

    waiting = []

    def unit_image(h, dz, other):
        j = x // 2
        if other:
            j = 1 - j
        zz = step_of(z, dz)
        o, to = zz * 4 + 2 * j, pl.ds(pl.multiple_of(zz * 32 + j * 16, 16), 16)

        def put(ref, first, second, at_sector):
            for s in range(8):
                two = jnp.concatenate([first[s * 8 : s * 8 + 8], second[s * 8 : s * 8 + 8]], axis=0)
                ref[h * 16 + at_sector + s, to, :] = two.astype(BF16)

        def drain(u):
            if u == 0:
                put(full, got[h, o, :64].astype(F32), got[h, o + 1, :64].astype(F32), 0)
                put(full, got[h, o, 64:].astype(F32), got[h, o + 1, 64:].astype(F32), 8)
            for unit in range(2):
                mine = acc[unit][4 * (u % 2) : 4 * (u % 2) + 4]
                for n in range(2):
                    put(image.at[2 * u + unit], pltpu.matmul_pop(mine[n]), pltpu.matmul_pop(mine[2 + n]), 8 * n)

        for u in range(4):
            for unit in range(2):
                pltpu.matmul_push_rhs(right[2 * u + unit], u % 2, unit)
                for n in range(2):
                    feed(unit, 4 * (u % 2) + 2 * n, got[h, o + n], u % 2 if n == 0 else None)
            if waiting:
                waiting.pop()()
            waiting.append(functools.partial(drain, u))

    both_ways = ((3, 0, 1), (1, 1, -1))

    def from_p(h):
        for dp, half, sp in both_ways:
            await_piece(h, dp, 0, None)
            pass_on(h, dp, 0, half, sp, 0)
            for sq in (1, -1):
                pass_on(h, dp, 0, None, 0, sq)

    def from_p2(h):
        for half in range(2):
            await_piece(h, 2, 0, half)
        for sq in (1, -1):
            pass_on(h, 2, 0, None, 0, sq)

    def from_q(h, dp):
        for dq, half, sq in both_ways:
            await_piece(h, dp, dq, None)
            pass_on(h, dp, dq, half, 0, sq)

    def from_q2(h, dp):
        for half in range(2):
            await_piece(h, dp, 2, half)

    loads[11].wait()
    loads[12].wait()
    scale(0)
    from_p(0)
    from_p(1)
    scale(1)
    from_q(0, 0)
    from_q(1, 0)
    loads[2].wait()
    unit_image(0, 0, 0)
    unit_image(1, 0, 0)
    from_p2(0)
    from_p2(1)
    unit_image(0, 0, 1)
    from_q2(0, 0)
    from_q2(1, 0)
    unit_image(1, 0, 1)
    scale(2)
    from_q(0, 3)
    from_q(1, 3)
    scale(3)
    from_q(0, 1)
    from_q(1, 1)
    unit_image(0, 3, 0)
    unit_image(1, 3, 0)
    unit_image(0, 1, 0)
    unit_image(1, 1, 0)
    from_q(0, 2)
    from_q(1, 2)
    unit_image(0, 3, 1)
    unit_image(0, 1, 1)
    unit_image(1, 2, 0)
    for h in range(2):
        from_q2(h, 3)
        from_q2(h, 1)
    unit_image(0, 2, 0)
    unit_image(1, 3, 1)
    unit_image(1, 1, 1)
    from_q2(0, 2)
    from_q2(1, 2)
    unit_image(0, 2, 1)
    unit_image(1, 2, 1)
    waiting.pop()()

    def source(k, s):
        return lax.rem(src_ref[k, s], 32)

    def sigma_chunk(c):
        def issue(t, u):
            for t2 in range(4):
                for e in range(2):
                    s = CUTS[c] + 2 * t + e
                    rhs = jnp.concatenate([image[k, source(k, s)] for k in (2 * t2, 2 * t2 + 1)], axis=0)
                    lhs = jnp.concatenate([scaled[2 * t2, s], scaled[2 * t2 + 1, s]], axis=1)
                    pltpu.matmul_push_rhs(rhs, t2 % 2, e)
                    feed(e, 2 * (u % 2), lhs, t2 % 2)

        def drain(t, u):
            rows = pl.ds(pl.multiple_of(CUTS[c] * 8 + t * 16, 16), 16)
            for n in range(2):
                first, second = pltpu.matmul_pop(acc[0][2 * (u % 2) + n]), pltpu.matmul_pop(acc[1][2 * (u % 2) + n])
                for o in range(8):
                    two = jnp.concatenate([first[o * 8 : o * 8 + 8], second[o * 8 : o * 8 + 8]], axis=0).astype(BF16)
                    parts[0, 2 * n + o // 4, o % 4, rows, :] = two[:, :128]
                    parts[1, o % 4, 2 * n + o // 4, rows, :] = two[:, 128:]

        in_turns((CUTS[c + 1] - CUTS[c]) // 2, issue, drain, 2)

    steps = ((0, 1), (1, 3))

    def all_rows(c):
        return pl.ds(CUTS[c] * 8, (CUTS[c + 1] - CUTS[c]) * 8)

    def half_of(c, d):
        span = (CUTS[c + 1] - CUTS[c]) * 4
        return pl.ds(CUTS[c] * 8 + d * span, span)

    def small(c):
        return pl.ds(CUTS[c] * 4, (CUTS[c + 1] - CUTS[c]) * 4)

    def sum1(c):
        for h in range(2):
            p, q = coords[h]
            for d, step in steps:
                start(
                    parts.at[flows[h], turn(q, 2), :, half_of(c, d), :], hop1.at[h, d, :, small(c), :],
                    2, sum_sem.at[0, h, d, c], at(h, 0, step),
                )

    def sum2(c):
        for h in range(2):
            p, q = coords[h]
            for d, step in steps:
                arrived(hop1.at[h, d, :, small(c), :], sum_sem.at[0, h, d, c])
                near = step_of(q, step)
                old = parts[flows[h], near, :, half_of(c, d), :].astype(F32)
                parts[flows[h], near, :, half_of(c, d), :] = (old + hop1[h, d, :, small(c), :].astype(F32)).astype(BF16)
                start(
                    parts.at[flows[h], near, :, all_rows(c), :], hop2.at[h, d, :, all_rows(c), :],
                    3, sum_sem.at[1, h, d, c], at(h, 0, step),
                )

    def sum3(c):
        for h in range(2):
            p, q = coords[h]
            rows = all_rows(c)
            for d, step in steps:
                arrived(hop2.at[h, d, :, rows, :], sum_sem.at[1, h, d, c])
            total = parts[flows[h], q, :, rows, :].astype(F32)
            total = total + hop2[h, 0, :, rows, :].astype(F32) + hop2[h, 1, :, rows, :].astype(F32)
            kept[h, :, rows, :] = total.astype(BF16)
            for d, step in steps:
                start(
                    kept.at[h, turn(p, 2), half_of(c, d), :], hop3.at[h, d, small(c), :],
                    4, sum_sem.at[2, h, d, c], at(h, step, 0),
                )

    def sum4(c):
        for h in range(2):
            p, q = coords[h]
            for d, step in steps:
                arrived(hop3.at[h, d, small(c), :], sum_sem.at[2, h, d, c])
                near = step_of(p, step)
                old = kept[h, near, half_of(c, d), :].astype(F32)
                kept[h, near, half_of(c, d), :] = (old + hop3[h, d, small(c), :].astype(F32)).astype(BF16)
                start(
                    kept.at[h, near, all_rows(c), :], hop4.at[h, d, all_rows(c), :],
                    5, sum_sem.at[3, h, d, c], at(h, step, 0),
                )

    leaves = []

    def sum5(c):
        rows = all_rows(c)
        for h in range(2):
            p, q = coords[h]
            for d, step in steps:
                arrived(hop4.at[h, d, rows, :], sum_sem.at[3, h, d, c])
            total = kept[h, p, rows, :].astype(F32) + hop4[h, 0, rows, :].astype(F32) + hop4[h, 1, rows, :].astype(F32)
            sig_ref[rows, pl.ds(pl.multiple_of(flows[h] * 128, 128), 128)] = total * (128 ** -0.5)
        leaves.append(pltpu.make_async_copy(sig_ref.at[rows, :], sig_out.at[rows, :], leave_sem.at[c]))
        leaves[-1].start()

    def mix(ks, turning=False):
        none = jnp.zeros((128, 128), BF16)

        def issue(t, u):
            for j in range(2):
                rhs = jnp.concatenate([full[source(ks[j], 2 * t + n)] for n in range(2)], axis=0)
                pltpu.matmul_push_rhs(rhs, u % 2, j)
                for n in range(2):
                    one = left[ks[j], 2 * t + n]
                    lhs = jnp.concatenate([one, none] if n == 0 else [none, one], axis=1)
                    feed(j, 4 * (u % 2) + 2 * n, lhs, u % 2 if n == 0 else None)

        def drain(t, u):
            if turning:
                for n in range(2):
                    full_t[t, :, n * 128 : n * 128 + 128] = full[2 * t + n].T
            for j in range(2):
                for n in range(4):
                    zed[j, t, n * 64 : n * 64 + 64, :] = pltpu.matmul_pop(acc[j][4 * (u % 2) + n]).astype(BF16)

        in_turns(16, issue, drain, 4)

    def renorm(slot):
        @pl.loop(0, 2)
        def _(i):
            for e in range(8):
                for j in range(2):
                    pltpu.matmul_push_rhs(zed[j, 8 * i + e], e % 2, j)
                    feed(j, 0, full_t[8 * i + e], e % 2)

        for j in range(2):
            for n in range(4):
                block[slot + j, n * 64 : n * 64 + 64, :] = (pltpu.matmul_pop(acc[j][n]) * (4096 ** -0.5)).astype(BF16)

    def push(src, dst, kind, recv_sem, target):
        pltpu.make_async_remote_copy(
            src_ref=src, dst_ref=dst, send_sem=send_sem.at[kind], recv_sem=recv_sem,
            device_id=(op, target), device_id_type=MESH,
        ).start()

    def ship(slot, dy, target):
        push(block.at[slot], ren_ref.at[sec], 6, swap_sem.at[step_of(0, dy), core], target)

    def half_rows(d):
        return pl.ds(d * 128, 128)

    def ship_far():
        for j in range(2):
            for d, step in steps:
                push(block.at[j, half_rows(d)], relay.at[d, j], 6, relay_sem.at[d, j], step_of(y, step) * 2 + core)

    def relay_far():
        for j in range(2):
            for d, step in steps:
                arrived(relay.at[d, j], relay_sem.at[d, j])
                sender = step_of(y, 4 - step) * 2 + core
                push(relay.at[d, j], ren_ref.at[sender, half_rows(d)], 7, far_sem.at[d, core], step_of(y, step) * 2 + lax.rem(j + core, 2))

    def swapped(dy, sender_core):
        sender = turn(y, 4 - dy) * 2 + sender_core
        arrived(ren_ref.at[sender], swap_sem.at[dy, sender_core])

    far = [turn(y, 2) * 2 + lax.rem(j + core, 2) for j in range(2)]
    near = [[step_of(y, dy) * 2 + lax.rem(j + core, 2) for dy in (1, 3)] for j in range(2)]
    here = [2 * y + j for j in range(2)]

    sigma_chunk(0)
    sum1(0)
    mix(far, turning=True)
    renorm(0)
    ship_far()
    sum2(0)
    sigma_chunk(1)
    sum1(1)
    sigma_chunk(2)
    sum1(2)
    sum3(0)
    mix(near[0])
    relay_far()
    sum2(1)
    renorm(2)
    ship(2, 1, near[0][0])
    ship(3, 3, near[0][1])
    sum2(2)
    sum4(0)
    mix(near[1])
    renorm(4)
    ship(4, 1, near[1][0])
    ship(5, 3, near[1][1])
    sum3(1)
    sum5(0)
    mix(here)
    sum3(2)
    sum4(1)
    renorm(6)
    ship(7 - core, 0, 2 * y + 1 - core)
    own = pltpu.make_async_copy(block.at[6 + core], ren_ref.at[sec], own_sem)
    own.start()
    sum4(2)
    sum5(1)
    sum5(2)
    for dy in (1, 3):
        for c in range(2):
            swapped(dy, c)
    for c in range(2):
        for d in range(2):
            arrived(ren_ref.at[turn(y, 2) * 2 + c, half_rows(d)], far_sem.at[d, c])
    swapped(0, 1 - core)
    own.wait()
    for copy in leaves:
        copy.wait()
    all_sent = (got.at[0, pl.ds(0, 15)], got.at[1, pl.ds(0, 15)], hop1, hop2, hop3, hop4, block.at[pl.ds(0, 7)], relay)
    for kind, ref in enumerate(all_sent):
        pltpu.make_async_copy(ref, ref, send_sem.at[kind]).wait()


def with_totals(*refs):
    totals = [pltpu.ACC(unit)((64, 256), F32) for unit in range(2) for _ in range(8)]
    pl.run_scoped(functools.partial(kernel, *refs), *totals)


def finish(sig_ref, ren_ref, sigma_ref, renorm_ref, sig, sigma, narrow, wide, in_sem, out_sem):
    come = [pltpu.make_async_copy(ren_ref.at[i], narrow.at[i], in_sem.at[i]) for i in range(8)]
    come.append(pltpu.make_async_copy(sig_ref, sig, in_sem.at[8]))
    go = [pltpu.make_async_copy(wide.at[i], renorm_ref.at[i], out_sem.at[i]) for i in range(8)]
    go.append(pltpu.make_async_copy(sigma, sigma_ref, out_sem.at[8]))
    for copy in come:
        copy.start()
    for i in range(8):
        come[i].wait()
        wide[i] = narrow[i].astype(F32)
        go[i].start()
    come[8].wait()
    sigma[...] = sig[...].astype(BF16)
    go[8].start()
    for copy in go:
        copy.wait()


def body(psi, left_env, right_env, source, coupling):
    vm = pltpu.VMEM
    sig, ren = pl.pallas_call(
        with_totals,
        out_shape=(jax.ShapeDtypeStruct((256, 256), F32), jax.ShapeDtypeStruct((8, 256, 256), BF16)),
        in_specs=[pl.BlockSpec(memory_space=pl.ANY)] * 5,
        out_specs=(pl.BlockSpec(memory_space=pl.ANY), pl.BlockSpec(memory_space=pl.ANY)),
        scratch_shapes=[
            pltpu.SMEM((8, 32), jnp.int32),
            pltpu.SMEM((8, 32), jnp.int32),
            vm((256, 256), F32),
            vm((8, 32, 128, 128), BF16),
            vm((8, 32, 128, 128), BF16),
            vm((8, 256, 256), BF16),
            vm((2, 16, 128, 256), BF16),
            vm((32, 128, 256), BF16),
            vm((16, 256, 256), BF16),
            vm((8, 32, 128, 256), BF16),
            vm((2, 16, 256, 256), BF16),
            vm((2, 4, 4, 256, 128), BF16),
            vm((8, 256, 256), BF16),
            vm((2, 2, 4, 128, 128), BF16),
            vm((2, 2, 4, 256, 128), BF16),
            vm((2, 4, 256, 128), BF16),
            vm((2, 2, 128, 128), BF16),
            vm((2, 2, 256, 128), BF16),
            vm((2, 2, 128, 256), BF16),
            pltpu.SemaphoreType.DMA((13,)),
            pltpu.SemaphoreType.DMA((8,)),
            pltpu.SemaphoreType.DMA((2, 16, 2)),
            pltpu.SemaphoreType.DMA((4, 2, 2, CHUNKS)),
            pltpu.SemaphoreType.DMA((4, 2)),
            pltpu.SemaphoreType.DMA((2, 2)),
            pltpu.SemaphoreType.DMA((2, 2)),
            pltpu.SemaphoreType.DMA,
            pltpu.SemaphoreType.DMA((CHUNKS,)),
        ],
        compiler_params=pltpu.CompilerParams(
            collective_id=0, has_side_effects=True, vmem_limit_bytes=60 * 1024 * 1024
        ),
        cost_estimate=pl.CostEstimate(flops=13 * 10**9, bytes_accessed=12 * 2**20, transcendentals=0),
        name="dmrg_step",
    )(psi.reshape(256, 256), left_env, right_env.reshape(8, 256, 256), source, coupling)
    sigma, renorm = pl.pallas_call(
        finish,
        out_shape=(jax.ShapeDtypeStruct((256, 256), BF16), jax.ShapeDtypeStruct((8, 256, 256), F32)),
        in_specs=[pl.BlockSpec(memory_space=pl.ANY)] * 2,
        out_specs=(pl.BlockSpec(memory_space=pl.ANY), pl.BlockSpec(memory_space=pl.ANY)),
        scratch_shapes=[
            vm((256, 256), F32),
            vm((256, 256), BF16),
            vm((8, 256, 256), BF16),
            vm((8, 256, 256), F32),
            pltpu.SemaphoreType.DMA((9,)),
            pltpu.SemaphoreType.DMA((9,)),
        ],
        compiler_params=pltpu.CompilerParams(vmem_limit_bytes=60 * 1024 * 1024),
        name="finish",
    )(sig, ren)
    return sigma.reshape(32, 8, 256), renorm[None]


def solution(mesh):
    placed = (
        P("sec", "op", None),
        P("op", "sec", None, None),
        P("op", "sec", None, None),
        P("op", "sec"),
        P("op", "sec"),
    )
    return jax.shard_map(
        body,
        mesh=mesh,
        in_specs=placed,
        out_specs=(P("sec", "op", None), P(("op", "sec"), None, None, None)),
        check_vma=False,
    )
```

```python
import functools

import jax
import jax.numpy as jnp
from jax import lax
from jax.experimental import pallas as pl
from jax.experimental.pallas import tpu as pltpu
from jax.sharding import PartitionSpec as P

COEFS = (1.0, -0.5773503, 0.8164966, -0.7071068)
MESH = pl.DeviceIdType.MESH
F32 = jnp.float32
BF16 = jnp.bfloat16
CUTS = (0, 8, 20, 32)
CHUNKS = len(CUTS) - 1


def turn(a, step):
    return lax.rem(a + step, 4)


def kernel(
    psi_ref, left_ref, right_ref, src_hbm, cpl_hbm,
    sig_out, ren_ref,
    src_ref, cpl_ref, sig_ref, left, scaled, right, got, full, full_t, image, zed, parts, block,
    hop1, hop2, kept, hop3, hop4,
    load_sem, send_sem, gather_sem, sum_sem, swap_sem, own_sem, leave_sem,
    *totals,
):
    acc = (totals[:8], totals[8:])
    op, sec = lax.axis_index("op"), lax.axis_index("sec")
    z, x = op // 4, op % 4
    y, core = sec // 2, sec % 2
    coords = ((x, z), (z, x))

    barrier = pltpu.get_barrier_semaphore()
    peers = [(z * 4 + turn(x, 1), sec), (z * 4 + turn(x, 3), sec), (turn(z, 1) * 4 + x, sec), (turn(z, 3) * 4 + x, sec)]
    peers += [(op, lax.rem(sec + i, 8)) for i in range(1, 8)]
    for peer in peers:
        pl.semaphore_signal(barrier, inc=1, device_id=peer, device_id_type=MESH)
    loads = [
        pltpu.make_async_copy(psi_ref.at[pl.ds(h * 128, 128)], got.at[h, op], load_sem.at[h]) for h in range(2)
    ]
    loads.append(pltpu.make_async_copy(right_ref, right, load_sem.at[2]))
    loads += [pltpu.make_async_copy(left_ref.at[k], left.at[k], load_sem.at[3 + k]) for k in range(8)]
    loads.append(pltpu.make_async_copy(cpl_hbm, cpl_ref, load_sem.at[11]))
    loads.append(pltpu.make_async_copy(src_hbm, src_ref, load_sem.at[12]))
    for copy in loads[:2] + loads[11:] + loads[2:11]:
        copy.start()
    pl.semaphore_wait(barrier, len(peers))

    def place(h, p, q):
        return q * 4 + p if h == 0 else p * 4 + q

    def at(h, dp, dq):
        p, q = coords[h]
        return place(h, turn(p, dp), turn(q, dq))

    def start(src, dst, kind, recv_sem, target):
        pltpu.make_async_remote_copy(
            src_ref=src, dst_ref=dst, send_sem=send_sem.at[kind], recv_sem=recv_sem,
            device_id=(target, sec), device_id_type=MESH,
        ).start()

    def arrived(dst, recv_sem):
        pltpu.make_async_remote_copy(
            src_ref=dst, dst_ref=dst, send_sem=send_sem.at[0], recv_sem=recv_sem,
            device_id=(op, sec), device_id_type=MESH,
        ).wait_recv()

    def piece(h, dp, dq, half):
        ref = got.at[h, at(h, dp, dq)]
        return ref if half is None else ref.at[pl.ds(half * 64, 64)]

    def pass_on(h, dp, dq, half, sp, sq):
        ref = piece(h, dp, dq, half)
        rel = (dp - sp) % 4 * 4 + (dq - sq) % 4
        start(ref, ref, h, gather_sem.at[h, rel, 0 if half is None else half], at(h, sp % 4, sq % 4))

    def await_piece(h, dp, dq, half):
        arrived(piece(h, dp, dq, half), gather_sem.at[h, dp * 4 + dq, 0 if half is None else half])

    for h in range(2):
        loads[h].wait()
        for sp in (1, -1):
            pass_on(h, 0, 0, None, sp, 0)
    for h in range(2):
        for sq in (1, -1):
            pass_on(h, 0, 0, None, 0, sq)

    def scale(part):
        for k in (2 * part, 2 * part + 1):
            loads[3 + k].wait()

        @pl.loop(2 * part, 2 * part + 2)
        def _(k):
            @pl.loop(0, 32, unroll=8)
            def _(s):
                level = cpl_ref[k, s]
                coef = jnp.where(
                    level == 0, COEFS[0], jnp.where(level == 1, COEFS[1], jnp.where(level == 2, COEFS[2], COEFS[3]))
                )
                scaled[k, s] = (left[k, s].astype(F32) * coef).astype(BF16)

    def feed(unit, base, lhs, reg):
        for n in range(lhs.shape[0] // 64):
            pltpu.matmul_acc_lhs(acc[unit][base + n], lhs[n * 64 : n * 64 + 64], reg if n == 0 else None)

    def in_turns(steps, issue, drain, unroll):
        issue(0, 0)

        @pl.loop(0, steps // unroll - 1)
        def _(i):
            for u in range(unroll):
                issue(i * unroll + u + 1, (u + 1) % unroll)
                drain(i * unroll + u, u)

        for u in range(unroll):
            t = steps - unroll + u
            if u + 1 < unroll:
                issue(t + 1, u + 1)
            drain(t, u)

    waiting = []

    def unit_image(h, dz, other):
        j = x // 2
        if other:
            j = 1 - j
        zz = turn(z, dz)
        o, to = zz * 4 + 2 * j, pl.ds(pl.multiple_of(zz * 32 + j * 16, 16), 16)

        def put(ref, first, second, at_sector):
            for s in range(8):
                two = jnp.concatenate([first[s * 8 : s * 8 + 8], second[s * 8 : s * 8 + 8]], axis=0)
                ref[h * 16 + at_sector + s, to, :] = two.astype(BF16)

        def drain(u):
            if u == 0:
                put(full, got[h, o, :64].astype(F32), got[h, o + 1, :64].astype(F32), 0)
                put(full, got[h, o, 64:].astype(F32), got[h, o + 1, 64:].astype(F32), 8)
            for unit in range(2):
                mine = acc[unit][4 * (u % 2) : 4 * (u % 2) + 4]
                for n in range(2):
                    put(image.at[2 * u + unit], pltpu.matmul_pop(mine[n]), pltpu.matmul_pop(mine[2 + n]), 8 * n)

        for u in range(4):
            for unit in range(2):
                pltpu.matmul_push_rhs(right[2 * u + unit], u % 2, unit)
                for n in range(2):
                    feed(unit, 4 * (u % 2) + 2 * n, got[h, o + n], u % 2 if n == 0 else None)
            if waiting:
                waiting.pop()()
            waiting.append(functools.partial(drain, u))

    both_ways = ((3, 0, 1), (1, 1, -1))

    def from_p(h):
        for dp, half, sp in both_ways:
            await_piece(h, dp, 0, None)
            pass_on(h, dp, 0, half, sp, 0)
            for sq in (1, -1):
                pass_on(h, dp, 0, None, 0, sq)

    def from_p2(h):
        for half in range(2):
            await_piece(h, 2, 0, half)
        for sq in (1, -1):
            pass_on(h, 2, 0, None, 0, sq)

    def from_q(h, dp):
        for dq, half, sq in both_ways:
            await_piece(h, dp, dq, None)
            pass_on(h, dp, dq, half, 0, sq)

    def from_q2(h, dp):
        for half in range(2):
            await_piece(h, dp, 2, half)

    loads[11].wait()
    loads[12].wait()
    scale(0)
    from_p(0)
    from_p(1)
    scale(1)
    from_q(0, 0)
    from_q(1, 0)
    loads[2].wait()
    unit_image(0, 0, 0)
    unit_image(1, 0, 0)
    from_p2(0)
    from_p2(1)
    unit_image(0, 0, 1)
    from_q2(0, 0)
    from_q2(1, 0)
    unit_image(1, 0, 1)
    scale(2)
    from_q(0, 3)
    from_q(1, 3)
    scale(3)
    from_q(0, 1)
    from_q(1, 1)
    unit_image(0, 3, 0)
    unit_image(1, 3, 0)
    unit_image(0, 1, 0)
    unit_image(1, 1, 0)
    from_q(0, 2)
    from_q(1, 2)
    unit_image(0, 3, 1)
    unit_image(0, 1, 1)
    unit_image(1, 2, 0)
    from_q2(0, 3)
    from_q2(0, 1)
    unit_image(0, 2, 0)
    from_q2(1, 3)
    unit_image(1, 3, 1)
    from_q2(1, 1)
    unit_image(1, 1, 1)
    from_q2(0, 2)
    unit_image(0, 2, 1)
    from_q2(1, 2)
    unit_image(1, 2, 1)
    waiting.pop()()

    def source(k, s):
        return lax.rem(src_ref[k, s], 32)

    def sigma_chunk(c):
        def issue(t, u):
            for t2 in range(4):
                for e in range(2):
                    s = CUTS[c] + 2 * t + e
                    rhs = jnp.concatenate([image[k, source(k, s)] for k in (2 * t2, 2 * t2 + 1)], axis=0)
                    lhs = jnp.concatenate([scaled[2 * t2, s], scaled[2 * t2 + 1, s]], axis=1)
                    pltpu.matmul_push_rhs(rhs, t2 % 2, e)
                    feed(e, 2 * (u % 2), lhs, t2 % 2)

        def drain(t, u):
            rows = pl.ds(pl.multiple_of(CUTS[c] * 8 + t * 16, 16), 16)
            for n in range(2):
                first, second = pltpu.matmul_pop(acc[0][2 * (u % 2) + n]), pltpu.matmul_pop(acc[1][2 * (u % 2) + n])
                for o in range(8):
                    two = jnp.concatenate([first[o * 8 : o * 8 + 8], second[o * 8 : o * 8 + 8]], axis=0).astype(BF16)
                    parts[0, 2 * n + o // 4, o % 4, rows, :] = two[:, :128]
                    parts[1, o % 4, 2 * n + o // 4, rows, :] = two[:, 128:]

        in_turns((CUTS[c + 1] - CUTS[c]) // 2, issue, drain, 2)

    steps = ((0, 1), (1, 3))

    def all_rows(c):
        return pl.ds(CUTS[c] * 8, (CUTS[c + 1] - CUTS[c]) * 8)

    def half_of(c, d):
        span = (CUTS[c + 1] - CUTS[c]) * 4
        return pl.ds(CUTS[c] * 8 + d * span, span)

    def small(c):
        return pl.ds(CUTS[c] * 4, (CUTS[c + 1] - CUTS[c]) * 4)

    def sum1(c):
        for h in range(2):
            p, q = coords[h]
            for d, step in steps:
                start(
                    parts.at[h, turn(q, 2), :, half_of(c, d), :], hop1.at[h, d, :, small(c), :],
                    2, sum_sem.at[0, h, d, c], at(h, 0, step),
                )

    def sum2(c):
        for h in range(2):
            p, q = coords[h]
            for d, step in steps:
                arrived(hop1.at[h, d, :, small(c), :], sum_sem.at[0, h, d, c])
                near = turn(q, step)
                old = parts[h, near, :, half_of(c, d), :].astype(F32)
                parts[h, near, :, half_of(c, d), :] = (old + hop1[h, d, :, small(c), :].astype(F32)).astype(BF16)
                start(
                    parts.at[h, near, :, all_rows(c), :], hop2.at[h, d, :, all_rows(c), :],
                    3, sum_sem.at[1, h, d, c], at(h, 0, step),
                )

    def sum3(c):
        for h in range(2):
            p, q = coords[h]
            rows = all_rows(c)
            for d, step in steps:
                arrived(hop2.at[h, d, :, rows, :], sum_sem.at[1, h, d, c])
            total = parts[h, q, :, rows, :].astype(F32)
            total = total + hop2[h, 0, :, rows, :].astype(F32) + hop2[h, 1, :, rows, :].astype(F32)
            kept[h, :, rows, :] = total.astype(BF16)
            for d, step in steps:
                start(
                    kept.at[h, turn(p, 2), half_of(c, d), :], hop3.at[h, d, small(c), :],
                    4, sum_sem.at[2, h, d, c], at(h, step, 0),
                )

    def sum4(c):
        for h in range(2):
            p, q = coords[h]
            for d, step in steps:
                arrived(hop3.at[h, d, small(c), :], sum_sem.at[2, h, d, c])
                near = turn(p, step)
                old = kept[h, near, half_of(c, d), :].astype(F32)
                kept[h, near, half_of(c, d), :] = (old + hop3[h, d, small(c), :].astype(F32)).astype(BF16)
                start(
                    kept.at[h, near, all_rows(c), :], hop4.at[h, d, all_rows(c), :],
                    5, sum_sem.at[3, h, d, c], at(h, step, 0),
                )

    leaves = []

    def sum5(c):
        rows = all_rows(c)
        for h in range(2):
            p, q = coords[h]
            for d, step in steps:
                arrived(hop4.at[h, d, rows, :], sum_sem.at[3, h, d, c])
            total = kept[h, p, rows, :].astype(F32) + hop4[h, 0, rows, :].astype(F32) + hop4[h, 1, rows, :].astype(F32)
            sig_ref[rows, pl.ds(h * 128, 128)] = total * (128 ** -0.5)
        leaves.append(pltpu.make_async_copy(sig_ref.at[rows, :], sig_out.at[rows, :], leave_sem.at[c]))
        leaves[-1].start()

    def mix(ks, turning=False):
        none = jnp.zeros((128, 128), BF16)

        def issue(t, u):
            for j in range(2):
                rhs = jnp.concatenate([full[source(ks[j], 2 * t + n)] for n in range(2)], axis=0)
                pltpu.matmul_push_rhs(rhs, u % 2, j)
                for n in range(2):
                    one = left[ks[j], 2 * t + n]
                    lhs = jnp.concatenate([one, none] if n == 0 else [none, one], axis=1)
                    feed(j, 4 * (u % 2) + 2 * n, lhs, u % 2 if n == 0 else None)

        def drain(t, u):
            if turning:
                for n in range(2):
                    full_t[t, :, n * 128 : n * 128 + 128] = full[2 * t + n].T
            for j in range(2):
                for n in range(4):
                    zed[j, t, n * 64 : n * 64 + 64, :] = pltpu.matmul_pop(acc[j][4 * (u % 2) + n]).astype(BF16)

        in_turns(16, issue, drain, 4)

    def renorm(slot):
        @pl.loop(0, 2)
        def _(i):
            for e in range(8):
                for j in range(2):
                    pltpu.matmul_push_rhs(zed[j, 8 * i + e], e % 2, j)
                    feed(j, 0, full_t[8 * i + e], e % 2)

        for j in range(2):
            for n in range(4):
                block[slot + j, n * 64 : n * 64 + 64, :] = (pltpu.matmul_pop(acc[j][n]) * (4096 ** -0.5)).astype(BF16)

    def push(src, dst, kind, recv_sem, target):
        pltpu.make_async_remote_copy(
            src_ref=src, dst_ref=dst, send_sem=send_sem.at[kind], recv_sem=recv_sem,
            device_id=(op, target), device_id_type=MESH,
        ).start()

    def ship(slot, dy, target):
        push(block.at[slot], ren_ref.at[sec], 6, swap_sem.at[dy, core], target)

    def swapped(dy, sender_core):
        sender = turn(y, 4 - dy) * 2 + sender_core
        arrived(ren_ref.at[sender], swap_sem.at[dy, sender_core])

    far = [turn(y, 2) * 2 + j for j in range(2)]
    near = [[turn(y, dy) * 2 + j for dy in (1, 3)] for j in range(2)]
    here = [2 * y + j for j in range(2)]

    sigma_chunk(0)
    sum1(0)
    sigma_chunk(1)
    sum1(1)
    mix(far, turning=True)
    sum2(0)
    renorm(0)
    sum2(1)
    ship(0, 2, far[0])
    ship(1, 2, far[1])
    sigma_chunk(2)
    sum1(2)
    sum3(0)
    mix(near[0])
    sum3(1)
    renorm(2)
    sum2(2)
    sum4(0)
    ship(2, 1, near[0][0])
    ship(3, 3, near[0][1])
    mix(near[1])
    sum4(1)
    renorm(4)
    sum3(2)
    sum5(0)
    ship(4, 1, near[1][0])
    ship(5, 3, near[1][1])
    mix(here)
    sum4(2)
    sum5(1)
    renorm(6)
    ship(7 - core, 0, 2 * y + 1 - core)
    own = pltpu.make_async_copy(block.at[6 + core], ren_ref.at[sec], own_sem)
    own.start()
    sum5(2)
    for dy in (2, 1, 3):
        for c in range(2):
            swapped(dy, c)
    swapped(0, 1 - core)
    own.wait()
    for copy in leaves:
        copy.wait()
    all_sent = (got.at[0, pl.ds(0, 15)], got.at[1, pl.ds(0, 15)], hop1, hop2, hop3, hop4, block.at[pl.ds(0, 7)])
    for kind, ref in enumerate(all_sent):
        pltpu.make_async_copy(ref, ref, send_sem.at[kind]).wait()


def with_totals(*refs):
    totals = [pltpu.ACC(unit)((64, 256), F32) for unit in range(2) for _ in range(8)]
    pl.run_scoped(functools.partial(kernel, *refs), *totals)


def finish(sig_ref, ren_ref, sigma_ref, renorm_ref, sig, sigma, narrow, wide, in_sem, out_sem):
    come = [pltpu.make_async_copy(ren_ref.at[i], narrow.at[i], in_sem.at[i]) for i in range(8)]
    come.append(pltpu.make_async_copy(sig_ref, sig, in_sem.at[8]))
    go = [pltpu.make_async_copy(wide.at[i], renorm_ref.at[i], out_sem.at[i]) for i in range(8)]
    go.append(pltpu.make_async_copy(sigma, sigma_ref, out_sem.at[8]))
    for copy in come:
        copy.start()
    for i in range(8):
        come[i].wait()
        wide[i] = narrow[i].astype(F32)
        go[i].start()
    come[8].wait()
    sigma[...] = sig[...].astype(BF16)
    go[8].start()
    for copy in go:
        copy.wait()


def body(psi, left_env, right_env, source, coupling):
    vm = pltpu.VMEM
    sig, ren = pl.pallas_call(
        with_totals,
        out_shape=(jax.ShapeDtypeStruct((256, 256), F32), jax.ShapeDtypeStruct((8, 256, 256), BF16)),
        in_specs=[pl.BlockSpec(memory_space=pl.ANY)] * 5,
        out_specs=(pl.BlockSpec(memory_space=pl.ANY), pl.BlockSpec(memory_space=pl.ANY)),
        scratch_shapes=[
            pltpu.SMEM((8, 32), jnp.int32),
            pltpu.SMEM((8, 32), jnp.int32),
            vm((256, 256), F32),
            vm((8, 32, 128, 128), BF16),
            vm((8, 32, 128, 128), BF16),
            vm((8, 256, 256), BF16),
            vm((2, 16, 128, 256), BF16),
            vm((32, 128, 256), BF16),
            vm((16, 256, 256), BF16),
            vm((8, 32, 128, 256), BF16),
            vm((2, 16, 256, 256), BF16),
            vm((2, 4, 4, 256, 128), BF16),
            vm((8, 256, 256), BF16),
            vm((2, 2, 4, 128, 128), BF16),
            vm((2, 2, 4, 256, 128), BF16),
            vm((2, 4, 256, 128), BF16),
            vm((2, 2, 128, 128), BF16),
            vm((2, 2, 256, 128), BF16),
            pltpu.SemaphoreType.DMA((13,)),
            pltpu.SemaphoreType.DMA((7,)),
            pltpu.SemaphoreType.DMA((2, 16, 2)),
            pltpu.SemaphoreType.DMA((4, 2, 2, CHUNKS)),
            pltpu.SemaphoreType.DMA((4, 2)),
            pltpu.SemaphoreType.DMA,
            pltpu.SemaphoreType.DMA((CHUNKS,)),
        ],
        compiler_params=pltpu.CompilerParams(
            collective_id=0, has_side_effects=True, vmem_limit_bytes=60 * 1024 * 1024
        ),
        cost_estimate=pl.CostEstimate(flops=13 * 10**9, bytes_accessed=12 * 2**20, transcendentals=0),
        name="dmrg_step",
    )(psi.reshape(256, 256), left_env, right_env.reshape(8, 256, 256), source, coupling)
    sigma, renorm = pl.pallas_call(
        finish,
        out_shape=(jax.ShapeDtypeStruct((256, 256), BF16), jax.ShapeDtypeStruct((8, 256, 256), F32)),
        in_specs=[pl.BlockSpec(memory_space=pl.ANY)] * 2,
        out_specs=(pl.BlockSpec(memory_space=pl.ANY), pl.BlockSpec(memory_space=pl.ANY)),
        scratch_shapes=[
            vm((256, 256), F32),
            vm((256, 256), BF16),
            vm((8, 256, 256), BF16),
            vm((8, 256, 256), F32),
            pltpu.SemaphoreType.DMA((9,)),
            pltpu.SemaphoreType.DMA((9,)),
        ],
        compiler_params=pltpu.CompilerParams(vmem_limit_bytes=60 * 1024 * 1024),
        name="finish",
    )(sig, ren)
    return sigma.reshape(32, 8, 256), renorm[None]


def solution(mesh):
    placed = (
        P("sec", "op", None),
        P("op", "sec", None, None),
        P("op", "sec", None, None),
        P("op", "sec"),
        P("op", "sec"),
    )
    return jax.shard_map(
        body,
        mesh=mesh,
        in_specs=placed,
        out_specs=(P("sec", "op", None), P(("op", "sec"), None, None, None)),
        check_vma=False,
    )
```

```python
import functools

import jax
import jax.numpy as jnp
from jax import lax
from jax.experimental import pallas as pl
from jax.experimental.pallas import tpu as pltpu
from jax.sharding import PartitionSpec as P

COEFS = (1.0, -0.5773503, 0.8164966, -0.7071068)
MESH = pl.DeviceIdType.MESH
F32 = jnp.float32
BF16 = jnp.bfloat16
CUTS = (0, 8, 20, 32)
CHUNKS = len(CUTS) - 1


def turn(a, step):
    return lax.rem(a + step, 4)


def kernel(
    psi_ref, left_ref, right_ref, src_hbm, cpl_hbm,
    sig_out, ren_ref,
    src_ref, cpl_ref, sig_ref, left, scaled, right, got, full, full_t, image, zed, parts, block,
    hop1, hop2, kept, hop3,
    load_sem, send_sem, gather_sem, sum_sem, swap_sem, own_sem, leave_sem,
    *totals,
):
    acc = (totals[:8], totals[8:])
    op, sec = lax.axis_index("op"), lax.axis_index("sec")
    z, x = op // 4, op % 4
    y, core = sec // 2, sec % 2
    coords = ((x, z), (z, x))

    barrier = pltpu.get_barrier_semaphore()
    peers = [(z * 4 + turn(x, 1), sec), (z * 4 + turn(x, 3), sec), (turn(z, 1) * 4 + x, sec), (turn(z, 3) * 4 + x, sec)]
    peers += [(z * 4 + turn(x, 2), sec), (turn(z, 2) * 4 + x, sec)]
    peers += [(op, lax.rem(sec + i, 8)) for i in range(1, 8)]
    for peer in peers:
        pl.semaphore_signal(barrier, inc=1, device_id=peer, device_id_type=MESH)
    loads = [
        pltpu.make_async_copy(psi_ref.at[pl.ds(h * 128, 128)], got.at[h, op], load_sem.at[h]) for h in range(2)
    ]
    loads.append(pltpu.make_async_copy(right_ref, right, load_sem.at[2]))
    loads += [pltpu.make_async_copy(left_ref.at[k], left.at[k], load_sem.at[3 + k]) for k in range(8)]
    loads.append(pltpu.make_async_copy(cpl_hbm, cpl_ref, load_sem.at[11]))
    loads.append(pltpu.make_async_copy(src_hbm, src_ref, load_sem.at[12]))
    for copy in loads[:2] + loads[11:] + loads[2:11]:
        copy.start()
    pl.semaphore_wait(barrier, len(peers))

    def place(h, p, q):
        return q * 4 + p if h == 0 else p * 4 + q

    def at(h, dp, dq):
        p, q = coords[h]
        return place(h, turn(p, dp), turn(q, dq))

    def start(src, dst, kind, recv_sem, target):
        pltpu.make_async_remote_copy(
            src_ref=src, dst_ref=dst, send_sem=send_sem.at[kind], recv_sem=recv_sem,
            device_id=(target, sec), device_id_type=MESH,
        ).start()

    def arrived(dst, recv_sem):
        pltpu.make_async_remote_copy(
            src_ref=dst, dst_ref=dst, send_sem=send_sem.at[0], recv_sem=recv_sem,
            device_id=(op, sec), device_id_type=MESH,
        ).wait_recv()

    def piece(h, dp, dq, half):
        ref = got.at[h, at(h, dp, dq)]
        return ref if half is None else ref.at[pl.ds(half * 64, 64)]

    def pass_on(h, dp, dq, half, sp, sq):
        ref = piece(h, dp, dq, half)
        rel = (dp - sp) % 4 * 4 + (dq - sq) % 4
        start(ref, ref, h, gather_sem.at[h, rel, 0 if half is None else half], at(h, sp % 4, sq % 4))

    def await_piece(h, dp, dq, half):
        arrived(piece(h, dp, dq, half), gather_sem.at[h, dp * 4 + dq, 0 if half is None else half])

    for h in range(2):
        loads[h].wait()
        for sp in (1, -1, 2):
            pass_on(h, 0, 0, None, sp, 0)
    for h in range(2):
        for sq in (1, -1):
            pass_on(h, 0, 0, None, 0, sq)

    def scale(part):
        for k in (2 * part, 2 * part + 1):
            loads[3 + k].wait()

        @pl.loop(2 * part, 2 * part + 2)
        def _(k):
            @pl.loop(0, 32, unroll=8)
            def _(s):
                level = cpl_ref[k, s]
                coef = jnp.where(
                    level == 0, COEFS[0], jnp.where(level == 1, COEFS[1], jnp.where(level == 2, COEFS[2], COEFS[3]))
                )
                scaled[k, s] = (left[k, s].astype(F32) * coef).astype(BF16)

    def feed(unit, base, lhs, reg):
        for n in range(lhs.shape[0] // 64):
            pltpu.matmul_acc_lhs(acc[unit][base + n], lhs[n * 64 : n * 64 + 64], reg if n == 0 else None)

    def in_turns(steps, issue, drain, unroll):
        issue(0, 0)

        @pl.loop(0, steps // unroll - 1)
        def _(i):
            for u in range(unroll):
                issue(i * unroll + u + 1, (u + 1) % unroll)
                drain(i * unroll + u, u)

        for u in range(unroll):
            t = steps - unroll + u
            if u + 1 < unroll:
                issue(t + 1, u + 1)
            drain(t, u)

    waiting = []

    def unit_image(h, dz, other):
        j = x // 2
        if other:
            j = 1 - j
        zz = turn(z, dz)
        o, to = zz * 4 + 2 * j, pl.ds(pl.multiple_of(zz * 32 + j * 16, 16), 16)

        def put(ref, first, second, at_sector):
            for s in range(8):
                two = jnp.concatenate([first[s * 8 : s * 8 + 8], second[s * 8 : s * 8 + 8]], axis=0)
                ref[h * 16 + at_sector + s, to, :] = two.astype(BF16)

        def drain(u):
            if u == 0:
                put(full, got[h, o, :64].astype(F32), got[h, o + 1, :64].astype(F32), 0)
                put(full, got[h, o, 64:].astype(F32), got[h, o + 1, 64:].astype(F32), 8)
            for unit in range(2):
                mine = acc[unit][4 * (u % 2) : 4 * (u % 2) + 4]
                for n in range(2):
                    put(image.at[2 * u + unit], pltpu.matmul_pop(mine[n]), pltpu.matmul_pop(mine[2 + n]), 8 * n)

        for u in range(4):
            for unit in range(2):
                pltpu.matmul_push_rhs(right[2 * u + unit], u % 2, unit)
                for n in range(2):
                    feed(unit, 4 * (u % 2) + 2 * n, got[h, o + n], u % 2 if n == 0 else None)
            if waiting:
                waiting.pop()()
            waiting.append(functools.partial(drain, u))

    both_ways = ((3, 0, 1), (1, 1, -1))

    def from_p(h):
        for dp in (3, 1, 2):
            await_piece(h, dp, 0, None)
            for sq in (1, -1):
                pass_on(h, dp, 0, None, 0, sq)

    def from_q(h, dp):
        for dq, half, sq in both_ways:
            await_piece(h, dp, dq, None)
            pass_on(h, dp, dq, half, 0, sq)

    def from_q2(h, dp):
        for half in range(2):
            await_piece(h, dp, 2, half)

    loads[11].wait()
    loads[12].wait()
    scale(0)
    from_p(0)
    from_p(1)
    scale(1)
    from_q(0, 0)
    from_q(1, 0)
    loads[2].wait()
    unit_image(0, 0, 0)
    unit_image(0, 0, 1)
    unit_image(1, 0, 0)
    scale(2)
    from_q2(0, 0)
    from_q2(1, 0)
    unit_image(1, 0, 1)
    from_q(0, 3)
    from_q(1, 3)
    scale(3)
    from_q(0, 1)
    from_q(1, 1)
    unit_image(0, 3, 0)
    unit_image(1, 3, 0)
    from_q(0, 2)
    from_q(1, 2)
    unit_image(0, 1, 0)
    unit_image(1, 1, 0)
    unit_image(0, 3, 1)
    unit_image(0, 1, 1)
    unit_image(1, 2, 0)
    from_q2(0, 3)
    from_q2(0, 1)
    unit_image(0, 2, 0)
    from_q2(1, 3)
    unit_image(1, 3, 1)
    from_q2(1, 1)
    unit_image(1, 1, 1)
    from_q2(0, 2)
    unit_image(0, 2, 1)
    from_q2(1, 2)
    unit_image(1, 2, 1)
    waiting.pop()()

    def source(k, s):
        return lax.rem(src_ref[k, s], 32)

    def sigma_chunk(c):
        def issue(t, u):
            for t2 in range(4):
                for e in range(2):
                    s = CUTS[c] + 2 * t + e
                    rhs = jnp.concatenate([image[k, source(k, s)] for k in (2 * t2, 2 * t2 + 1)], axis=0)
                    lhs = jnp.concatenate([scaled[2 * t2, s], scaled[2 * t2 + 1, s]], axis=1)
                    pltpu.matmul_push_rhs(rhs, t2 % 2, e)
                    feed(e, 2 * (u % 2), lhs, t2 % 2)

        def drain(t, u):
            rows = pl.ds(pl.multiple_of(CUTS[c] * 8 + t * 16, 16), 16)
            for n in range(2):
                first, second = pltpu.matmul_pop(acc[0][2 * (u % 2) + n]), pltpu.matmul_pop(acc[1][2 * (u % 2) + n])
                for o in range(8):
                    two = jnp.concatenate([first[o * 8 : o * 8 + 8], second[o * 8 : o * 8 + 8]], axis=0).astype(BF16)
                    parts[0, 2 * n + o // 4, o % 4, rows, :] = two[:, :128]
                    parts[1, o % 4, 2 * n + o // 4, rows, :] = two[:, 128:]

        in_turns((CUTS[c + 1] - CUTS[c]) // 2, issue, drain, 2)

    steps = ((0, 1), (1, 3))

    def all_rows(c):
        return pl.ds(CUTS[c] * 8, (CUTS[c + 1] - CUTS[c]) * 8)

    def half_of(c, d):
        span = (CUTS[c + 1] - CUTS[c]) * 4
        return pl.ds(CUTS[c] * 8 + d * span, span)

    def small(c):
        return pl.ds(CUTS[c] * 4, (CUTS[c + 1] - CUTS[c]) * 4)

    def sum1(c):
        for h in range(2):
            p, q = coords[h]
            for d, step in steps:
                start(
                    parts.at[h, turn(q, 2), :, half_of(c, d), :], hop1.at[h, d, :, small(c), :],
                    2, sum_sem.at[0, h, d, c], at(h, 0, step),
                )

    def sum2(c):
        for h in range(2):
            p, q = coords[h]
            for d, step in steps:
                arrived(hop1.at[h, d, :, small(c), :], sum_sem.at[0, h, d, c])
                near = turn(q, step)
                old = parts[h, near, :, half_of(c, d), :].astype(F32)
                parts[h, near, :, half_of(c, d), :] = (old + hop1[h, d, :, small(c), :].astype(F32)).astype(BF16)
                start(
                    parts.at[h, near, :, all_rows(c), :], hop2.at[h, d, :, all_rows(c), :],
                    3, sum_sem.at[1, h, d, c], at(h, 0, step),
                )

    def sum3(c):
        for h in range(2):
            p, q = coords[h]
            rows = all_rows(c)
            for d, step in steps:
                arrived(hop2.at[h, d, :, rows, :], sum_sem.at[1, h, d, c])
            total = parts[h, q, :, rows, :].astype(F32)
            total = total + hop2[h, 0, :, rows, :].astype(F32) + hop2[h, 1, :, rows, :].astype(F32)
            kept[h, :, rows, :] = total.astype(BF16)
            for i, step in enumerate((1, 3, 2)):
                start(
                    kept.at[h, turn(p, step), rows, :], hop3.at[h, i, rows, :],
                    4, sum_sem.at[2, h, i, c], at(h, step, 0),
                )

    leaves = []

    def sum5(c):
        rows = all_rows(c)
        for h in range(2):
            p, q = coords[h]
            total = kept[h, p, rows, :].astype(F32)
            for i in range(3):
                arrived(hop3.at[h, i, rows, :], sum_sem.at[2, h, i, c])
                total = total + hop3[h, i, rows, :].astype(F32)
            sig_ref[rows, pl.ds(h * 128, 128)] = total * (128 ** -0.5)
        leaves.append(pltpu.make_async_copy(sig_ref.at[rows, :], sig_out.at[rows, :], leave_sem.at[c]))
        leaves[-1].start()

    def mix(ks, turning=False):
        none = jnp.zeros((128, 128), BF16)

        def issue(t, u):
            for j in range(2):
                rhs = jnp.concatenate([full[source(ks[j], 2 * t + n)] for n in range(2)], axis=0)
                pltpu.matmul_push_rhs(rhs, u % 2, j)
                for n in range(2):
                    one = left[ks[j], 2 * t + n]
                    lhs = jnp.concatenate([one, none] if n == 0 else [none, one], axis=1)
                    feed(j, 4 * (u % 2) + 2 * n, lhs, u % 2 if n == 0 else None)

        def drain(t, u):
            if turning:
                for n in range(2):
                    full_t[t, :, n * 128 : n * 128 + 128] = full[2 * t + n].T
            for j in range(2):
                for n in range(4):
                    zed[j, t, n * 64 : n * 64 + 64, :] = pltpu.matmul_pop(acc[j][4 * (u % 2) + n]).astype(BF16)

        in_turns(16, issue, drain, 4)

    def renorm(slot):
        @pl.loop(0, 2)
        def _(i):
            for e in range(8):
                for j in range(2):
                    pltpu.matmul_push_rhs(zed[j, 8 * i + e], e % 2, j)
                    feed(j, 0, full_t[8 * i + e], e % 2)

        for j in range(2):
            for n in range(4):
                block[slot + j, n * 64 : n * 64 + 64, :] = (pltpu.matmul_pop(acc[j][n]) * (4096 ** -0.5)).astype(BF16)

    def push(src, dst, kind, recv_sem, target):
        pltpu.make_async_remote_copy(
            src_ref=src, dst_ref=dst, send_sem=send_sem.at[kind], recv_sem=recv_sem,
            device_id=(op, target), device_id_type=MESH,
        ).start()

    def ship(slot, dy, target):
        push(block.at[slot], ren_ref.at[sec], 5, swap_sem.at[dy, core], target)

    def swapped(dy, sender_core):
        sender = turn(y, 4 - dy) * 2 + sender_core
        arrived(ren_ref.at[sender], swap_sem.at[dy, sender_core])

    far = [turn(y, 2) * 2 + j for j in range(2)]
    near = [[turn(y, dy) * 2 + j for dy in (1, 3)] for j in range(2)]
    here = [2 * y + j for j in range(2)]

    sigma_chunk(0)
    sum1(0)
    sigma_chunk(1)
    sum1(1)
    mix(far, turning=True)
    sum2(0)
    renorm(0)
    sum2(1)
    ship(0, 2, far[0])
    ship(1, 2, far[1])
    sigma_chunk(2)
    sum1(2)
    sum3(0)
    mix(near[0])
    sum3(1)
    renorm(2)
    sum2(2)
    ship(2, 1, near[0][0])
    ship(3, 3, near[0][1])
    mix(near[1])
    sum5(0)
    renorm(4)
    sum3(2)
    ship(4, 1, near[1][0])
    ship(5, 3, near[1][1])
    mix(here)
    sum5(1)
    renorm(6)
    ship(7 - core, 0, 2 * y + 1 - core)
    own = pltpu.make_async_copy(block.at[6 + core], ren_ref.at[sec], own_sem)
    own.start()
    sum5(2)
    for dy in (2, 1, 3):
        for c in range(2):
            swapped(dy, c)
    swapped(0, 1 - core)
    own.wait()
    for copy in leaves:
        copy.wait()
    all_sent = (got.at[0, pl.ds(0, 15)], got.at[1, pl.ds(0, 15)], hop1, hop2, hop3, block.at[pl.ds(0, 7)])
    for kind, ref in enumerate(all_sent):
        pltpu.make_async_copy(ref, ref, send_sem.at[kind]).wait()


def with_totals(*refs):
    totals = [pltpu.ACC(unit)((64, 256), F32) for unit in range(2) for _ in range(8)]
    pl.run_scoped(functools.partial(kernel, *refs), *totals)


def finish(sig_ref, ren_ref, sigma_ref, renorm_ref, sig, sigma, narrow, wide, in_sem, out_sem):
    come = [pltpu.make_async_copy(ren_ref.at[i], narrow.at[i], in_sem.at[i]) for i in range(8)]
    come.append(pltpu.make_async_copy(sig_ref, sig, in_sem.at[8]))
    go = [pltpu.make_async_copy(wide.at[i], renorm_ref.at[i], out_sem.at[i]) for i in range(8)]
    go.append(pltpu.make_async_copy(sigma, sigma_ref, out_sem.at[8]))
    for copy in come:
        copy.start()
    for i in range(8):
        come[i].wait()
        wide[i] = narrow[i].astype(F32)
        go[i].start()
    come[8].wait()
    sigma[...] = sig[...].astype(BF16)
    go[8].start()
    for copy in go:
        copy.wait()


def body(psi, left_env, right_env, source, coupling):
    vm = pltpu.VMEM
    sig, ren = pl.pallas_call(
        with_totals,
        out_shape=(jax.ShapeDtypeStruct((256, 256), F32), jax.ShapeDtypeStruct((8, 256, 256), BF16)),
        in_specs=[pl.BlockSpec(memory_space=pl.ANY)] * 5,
        out_specs=(pl.BlockSpec(memory_space=pl.ANY), pl.BlockSpec(memory_space=pl.ANY)),
        scratch_shapes=[
            pltpu.SMEM((8, 32), jnp.int32),
            pltpu.SMEM((8, 32), jnp.int32),
            vm((256, 256), F32),
            vm((8, 32, 128, 128), BF16),
            vm((8, 32, 128, 128), BF16),
            vm((8, 256, 256), BF16),
            vm((2, 16, 128, 256), BF16),
            vm((32, 128, 256), BF16),
            vm((16, 256, 256), BF16),
            vm((8, 32, 128, 256), BF16),
            vm((2, 16, 256, 256), BF16),
            vm((2, 4, 4, 256, 128), BF16),
            vm((8, 256, 256), BF16),
            vm((2, 2, 4, 128, 128), BF16),
            vm((2, 2, 4, 256, 128), BF16),
            vm((2, 4, 256, 128), BF16),
            vm((2, 3, 256, 128), BF16),
            pltpu.SemaphoreType.DMA((13,)),
            pltpu.SemaphoreType.DMA((6,)),
            pltpu.SemaphoreType.DMA((2, 16, 2)),
            pltpu.SemaphoreType.DMA((3, 2, 3, CHUNKS)),
            pltpu.SemaphoreType.DMA((4, 2)),
            pltpu.SemaphoreType.DMA,
            pltpu.SemaphoreType.DMA((CHUNKS,)),
        ],
        compiler_params=pltpu.CompilerParams(
            collective_id=0, has_side_effects=True, vmem_limit_bytes=60 * 1024 * 1024
        ),
        cost_estimate=pl.CostEstimate(flops=13 * 10**9, bytes_accessed=12 * 2**20, transcendentals=0),
        name="dmrg_step",
    )(psi.reshape(256, 256), left_env, right_env.reshape(8, 256, 256), source, coupling)
    sigma, renorm = pl.pallas_call(
        finish,
        out_shape=(jax.ShapeDtypeStruct((256, 256), BF16), jax.ShapeDtypeStruct((8, 256, 256), F32)),
        in_specs=[pl.BlockSpec(memory_space=pl.ANY)] * 2,
        out_specs=(pl.BlockSpec(memory_space=pl.ANY), pl.BlockSpec(memory_space=pl.ANY)),
        scratch_shapes=[
            vm((256, 256), F32),
            vm((256, 256), BF16),
            vm((8, 256, 256), BF16),
            vm((8, 256, 256), F32),
            pltpu.SemaphoreType.DMA((9,)),
            pltpu.SemaphoreType.DMA((9,)),
        ],
        compiler_params=pltpu.CompilerParams(vmem_limit_bytes=60 * 1024 * 1024),
        name="finish",
    )(sig, ren)
    return sigma.reshape(32, 8, 256), renorm[None]


def solution(mesh):
    placed = (
        P("sec", "op", None),
        P("op", "sec", None, None),
        P("op", "sec", None, None),
        P("op", "sec"),
        P("op", "sec"),
    )
    return jax.shard_map(
        body,
        mesh=mesh,
        in_specs=placed,
        out_specs=(P("sec", "op", None), P(("op", "sec"), None, None, None)),
        check_vma=False,
    )
```

```python
import functools

import jax
import jax.numpy as jnp
from jax import lax
from jax.experimental import pallas as pl
from jax.experimental.pallas import tpu as pltpu
from jax.sharding import PartitionSpec as P

COEFS = (1.0, -0.5773503, 0.8164966, -0.7071068)
MESH = pl.DeviceIdType.MESH
F32 = jnp.float32
BF16 = jnp.bfloat16
CUTS = (0, 8, 20, 32)
CHUNKS = len(CUTS) - 1


def turn(a, step):
    return lax.rem(a + step, 4)


def kernel(
    psi_ref, left_ref, right_ref, src_hbm, cpl_hbm,
    sig_out, ren_ref,
    src_ref, cpl_ref, sig_ref, left, scaled, right, got, full, full_t, image, zed, parts, block,
    hop1, hop2, kept, hop3,
    load_sem, send_sem, gather_sem, sum_sem, swap_sem, own_sem, leave_sem,
    *totals,
):
    acc = (totals[:8], totals[8:])
    op, sec = lax.axis_index("op"), lax.axis_index("sec")
    z, x = op // 4, op % 4
    y, core = sec // 2, sec % 2
    coords = ((x, z), (z, x))

    barrier = pltpu.get_barrier_semaphore()
    peers = [(z * 4 + turn(x, 1), sec), (z * 4 + turn(x, 3), sec), (turn(z, 1) * 4 + x, sec), (turn(z, 3) * 4 + x, sec)]
    peers += [(z * 4 + turn(x, 2), sec), (turn(z, 2) * 4 + x, sec)]
    peers += [(op, lax.rem(sec + i, 8)) for i in range(1, 8)]
    for peer in peers:
        pl.semaphore_signal(barrier, inc=1, device_id=peer, device_id_type=MESH)
    loads = [
        pltpu.make_async_copy(psi_ref.at[pl.ds(h * 128, 128)], got.at[h, op], load_sem.at[h]) for h in range(2)
    ]
    loads.append(pltpu.make_async_copy(right_ref, right, load_sem.at[2]))
    loads += [pltpu.make_async_copy(left_ref.at[k], left.at[k], load_sem.at[3 + k]) for k in range(8)]
    loads.append(pltpu.make_async_copy(cpl_hbm, cpl_ref, load_sem.at[11]))
    loads.append(pltpu.make_async_copy(src_hbm, src_ref, load_sem.at[12]))
    for copy in loads[:2] + loads[11:] + loads[2:11]:
        copy.start()
    pl.semaphore_wait(barrier, len(peers))

    def place(h, p, q):
        return q * 4 + p if h == 0 else p * 4 + q

    def at(h, dp, dq):
        p, q = coords[h]
        return place(h, turn(p, dp), turn(q, dq))

    def start(src, dst, kind, recv_sem, target):
        pltpu.make_async_remote_copy(
            src_ref=src, dst_ref=dst, send_sem=send_sem.at[kind], recv_sem=recv_sem,
            device_id=(target, sec), device_id_type=MESH,
        ).start()

    def arrived(dst, recv_sem):
        pltpu.make_async_remote_copy(
            src_ref=dst, dst_ref=dst, send_sem=send_sem.at[0], recv_sem=recv_sem,
            device_id=(op, sec), device_id_type=MESH,
        ).wait_recv()

    def piece(h, dp, dq, half):
        ref = got.at[h, at(h, dp, dq)]
        return ref if half is None else ref.at[pl.ds(half * 64, 64)]

    def pass_on(h, dp, dq, half, sp, sq):
        ref = piece(h, dp, dq, half)
        rel = (dp - sp) % 4 * 4 + (dq - sq) % 4
        start(ref, ref, h, gather_sem.at[h, rel, 0 if half is None else half], at(h, sp % 4, sq % 4))

    def await_piece(h, dp, dq, half):
        arrived(piece(h, dp, dq, half), gather_sem.at[h, dp * 4 + dq, 0 if half is None else half])

    for h in range(2):
        loads[h].wait()
        for sp in (1, -1, 2):
            pass_on(h, 0, 0, None, sp, 0)
    for h in range(2):
        for sq in (1, -1):
            pass_on(h, 0, 0, None, 0, sq)

    def scale(part):
        for k in (2 * part, 2 * part + 1):
            loads[3 + k].wait()

        @pl.loop(2 * part, 2 * part + 2)
        def _(k):
            @pl.loop(0, 32, unroll=4)
            def _(s):
                level = cpl_ref[k, s]
                coef = jnp.where(
                    level == 0, COEFS[0], jnp.where(level == 1, COEFS[1], jnp.where(level == 2, COEFS[2], COEFS[3]))
                )
                scaled[k, s] = (left[k, s].astype(F32) * coef).astype(BF16)

    def feed(unit, base, lhs, reg):
        for n in range(lhs.shape[0] // 64):
            pltpu.matmul_acc_lhs(acc[unit][base + n], lhs[n * 64 : n * 64 + 64], reg if n == 0 else None)

    def in_turns(steps, issue, drain, unroll):
        issue(0, 0)

        @pl.loop(0, steps // unroll - 1)
        def _(i):
            for u in range(unroll):
                issue(i * unroll + u + 1, (u + 1) % unroll)
                drain(i * unroll + u, u)

        for u in range(unroll):
            t = steps - unroll + u
            if u + 1 < unroll:
                issue(t + 1, u + 1)
            drain(t, u)

    def unit_image(h, dz, other):
        j = x // 2
        j = j + other * (1 - 2 * j)
        zz = lax.rem(z + dz, 4)
        o, to = zz * 4 + 2 * j, pl.ds(pl.multiple_of(zz * 32 + j * 16, 16), 16)

        def put(ref, first, second, at_sector):
            for s in range(8):
                two = jnp.concatenate([first[s * 8 : s * 8 + 8], second[s * 8 : s * 8 + 8]], axis=0)
                ref[h * 16 + at_sector + s, to, :] = two.astype(BF16)

        def issue(u):
            for unit in range(2):
                pltpu.matmul_push_rhs(right[2 * u + unit], u % 2, unit)
                for n in range(2):
                    feed(unit, 4 * (u % 2) + 2 * n, got[h, o + n], u % 2 if n == 0 else None)

        def drain(u):
            for unit in range(2):
                mine = acc[unit][4 * (u % 2) : 4 * (u % 2) + 4]
                for n in range(2):
                    put(image.at[2 * u + unit], pltpu.matmul_pop(mine[n]), pltpu.matmul_pop(mine[2 + n]), 8 * n)

        issue(0)
        put(full, got[h, o, :64].astype(F32), got[h, o + 1, :64].astype(F32), 0)
        put(full, got[h, o, 64:].astype(F32), got[h, o + 1, 64:].astype(F32), 8)
        for u in range(1, 4):
            issue(u)
            drain(u - 1)
        drain(3)

    def unit_images(count, which):
        @pl.loop(0, count)
        def _(i):
            unit_image(*which(i))

    both_ways = ((3, 0, 1), (1, 1, -1))

    def from_p(h):
        for dp in (3, 1, 2):
            await_piece(h, dp, 0, None)
            for sq in (1, -1):
                pass_on(h, dp, 0, None, 0, sq)

    def from_q(h, dp):
        for dq, half, sq in both_ways:
            await_piece(h, dp, dq, None)
            pass_on(h, dp, dq, half, 0, sq)

    def from_q2(h, dp):
        for half in range(2):
            await_piece(h, dp, 2, half)

    loads[11].wait()
    loads[12].wait()
    scale(0)
    from_p(0)
    from_p(1)
    scale(1)
    from_q(0, 0)
    from_q(1, 0)
    loads[2].wait()
    unit_images(3, lambda i: (i // 2, 0, lax.rem(i, 2)))
    scale(2)
    from_q2(0, 0)
    from_q2(1, 0)
    unit_images(1, lambda i: (1, 0, 1))
    from_q(0, 3)
    from_q(1, 3)
    scale(3)
    from_q(0, 1)
    from_q(1, 1)
    unit_images(2, lambda i: (i, 3, 0))
    from_q(0, 2)
    from_q(1, 2)
    unit_images(2, lambda i: (i, 1, 0))
    unit_images(3, lambda i: (i // 2, 3 + 2 * i + 3 * (i // 2), 1 - i // 2))
    for h in (1, 0):
        from_q2(h, 3)
        from_q2(h, 1)
    unit_images(3, lambda i: (1 - i // 2, 3 + 2 * i + 3 * (i // 2), 1 - i // 2))
    from_q2(0, 2)
    from_q2(1, 2)
    unit_images(2, lambda i: (i, 2, 1))

    def source(k, s):
        return lax.rem(src_ref[k, s], 32)

    def sigma_chunk(c):
        def issue(t, u):
            for t2 in range(4):
                for e in range(2):
                    s = CUTS[c] + 2 * t + e
                    rhs = jnp.concatenate([image[k, source(k, s)] for k in (2 * t2, 2 * t2 + 1)], axis=0)
                    lhs = jnp.concatenate([scaled[2 * t2, s], scaled[2 * t2 + 1, s]], axis=1)
                    pltpu.matmul_push_rhs(rhs, t2 % 2, e)
                    feed(e, 2 * (u % 2), lhs, t2 % 2)

        def drain(t, u):
            rows = pl.ds(pl.multiple_of(CUTS[c] * 8 + t * 16, 16), 16)
            for n in range(2):
                first, second = pltpu.matmul_pop(acc[0][2 * (u % 2) + n]), pltpu.matmul_pop(acc[1][2 * (u % 2) + n])
                for o in range(8):
                    two = jnp.concatenate([first[o * 8 : o * 8 + 8], second[o * 8 : o * 8 + 8]], axis=0).astype(BF16)
                    parts[0, 2 * n + o // 4, o % 4, rows, :] = two[:, :128]
                    parts[1, o % 4, 2 * n + o // 4, rows, :] = two[:, 128:]

        in_turns((CUTS[c + 1] - CUTS[c]) // 2, issue, drain, 2)

    steps = ((0, 1), (1, 3))

    def all_rows(c):
        return pl.ds(CUTS[c] * 8, (CUTS[c + 1] - CUTS[c]) * 8)

    def half_of(c, d):
        span = (CUTS[c + 1] - CUTS[c]) * 4
        return pl.ds(CUTS[c] * 8 + d * span, span)

    def small(c):
        return pl.ds(CUTS[c] * 4, (CUTS[c + 1] - CUTS[c]) * 4)

    def sum1(c):
        for h in range(2):
            p, q = coords[h]
            for d, step in steps:
                start(
                    parts.at[h, turn(q, 2), :, half_of(c, d), :], hop1.at[h, d, :, small(c), :],
                    2, sum_sem.at[0, h, d, c], at(h, 0, step),
                )

    def sum2(c):
        for h in range(2):
            p, q = coords[h]
            for d, step in steps:
                arrived(hop1.at[h, d, :, small(c), :], sum_sem.at[0, h, d, c])
                near = turn(q, step)
                old = parts[h, near, :, half_of(c, d), :].astype(F32)
                parts[h, near, :, half_of(c, d), :] = (old + hop1[h, d, :, small(c), :].astype(F32)).astype(BF16)
                start(
                    parts.at[h, near, :, all_rows(c), :], hop2.at[h, d, :, all_rows(c), :],
                    3, sum_sem.at[1, h, d, c], at(h, 0, step),
                )

    def sum3(c):
        for h in range(2):
            p, q = coords[h]
            rows = all_rows(c)
            for d, step in steps:
                arrived(hop2.at[h, d, :, rows, :], sum_sem.at[1, h, d, c])
            total = parts[h, q, :, rows, :].astype(F32)
            total = total + hop2[h, 0, :, rows, :].astype(F32) + hop2[h, 1, :, rows, :].astype(F32)
            kept[h, :, rows, :] = total.astype(BF16)
            for i, step in enumerate((1, 3, 2)):
                start(
                    kept.at[h, turn(p, step), rows, :], hop3.at[h, i, rows, :],
                    4, sum_sem.at[2, h, i, c], at(h, step, 0),
                )

    leaves = []

    def sum5(c):
        rows = all_rows(c)
        for h in range(2):
            p, q = coords[h]
            total = kept[h, p, rows, :].astype(F32)
            for i in range(3):
                arrived(hop3.at[h, i, rows, :], sum_sem.at[2, h, i, c])
                total = total + hop3[h, i, rows, :].astype(F32)
            sig_ref[rows, pl.ds(h * 128, 128)] = total * (128 ** -0.5)
        leaves.append(pltpu.make_async_copy(sig_ref.at[rows, :], sig_out.at[rows, :], leave_sem.at[c]))
        leaves[-1].start()

    def mix(ks, turning=False):
        none = jnp.zeros((128, 128), BF16)

        def issue(t, u):
            for j in range(2):
                rhs = jnp.concatenate([full[source(ks[j], 2 * t + n)] for n in range(2)], axis=0)
                pltpu.matmul_push_rhs(rhs, u % 2, j)
                for n in range(2):
                    one = left[ks[j], 2 * t + n]
                    lhs = jnp.concatenate([one, none] if n == 0 else [none, one], axis=1)
                    feed(j, 4 * (u % 2) + 2 * n, lhs, u % 2 if n == 0 else None)

        def drain(t, u):
            if turning:
                for n in range(2):
                    full_t[t, :, n * 128 : n * 128 + 128] = full[2 * t + n].T
            for j in range(2):
                for n in range(4):
                    zed[j, t, n * 64 : n * 64 + 64, :] = pltpu.matmul_pop(acc[j][4 * (u % 2) + n]).astype(BF16)

        in_turns(16, issue, drain, 2)

    def renorm(slot):
        @pl.loop(0, 4)
        def _(i):
            for e in range(4):
                for j in range(2):
                    pltpu.matmul_push_rhs(zed[j, 4 * i + e], e % 2, j)
                    feed(j, 0, full_t[4 * i + e], e % 2)

        for j in range(2):
            for n in range(4):
                block[slot + j, n * 64 : n * 64 + 64, :] = (pltpu.matmul_pop(acc[j][n]) * (4096 ** -0.5)).astype(BF16)

    def push(src, dst, kind, recv_sem, target):
        pltpu.make_async_remote_copy(
            src_ref=src, dst_ref=dst, send_sem=send_sem.at[kind], recv_sem=recv_sem,
            device_id=(op, target), device_id_type=MESH,
        ).start()

    def ship(slot, dy, target):
        push(block.at[slot], ren_ref.at[sec], 5, swap_sem.at[dy, core], target)

    def swapped(dy, sender_core):
        sender = turn(y, 4 - dy) * 2 + sender_core
        arrived(ren_ref.at[sender], swap_sem.at[dy, sender_core])

    far = [turn(y, 2) * 2 + j for j in range(2)]
    near = [[turn(y, dy) * 2 + j for dy in (1, 3)] for j in range(2)]
    here = [2 * y + j for j in range(2)]

    sigma_chunk(0)
    sum1(0)
    sigma_chunk(1)
    sum1(1)
    mix(far, turning=True)
    sum2(0)
    renorm(0)
    sum2(1)
    ship(0, 2, far[0])
    ship(1, 2, far[1])
    sigma_chunk(2)
    sum1(2)
    sum3(0)
    mix(near[0])
    sum3(1)
    renorm(2)
    sum2(2)
    ship(2, 1, near[0][0])
    ship(3, 3, near[0][1])
    mix(near[1])
    sum5(0)
    renorm(4)
    sum3(2)
    ship(4, 1, near[1][0])
    ship(5, 3, near[1][1])
    mix(here)
    sum5(1)
    renorm(6)
    ship(7 - core, 0, 2 * y + 1 - core)
    own = pltpu.make_async_copy(block.at[6 + core], ren_ref.at[sec], own_sem)
    own.start()
    sum5(2)
    for dy in (2, 1, 3):
        for c in range(2):
            swapped(dy, c)
    swapped(0, 1 - core)
    own.wait()
    for copy in leaves:
        copy.wait()
    all_sent = (got.at[0, pl.ds(0, 15)], got.at[1, pl.ds(0, 15)], hop1, hop2, hop3, block.at[pl.ds(0, 7)])
    for kind, ref in enumerate(all_sent):
        pltpu.make_async_copy(ref, ref, send_sem.at[kind]).wait()


def with_totals(*refs):
    totals = [pltpu.ACC(unit)((64, 256), F32) for unit in range(2) for _ in range(8)]
    pl.run_scoped(functools.partial(kernel, *refs), *totals)


def finish(sig_ref, ren_ref, sigma_ref, renorm_ref, sig, sigma, narrow, wide, in_sem, out_sem):
    come = [pltpu.make_async_copy(ren_ref.at[i], narrow.at[i], in_sem.at[i]) for i in range(8)]
    come.append(pltpu.make_async_copy(sig_ref, sig, in_sem.at[8]))
    go = [pltpu.make_async_copy(wide.at[i], renorm_ref.at[i], out_sem.at[i]) for i in range(8)]
    go.append(pltpu.make_async_copy(sigma, sigma_ref, out_sem.at[8]))
    for copy in come:
        copy.start()
    for i in range(8):
        come[i].wait()
        wide[i] = narrow[i].astype(F32)
        go[i].start()
    come[8].wait()
    sigma[...] = sig[...].astype(BF16)
    go[8].start()
    for copy in go:
        copy.wait()


def body(psi, left_env, right_env, source, coupling):
    vm = pltpu.VMEM
    sig, ren = pl.pallas_call(
        with_totals,
        out_shape=(jax.ShapeDtypeStruct((256, 256), F32), jax.ShapeDtypeStruct((8, 256, 256), BF16)),
        in_specs=[pl.BlockSpec(memory_space=pl.ANY)] * 5,
        out_specs=(pl.BlockSpec(memory_space=pl.ANY), pl.BlockSpec(memory_space=pl.ANY)),
        scratch_shapes=[
            pltpu.SMEM((8, 32), jnp.int32),
            pltpu.SMEM((8, 32), jnp.int32),
            vm((256, 256), F32),
            vm((8, 32, 128, 128), BF16),
            vm((8, 32, 128, 128), BF16),
            vm((8, 256, 256), BF16),
            vm((2, 16, 128, 256), BF16),
            vm((32, 128, 256), BF16),
            vm((16, 256, 256), BF16),
            vm((8, 32, 128, 256), BF16),
            vm((2, 16, 256, 256), BF16),
            vm((2, 4, 4, 256, 128), BF16),
            vm((8, 256, 256), BF16),
            vm((2, 2, 4, 128, 128), BF16),
            vm((2, 2, 4, 256, 128), BF16),
            vm((2, 4, 256, 128), BF16),
            vm((2, 3, 256, 128), BF16),
            pltpu.SemaphoreType.DMA((13,)),
            pltpu.SemaphoreType.DMA((6,)),
            pltpu.SemaphoreType.DMA((2, 16, 2)),
            pltpu.SemaphoreType.DMA((3, 2, 3, CHUNKS)),
            pltpu.SemaphoreType.DMA((4, 2)),
            pltpu.SemaphoreType.DMA,
            pltpu.SemaphoreType.DMA((CHUNKS,)),
        ],
        compiler_params=pltpu.CompilerParams(
            collective_id=0, has_side_effects=True, vmem_limit_bytes=60 * 1024 * 1024
        ),
        cost_estimate=pl.CostEstimate(flops=13 * 10**9, bytes_accessed=12 * 2**20, transcendentals=0),
        name="dmrg_step",
    )(psi.reshape(256, 256), left_env, right_env.reshape(8, 256, 256), source, coupling)
    sigma, renorm = pl.pallas_call(
        finish,
        out_shape=(jax.ShapeDtypeStruct((256, 256), BF16), jax.ShapeDtypeStruct((8, 256, 256), F32)),
        in_specs=[pl.BlockSpec(memory_space=pl.ANY)] * 2,
        out_specs=(pl.BlockSpec(memory_space=pl.ANY), pl.BlockSpec(memory_space=pl.ANY)),
        scratch_shapes=[
            vm((256, 256), F32),
            vm((256, 256), BF16),
            vm((8, 256, 256), BF16),
            vm((8, 256, 256), F32),
            pltpu.SemaphoreType.DMA((9,)),
            pltpu.SemaphoreType.DMA((9,)),
        ],
        compiler_params=pltpu.CompilerParams(vmem_limit_bytes=60 * 1024 * 1024),
        name="finish",
    )(sig, ren)
    return sigma.reshape(32, 8, 256), renorm[None]


def solution(mesh):
    placed = (
        P("sec", "op", None),
        P("op", "sec", None, None),
        P("op", "sec", None, None),
        P("op", "sec"),
        P("op", "sec"),
    )
    return jax.shard_map(
        body,
        mesh=mesh,
        in_specs=placed,
        out_specs=(P("sec", "op", None), P(("op", "sec"), None, None, None)),
        check_vma=False,
    )
```

```python
import functools

import jax
import jax.numpy as jnp
from jax import lax
from jax.experimental import pallas as pl
from jax.experimental.pallas import tpu as pltpu
from jax.sharding import PartitionSpec as P

COEFS = (1.0, -0.5773503, 0.8164966, -0.7071068)
MESH = pl.DeviceIdType.MESH
F32 = jnp.float32
BF16 = jnp.bfloat16
CUTS = (0, 8, 24, 32)
CHUNKS = len(CUTS) - 1


def turn(a, step):
    return lax.rem(a + step, 4)


def kernel(
    psi_ref, left_ref, right_ref, src_hbm, cpl_hbm,
    sig_out, ren_ref,
    src_ref, cpl_ref, sig_ref, left, scaled, right, got, full, full_t, image, zed, parts, block,
    hop1, hop2, kept, hop3,
    load_sem, send_sem, gather_sem, sum_sem, swap_sem, own_sem, leave_sem,
    *totals,
):
    acc = (totals[:8], totals[8:])
    op, sec = lax.axis_index("op"), lax.axis_index("sec")
    z, x = op // 4, op % 4
    y, core = sec // 2, sec % 2
    coords = ((x, z), (z, x))

    barrier = pltpu.get_barrier_semaphore()
    peers = [(z * 4 + turn(x, 1), sec), (z * 4 + turn(x, 3), sec), (turn(z, 1) * 4 + x, sec), (turn(z, 3) * 4 + x, sec)]
    peers += [(z * 4 + turn(x, 2), sec), (turn(z, 2) * 4 + x, sec)]
    peers += [(op, lax.rem(sec + i, 8)) for i in range(1, 8)]
    for peer in peers:
        pl.semaphore_signal(barrier, inc=1, device_id=peer, device_id_type=MESH)
    loads = [
        pltpu.make_async_copy(psi_ref.at[pl.ds(h * 128, 128)], got.at[h, op], load_sem.at[h]) for h in range(2)
    ]
    loads.append(pltpu.make_async_copy(right_ref, right, load_sem.at[2]))
    loads += [pltpu.make_async_copy(left_ref.at[k], left.at[k], load_sem.at[3 + k]) for k in range(8)]
    loads.append(pltpu.make_async_copy(cpl_hbm, cpl_ref, load_sem.at[11]))
    loads.append(pltpu.make_async_copy(src_hbm, src_ref, load_sem.at[12]))
    for copy in loads[:2] + loads[11:] + loads[2:11]:
        copy.start()
    pl.semaphore_wait(barrier, len(peers))

    def place(h, p, q):
        return q * 4 + p if h == 0 else p * 4 + q

    def at(h, dp, dq):
        p, q = coords[h]
        return place(h, turn(p, dp), turn(q, dq))

    def start(src, dst, kind, recv_sem, target):
        pltpu.make_async_remote_copy(
            src_ref=src, dst_ref=dst, send_sem=send_sem.at[kind], recv_sem=recv_sem,
            device_id=(target, sec), device_id_type=MESH,
        ).start()

    def arrived(dst, recv_sem):
        pltpu.make_async_remote_copy(
            src_ref=dst, dst_ref=dst, send_sem=send_sem.at[0], recv_sem=recv_sem,
            device_id=(op, sec), device_id_type=MESH,
        ).wait_recv()

    def piece(h, dp, dq, half):
        ref = got.at[h, at(h, dp, dq)]
        return ref if half is None else ref.at[pl.ds(half * 64, 64)]

    def pass_on(h, dp, dq, half, sp, sq):
        ref = piece(h, dp, dq, half)
        rel = (dp - sp) % 4 * 4 + (dq - sq) % 4
        start(ref, ref, h, gather_sem.at[h, rel, 0 if half is None else half], at(h, sp % 4, sq % 4))

    def await_piece(h, dp, dq, half):
        arrived(piece(h, dp, dq, half), gather_sem.at[h, dp * 4 + dq, 0 if half is None else half])

    for h in range(2):
        loads[h].wait()
        for sp in (1, -1, 2):
            pass_on(h, 0, 0, None, sp, 0)
    for h in range(2):
        for sq in (1, -1):
            pass_on(h, 0, 0, None, 0, sq)

    def scale(part):
        for k in (2 * part, 2 * part + 1):
            loads[3 + k].wait()

        @pl.loop(2 * part, 2 * part + 2)
        def _(k):
            @pl.loop(0, 32, unroll=8)
            def _(s):
                level = cpl_ref[k, s]
                coef = jnp.where(
                    level == 0, COEFS[0], jnp.where(level == 1, COEFS[1], jnp.where(level == 2, COEFS[2], COEFS[3]))
                )
                scaled[k, s] = (left[k, s].astype(F32) * coef).astype(BF16)

    def feed(unit, base, lhs, reg):
        for n in range(lhs.shape[0] // 64):
            pltpu.matmul_acc_lhs(acc[unit][base + n], lhs[n * 64 : n * 64 + 64], reg if n == 0 else None)

    def in_turns(steps, issue, drain, unroll):
        issue(0, 0)

        @pl.loop(0, steps // unroll - 1)
        def _(i):
            for u in range(unroll):
                issue(i * unroll + u + 1, (u + 1) % unroll)
                drain(i * unroll + u, u)

        for u in range(unroll):
            t = steps - unroll + u
            if u + 1 < unroll:
                issue(t + 1, u + 1)
            drain(t, u)

    waiting = []

    def unit_image(h, dz, other):
        j = x // 2
        if other:
            j = 1 - j
        zz = turn(z, dz)
        o, to = zz * 4 + 2 * j, pl.ds(pl.multiple_of(zz * 32 + j * 16, 16), 16)

        def put(ref, first, second, at_sector):
            for s in range(8):
                two = jnp.concatenate([first[s * 8 : s * 8 + 8], second[s * 8 : s * 8 + 8]], axis=0)
                ref[h * 16 + at_sector + s, to, :] = two.astype(BF16)

        def drain(u):
            if u == 0:
                put(full, got[h, o, :64].astype(F32), got[h, o + 1, :64].astype(F32), 0)
                put(full, got[h, o, 64:].astype(F32), got[h, o + 1, 64:].astype(F32), 8)
            for unit in range(2):
                mine = acc[unit][4 * (u % 2) : 4 * (u % 2) + 4]
                for n in range(2):
                    put(image.at[2 * u + unit], pltpu.matmul_pop(mine[n]), pltpu.matmul_pop(mine[2 + n]), 8 * n)

        for u in range(4):
            for unit in range(2):
                pltpu.matmul_push_rhs(right[2 * u + unit], u % 2, unit)
                for n in range(2):
                    feed(unit, 4 * (u % 2) + 2 * n, got[h, o + n], u % 2 if n == 0 else None)
            if waiting:
                waiting.pop()()
            waiting.append(functools.partial(drain, u))

    both_ways = ((3, 0, 1), (1, 1, -1))

    def from_p(h):
        for dp in (3, 1, 2):
            await_piece(h, dp, 0, None)
            for sq in (1, -1):
                pass_on(h, dp, 0, None, 0, sq)

    def from_q(h, dp):
        for dq, half, sq in both_ways:
            await_piece(h, dp, dq, None)
            pass_on(h, dp, dq, half, 0, sq)

    def from_q2(h, dp):
        for half in range(2):
            await_piece(h, dp, 2, half)

    loads[11].wait()
    loads[12].wait()
    scale(0)
    from_p(0)
    from_p(1)
    scale(1)
    from_q(0, 0)
    from_q(1, 0)
    loads[2].wait()
    unit_image(0, 0, 0)
    unit_image(0, 0, 1)
    unit_image(1, 0, 0)
    scale(2)
    from_q2(0, 0)
    from_q2(1, 0)
    unit_image(1, 0, 1)
    from_q(0, 3)
    from_q(1, 3)
    scale(3)
    from_q(0, 1)
    from_q(1, 1)
    unit_image(0, 3, 0)
    unit_image(1, 3, 0)
    from_q(0, 2)
    from_q(1, 2)
    unit_image(0, 1, 0)
    unit_image(1, 1, 0)
    unit_image(0, 3, 1)
    unit_image(0, 1, 1)
    unit_image(1, 2, 0)
    from_q2(0, 3)
    from_q2(0, 1)
    unit_image(0, 2, 0)
    from_q2(1, 3)
    unit_image(1, 3, 1)
    from_q2(1, 1)
    unit_image(1, 1, 1)
    from_q2(0, 2)
    unit_image(0, 2, 1)
    from_q2(1, 2)
    unit_image(1, 2, 1)
    waiting.pop()()

    def source(k, s):
        return lax.rem(src_ref[k, s], 32)

    def sigma_chunk(c):
        def issue(t, u):
            for t2 in range(4):
                for e in range(2):
                    s = CUTS[c] + 2 * t + e
                    rhs = jnp.concatenate([image[k, source(k, s)] for k in (2 * t2, 2 * t2 + 1)], axis=0)
                    lhs = jnp.concatenate([scaled[2 * t2, s], scaled[2 * t2 + 1, s]], axis=1)
                    pltpu.matmul_push_rhs(rhs, t2 % 2, e)
                    feed(e, 2 * (u % 2), lhs, t2 % 2)

        def drain(t, u):
            rows = pl.ds(pl.multiple_of(CUTS[c] * 8 + t * 16, 16), 16)
            if c < 2:
                turned = CUTS[c] // 2 + t
                for n in range(2):
                    full_t[turned, :, n * 128 : n * 128 + 128] = full[2 * turned + n].T
            for n in range(2):
                first, second = pltpu.matmul_pop(acc[0][2 * (u % 2) + n]), pltpu.matmul_pop(acc[1][2 * (u % 2) + n])
                for o in range(8):
                    two = jnp.concatenate([first[o * 8 : o * 8 + 8], second[o * 8 : o * 8 + 8]], axis=0).astype(BF16)
                    parts[0, 2 * n + o // 4, o % 4, rows, :] = two[:, :128]
                    parts[1, o % 4, 2 * n + o // 4, rows, :] = two[:, 128:]

        in_turns((CUTS[c + 1] - CUTS[c]) // 2, issue, drain, 2)

    steps = ((0, 1), (1, 3))

    def all_rows(c):
        return pl.ds(CUTS[c] * 8, (CUTS[c + 1] - CUTS[c]) * 8)

    def half_of(c, d):
        span = (CUTS[c + 1] - CUTS[c]) * 4
        return pl.ds(CUTS[c] * 8 + d * span, span)

    def small(c):
        return pl.ds(CUTS[c] * 4, (CUTS[c + 1] - CUTS[c]) * 4)

    def sum1(c):
        for h in range(2):
            p, q = coords[h]
            for d, step in steps:
                start(
                    parts.at[h, turn(q, 2), :, half_of(c, d), :], hop1.at[h, d, :, small(c), :],
                    2, sum_sem.at[0, h, d, c], at(h, 0, step),
                )

    def sum2(c):
        for h in range(2):
            p, q = coords[h]
            for d, step in steps:
                arrived(hop1.at[h, d, :, small(c), :], sum_sem.at[0, h, d, c])
                near = turn(q, step)
                old = parts[h, near, :, half_of(c, d), :].astype(F32)
                parts[h, near, :, half_of(c, d), :] = (old + hop1[h, d, :, small(c), :].astype(F32)).astype(BF16)
                start(
                    parts.at[h, near, :, all_rows(c), :], hop2.at[h, d, :, all_rows(c), :],
                    3, sum_sem.at[1, h, d, c], at(h, 0, step),
                )

    def sum3(c):
        for h in range(2):
            p, q = coords[h]
            rows = all_rows(c)
            for d, step in steps:
                arrived(hop2.at[h, d, :, rows, :], sum_sem.at[1, h, d, c])
            total = parts[h, q, :, rows, :].astype(F32)
            total = total + hop2[h, 0, :, rows, :].astype(F32) + hop2[h, 1, :, rows, :].astype(F32)
            kept[h, :, rows, :] = total.astype(BF16)
            for i, step in enumerate((1, 3, 2)):
                start(
                    kept.at[h, turn(p, step), rows, :], hop3.at[h, i, rows, :],
                    4, sum_sem.at[2, h, i, c], at(h, step, 0),
                )

    leaves = []

    def sum5(c):
        rows = all_rows(c)
        for h in range(2):
            p, q = coords[h]
            total = kept[h, p, rows, :].astype(F32)
            for i in range(3):
                arrived(hop3.at[h, i, rows, :], sum_sem.at[2, h, i, c])
                total = total + hop3[h, i, rows, :].astype(F32)
            sig_ref[rows, pl.ds(h * 128, 128)] = total * (128 ** -0.5)
        leaves.append(pltpu.make_async_copy(sig_ref.at[rows, :], sig_out.at[rows, :], leave_sem.at[c]))
        leaves[-1].start()

    def mix(ks, turning=False):
        none = jnp.zeros((128, 128), BF16)

        def issue(t, u):
            for j in range(2):
                rhs = jnp.concatenate([full[source(ks[j], 2 * t + n)] for n in range(2)], axis=0)
                pltpu.matmul_push_rhs(rhs, u % 2, j)
                for n in range(2):
                    one = left[ks[j], 2 * t + n]
                    lhs = jnp.concatenate([one, none] if n == 0 else [none, one], axis=1)
                    feed(j, 4 * (u % 2) + 2 * n, lhs, u % 2 if n == 0 else None)

        def drain(t, u):
            if turning:
                turned, n, m = CUTS[2] // 2 + t // 4, u % 2, u // 2
                full_t[turned, m * 128 : m * 128 + 128, n * 128 : n * 128 + 128] = full[
                    2 * turned + n, :, m * 128 : m * 128 + 128
                ].T
            for j in range(2):
                for n in range(4):
                    zed[j, t, n * 64 : n * 64 + 64, :] = pltpu.matmul_pop(acc[j][4 * (u % 2) + n]).astype(BF16)

        in_turns(16, issue, drain, 4)

    def renorm(slot):
        @pl.loop(0, 2)
        def _(i):
            for e in range(8):
                for j in range(2):
                    pltpu.matmul_push_rhs(zed[j, 8 * i + e], e % 2, j)
                    feed(j, 0, full_t[8 * i + e], e % 2)

        for j in range(2):
            for n in range(4):
                block[slot + j, n * 64 : n * 64 + 64, :] = (pltpu.matmul_pop(acc[j][n]) * (4096 ** -0.5)).astype(BF16)

    def push(src, dst, kind, recv_sem, target):
        pltpu.make_async_remote_copy(
            src_ref=src, dst_ref=dst, send_sem=send_sem.at[kind], recv_sem=recv_sem,
            device_id=(op, target), device_id_type=MESH,
        ).start()

    def ship(slot, dy, target):
        push(block.at[slot], ren_ref.at[sec], 5, swap_sem.at[dy, core], target)

    def swapped(dy, sender_core):
        sender = turn(y, 4 - dy) * 2 + sender_core
        arrived(ren_ref.at[sender], swap_sem.at[dy, sender_core])

    far = [turn(y, 2) * 2 + j for j in range(2)]
    near = [[turn(y, dy) * 2 + j for dy in (1, 3)] for j in range(2)]
    here = [2 * y + j for j in range(2)]

    sigma_chunk(0)
    sum1(0)
    sigma_chunk(1)
    sum1(1)
    mix(far, turning=True)
    sum2(0)
    renorm(0)
    ship(0, 2, far[0])
    ship(1, 2, far[1])
    sigma_chunk(2)
    sum1(2)
    sum2(1)
    mix(near[0])
    sum3(0)
    renorm(2)
    ship(2, 1, near[0][0])
    ship(3, 3, near[0][1])
    sum2(2)
    mix(near[1])
    renorm(4)
    ship(4, 1, near[1][0])
    ship(5, 3, near[1][1])
    sum3(1)
    mix(here)
    sum3(2)
    sum5(0)
    renorm(6)
    ship(7 - core, 0, 2 * y + 1 - core)
    own = pltpu.make_async_copy(block.at[6 + core], ren_ref.at[sec], own_sem)
    own.start()
    sum5(1)
    sum5(2)
    for dy in (2, 1, 3):
        for c in range(2):
            swapped(dy, c)
    swapped(0, 1 - core)
    own.wait()
    for copy in leaves:
        copy.wait()
    all_sent = (got.at[0, pl.ds(0, 15)], got.at[1, pl.ds(0, 15)], hop1, hop2, hop3, block.at[pl.ds(0, 7)])
    for kind, ref in enumerate(all_sent):
        pltpu.make_async_copy(ref, ref, send_sem.at[kind]).wait()


def with_totals(*refs):
    totals = [pltpu.ACC(unit)((64, 256), F32) for unit in range(2) for _ in range(8)]
    pl.run_scoped(functools.partial(kernel, *refs), *totals)


def finish(sig_ref, ren_ref, sigma_ref, renorm_ref, sig, sigma, narrow, wide, in_sem, out_sem):
    come = [pltpu.make_async_copy(ren_ref.at[i], narrow.at[i], in_sem.at[i]) for i in range(8)]
    come.append(pltpu.make_async_copy(sig_ref, sig, in_sem.at[8]))
    go = [pltpu.make_async_copy(wide.at[i], renorm_ref.at[i], out_sem.at[i]) for i in range(8)]
    go.append(pltpu.make_async_copy(sigma, sigma_ref, out_sem.at[8]))
    for copy in come:
        copy.start()
    for i in range(8):
        come[i].wait()
        wide[i] = narrow[i].astype(F32)
        go[i].start()
    come[8].wait()
    sigma[...] = sig[...].astype(BF16)
    go[8].start()
    for copy in go:
        copy.wait()


def body(psi, left_env, right_env, source, coupling):
    vm = pltpu.VMEM
    sig, ren = pl.pallas_call(
        with_totals,
        out_shape=(jax.ShapeDtypeStruct((256, 256), F32), jax.ShapeDtypeStruct((8, 256, 256), BF16)),
        in_specs=[pl.BlockSpec(memory_space=pl.ANY)] * 5,
        out_specs=(pl.BlockSpec(memory_space=pl.ANY), pl.BlockSpec(memory_space=pl.ANY)),
        scratch_shapes=[
            pltpu.SMEM((8, 32), jnp.int32),
            pltpu.SMEM((8, 32), jnp.int32),
            vm((256, 256), F32),
            vm((8, 32, 128, 128), BF16),
            vm((8, 32, 128, 128), BF16),
            vm((8, 256, 256), BF16),
            vm((2, 16, 128, 256), BF16),
            vm((32, 128, 256), BF16),
            vm((16, 256, 256), BF16),
            vm((8, 32, 128, 256), BF16),
            vm((2, 16, 256, 256), BF16),
            vm((2, 4, 4, 256, 128), BF16),
            vm((8, 256, 256), BF16),
            vm((2, 2, 4, 128, 128), BF16),
            vm((2, 2, 4, 256, 128), BF16),
            vm((2, 4, 256, 128), BF16),
            vm((2, 3, 256, 128), BF16),
            pltpu.SemaphoreType.DMA((13,)),
            pltpu.SemaphoreType.DMA((6,)),
            pltpu.SemaphoreType.DMA((2, 16, 2)),
            pltpu.SemaphoreType.DMA((3, 2, 3, CHUNKS)),
            pltpu.SemaphoreType.DMA((4, 2)),
            pltpu.SemaphoreType.DMA,
            pltpu.SemaphoreType.DMA((CHUNKS,)),
        ],
        compiler_params=pltpu.CompilerParams(
            collective_id=0, has_side_effects=True, vmem_limit_bytes=60 * 1024 * 1024
        ),
        cost_estimate=pl.CostEstimate(flops=13 * 10**9, bytes_accessed=12 * 2**20, transcendentals=0),
        name="dmrg_step",
    )(psi.reshape(256, 256), left_env, right_env.reshape(8, 256, 256), source, coupling)
    sigma, renorm = pl.pallas_call(
        finish,
        out_shape=(jax.ShapeDtypeStruct((256, 256), BF16), jax.ShapeDtypeStruct((8, 256, 256), F32)),
        in_specs=[pl.BlockSpec(memory_space=pl.ANY)] * 2,
        out_specs=(pl.BlockSpec(memory_space=pl.ANY), pl.BlockSpec(memory_space=pl.ANY)),
        scratch_shapes=[
            vm((256, 256), F32),
            vm((256, 256), BF16),
            vm((8, 256, 256), BF16),
            vm((8, 256, 256), F32),
            pltpu.SemaphoreType.DMA((9,)),
            pltpu.SemaphoreType.DMA((9,)),
        ],
        compiler_params=pltpu.CompilerParams(vmem_limit_bytes=60 * 1024 * 1024),
        name="finish",
    )(sig, ren)
    return sigma.reshape(32, 8, 256), renorm[None]


def solution(mesh):
    placed = (
        P("sec", "op", None),
        P("op", "sec", None, None),
        P("op", "sec", None, None),
        P("op", "sec"),
        P("op", "sec"),
    )
    return jax.shard_map(
        body,
        mesh=mesh,
        in_specs=placed,
        out_specs=(P("sec", "op", None), P(("op", "sec"), None, None, None)),
        check_vma=False,
    )
```

```python
import functools

import jax
import jax.numpy as jnp
from jax import lax
from jax.experimental import pallas as pl
from jax.experimental.pallas import tpu as pltpu
from jax.sharding import PartitionSpec as P

COEFS = (1.0, -0.5773503, 0.8164966, -0.7071068)
MESH = pl.DeviceIdType.MESH
F32 = jnp.float32
BF16 = jnp.bfloat16
CUTS = (0, 8, 24, 32)
CHUNKS = len(CUTS) - 1


def turn(a, step):
    return lax.rem(a + step, 4)


def kernel(
    psi_ref, left_ref, right_ref, src_hbm, cpl_hbm,
    sig_out, ren_ref,
    src_ref, cpl_ref, sig_ref, left, scaled, right, got, full, full_t, image, zed, parts, block,
    hop1, hop2, kept, hop3,
    load_sem, send_sem, gather_sem, sum_sem, swap_sem, own_sem, leave_sem,
    *totals,
):
    acc = (totals[:8], totals[8:])
    op, sec = lax.axis_index("op"), lax.axis_index("sec")
    z, x = op // 4, op % 4
    y, core = sec // 2, sec % 2
    coords = ((x, z), (z, x))

    barrier = pltpu.get_barrier_semaphore()
    peers = [(z * 4 + turn(x, 1), sec), (z * 4 + turn(x, 3), sec), (turn(z, 1) * 4 + x, sec), (turn(z, 3) * 4 + x, sec)]
    peers += [(z * 4 + turn(x, 2), sec), (turn(z, 2) * 4 + x, sec)]
    peers += [(op, lax.rem(sec + i, 8)) for i in range(1, 8)]
    for peer in peers:
        pl.semaphore_signal(barrier, inc=1, device_id=peer, device_id_type=MESH)
    loads = [
        pltpu.make_async_copy(psi_ref.at[pl.ds(h * 128, 128)], got.at[h, op], load_sem.at[h]) for h in range(2)
    ]
    loads.append(pltpu.make_async_copy(right_ref, right, load_sem.at[2]))
    loads += [pltpu.make_async_copy(left_ref.at[k], left.at[k], load_sem.at[3 + k]) for k in range(8)]
    loads.append(pltpu.make_async_copy(cpl_hbm, cpl_ref, load_sem.at[11]))
    loads.append(pltpu.make_async_copy(src_hbm, src_ref, load_sem.at[12]))
    for copy in loads[:2] + loads[11:] + loads[2:11]:
        copy.start()
    pl.semaphore_wait(barrier, len(peers))

    def place(h, p, q):
        return q * 4 + p if h == 0 else p * 4 + q

    def at(h, dp, dq):
        p, q = coords[h]
        return place(h, turn(p, dp), turn(q, dq))

    def start(src, dst, kind, recv_sem, target):
        pltpu.make_async_remote_copy(
            src_ref=src, dst_ref=dst, send_sem=send_sem.at[kind], recv_sem=recv_sem,
            device_id=(target, sec), device_id_type=MESH,
        ).start()

    def arrived(dst, recv_sem):
        pltpu.make_async_remote_copy(
            src_ref=dst, dst_ref=dst, send_sem=send_sem.at[0], recv_sem=recv_sem,
            device_id=(op, sec), device_id_type=MESH,
        ).wait_recv()

    def piece(h, dp, dq, half):
        ref = got.at[h, at(h, dp, dq)]
        return ref if half is None else ref.at[pl.ds(half * 64, 64)]

    def pass_on(h, dp, dq, half, sp, sq):
        ref = piece(h, dp, dq, half)
        rel = (dp - sp) % 4 * 4 + (dq - sq) % 4
        start(ref, ref, h, gather_sem.at[h, rel, 0 if half is None else half], at(h, sp % 4, sq % 4))

    def await_piece(h, dp, dq, half):
        arrived(piece(h, dp, dq, half), gather_sem.at[h, dp * 4 + dq, 0 if half is None else half])

    for h in range(2):
        loads[h].wait()
        for sp in (1, -1, 2):
            pass_on(h, 0, 0, None, sp, 0)
    for h in range(2):
        for sq in (1, -1):
            pass_on(h, 0, 0, None, 0, sq)

    def scale(part):
        for k in (2 * part, 2 * part + 1):
            loads[3 + k].wait()

        @pl.loop(2 * part, 2 * part + 2)
        def _(k):
            @pl.loop(0, 32, unroll=8)
            def _(s):
                level = cpl_ref[k, s]
                coef = jnp.where(
                    level == 0, COEFS[0], jnp.where(level == 1, COEFS[1], jnp.where(level == 2, COEFS[2], COEFS[3]))
                )
                scaled[k, s] = (left[k, s].astype(F32) * coef).astype(BF16)

    def feed(unit, base, lhs, reg):
        for n in range(lhs.shape[0] // 64):
            pltpu.matmul_acc_lhs(acc[unit][base + n], lhs[n * 64 : n * 64 + 64], reg if n == 0 else None)

    def in_turns(steps, issue, drain, unroll):
        issue(0, 0)

        @pl.loop(0, steps // unroll - 1)
        def _(i):
            for u in range(unroll):
                issue(i * unroll + u + 1, (u + 1) % unroll)
                drain(i * unroll + u, u)

        for u in range(unroll):
            t = steps - unroll + u
            if u + 1 < unroll:
                issue(t + 1, u + 1)
            drain(t, u)

    waiting = []

    def unit_image(h, dz, other):
        j = x // 2
        if other:
            j = 1 - j
        zz = turn(z, dz)
        o, to = zz * 4 + 2 * j, pl.ds(pl.multiple_of(zz * 32 + j * 16, 16), 16)

        def put(ref, first, second, at_sector):
            for s in range(8):
                two = jnp.concatenate([first[s * 8 : s * 8 + 8], second[s * 8 : s * 8 + 8]], axis=0)
                ref[h * 16 + at_sector + s, to, :] = two.astype(BF16)

        def drain(u):
            if u == 0:
                put(full, got[h, o, :64].astype(F32), got[h, o + 1, :64].astype(F32), 0)
                put(full, got[h, o, 64:].astype(F32), got[h, o + 1, 64:].astype(F32), 8)
            for unit in range(2):
                mine = acc[unit][4 * (u % 2) : 4 * (u % 2) + 4]
                for n in range(2):
                    put(image.at[2 * u + unit], pltpu.matmul_pop(mine[n]), pltpu.matmul_pop(mine[2 + n]), 8 * n)

        for u in range(4):
            for unit in range(2):
                pltpu.matmul_push_rhs(right[2 * u + unit], u % 2, unit)
                for n in range(2):
                    feed(unit, 4 * (u % 2) + 2 * n, got[h, o + n], u % 2 if n == 0 else None)
            if waiting:
                waiting.pop()()
            waiting.append(functools.partial(drain, u))

    both_ways = ((3, 0, 1), (1, 1, -1))

    def from_p(h):
        for dp in (3, 1, 2):
            await_piece(h, dp, 0, None)
            for sq in (1, -1):
                pass_on(h, dp, 0, None, 0, sq)

    def from_q(h, dp):
        for dq, half, sq in both_ways:
            await_piece(h, dp, dq, None)
            pass_on(h, dp, dq, half, 0, sq)

    def from_q2(h, dp):
        for half in range(2):
            await_piece(h, dp, 2, half)

    loads[11].wait()
    loads[12].wait()
    scale(0)
    from_p(0)
    from_p(1)
    scale(1)
    from_q(0, 0)
    from_q(1, 0)
    loads[2].wait()
    unit_image(0, 0, 0)
    unit_image(0, 0, 1)
    unit_image(1, 0, 0)
    scale(2)
    from_q2(0, 0)
    from_q2(1, 0)
    unit_image(1, 0, 1)
    from_q(0, 3)
    from_q(1, 3)
    scale(3)
    from_q(0, 1)
    from_q(1, 1)
    unit_image(0, 3, 0)
    unit_image(1, 3, 0)
    from_q(0, 2)
    from_q(1, 2)
    unit_image(0, 1, 0)
    unit_image(1, 1, 0)
    unit_image(0, 3, 1)
    unit_image(0, 1, 1)
    unit_image(1, 2, 0)
    from_q2(0, 3)
    from_q2(0, 1)
    unit_image(0, 2, 0)
    from_q2(1, 3)
    unit_image(1, 3, 1)
    from_q2(1, 1)
    unit_image(1, 1, 1)
    from_q2(0, 2)
    unit_image(0, 2, 1)
    from_q2(1, 2)
    unit_image(1, 2, 1)
    waiting.pop()()

    def source(k, s):
        return lax.rem(src_ref[k, s], 32)

    def sigma_chunk(c):
        def issue(t, u):
            for t2 in range(4):
                for e in range(2):
                    s = CUTS[c] + 2 * t + e
                    rhs = jnp.concatenate([image[k, source(k, s)] for k in (2 * t2, 2 * t2 + 1)], axis=0)
                    lhs = jnp.concatenate([scaled[2 * t2, s], scaled[2 * t2 + 1, s]], axis=1)
                    pltpu.matmul_push_rhs(rhs, t2 % 2, e)
                    feed(e, 2 * (u % 2), lhs, t2 % 2)

        def drain(t, u):
            rows = pl.ds(pl.multiple_of(CUTS[c] * 8 + t * 16, 16), 16)
            if c < 2:
                turned = CUTS[c] // 2 + t
                for n in range(2):
                    full_t[turned, :, n * 128 : n * 128 + 128] = full[2 * turned + n].T
            for n in range(2):
                first, second = pltpu.matmul_pop(acc[0][2 * (u % 2) + n]), pltpu.matmul_pop(acc[1][2 * (u % 2) + n])
                for o in range(8):
                    two = jnp.concatenate([first[o * 8 : o * 8 + 8], second[o * 8 : o * 8 + 8]], axis=0).astype(BF16)
                    parts[0, 2 * n + o // 4, o % 4, rows, :] = two[:, :128]
                    parts[1, o % 4, 2 * n + o // 4, rows, :] = two[:, 128:]

        in_turns((CUTS[c + 1] - CUTS[c]) // 2, issue, drain, 2)

    steps = ((0, 1), (1, 3))

    def all_rows(c):
        return pl.ds(CUTS[c] * 8, (CUTS[c + 1] - CUTS[c]) * 8)

    def half_of(c, d):
        span = (CUTS[c + 1] - CUTS[c]) * 4
        return pl.ds(CUTS[c] * 8 + d * span, span)

    def small(c):
        return pl.ds(CUTS[c] * 4, (CUTS[c + 1] - CUTS[c]) * 4)

    def sum1(c):
        for h in range(2):
            p, q = coords[h]
            for d, step in steps:
                start(
                    parts.at[h, turn(q, 2), :, half_of(c, d), :], hop1.at[h, d, :, small(c), :],
                    2, sum_sem.at[0, h, d, c], at(h, 0, step),
                )

    def sum2(c):
        for h in range(2):
            p, q = coords[h]
            for d, step in steps:
                arrived(hop1.at[h, d, :, small(c), :], sum_sem.at[0, h, d, c])
                near = turn(q, step)
                old = parts[h, near, :, half_of(c, d), :].astype(F32)
                parts[h, near, :, half_of(c, d), :] = (old + hop1[h, d, :, small(c), :].astype(F32)).astype(BF16)
                start(
                    parts.at[h, near, :, all_rows(c), :], hop2.at[h, d, :, all_rows(c), :],
                    3, sum_sem.at[1, h, d, c], at(h, 0, step),
                )

    def sum3(c):
        for h in range(2):
            p, q = coords[h]
            rows = all_rows(c)
            for d, step in steps:
                arrived(hop2.at[h, d, :, rows, :], sum_sem.at[1, h, d, c])
            total = parts[h, q, :, rows, :].astype(F32)
            total = total + hop2[h, 0, :, rows, :].astype(F32) + hop2[h, 1, :, rows, :].astype(F32)
            kept[h, :, rows, :] = total.astype(BF16)
            for i, step in enumerate((1, 3, 2)):
                start(
                    kept.at[h, turn(p, step), rows, :], hop3.at[h, i, rows, :],
                    4, sum_sem.at[2, h, i, c], at(h, step, 0),
                )

    leaves = []

    def sum5(c):
        rows = all_rows(c)
        for h in range(2):
            p, q = coords[h]
            total = kept[h, p, rows, :].astype(F32)
            for i in range(3):
                arrived(hop3.at[h, i, rows, :], sum_sem.at[2, h, i, c])
                total = total + hop3[h, i, rows, :].astype(F32)
            sig_ref[rows, pl.ds(h * 128, 128)] = total * (128 ** -0.5)
        leaves.append(pltpu.make_async_copy(sig_ref.at[rows, :], sig_out.at[rows, :], leave_sem.at[c]))
        leaves[-1].start()

    def mix(ks, turning=False):
        none = jnp.zeros((128, 128), BF16)

        def issue(t, u):
            for j in range(2):
                rhs = jnp.concatenate([full[source(ks[j], 2 * t + n)] for n in range(2)], axis=0)
                pltpu.matmul_push_rhs(rhs, u % 2, j)
                for n in range(2):
                    one = left[ks[j], 2 * t + n]
                    lhs = jnp.concatenate([one, none] if n == 0 else [none, one], axis=1)
                    feed(j, 4 * (u % 2) + 2 * n, lhs, u % 2 if n == 0 else None)

        def drain(t, u):
            if turning:
                turned, n, m = CUTS[2] // 2 + t // 4, u % 2, u // 2
                full_t[turned, m * 128 : m * 128 + 128, n * 128 : n * 128 + 128] = full[
                    2 * turned + n, :, m * 128 : m * 128 + 128
                ].T
            for j in range(2):
                for n in range(4):
                    zed[j, t, n * 64 : n * 64 + 64, :] = pltpu.matmul_pop(acc[j][4 * (u % 2) + n]).astype(BF16)

        in_turns(16, issue, drain, 4)

    def renorm(slot):
        @pl.loop(0, 2)
        def _(i):
            for e in range(8):
                for j in range(2):
                    pltpu.matmul_push_rhs(zed[j, 8 * i + e], e % 2, j)
                    feed(j, 0, full_t[8 * i + e], e % 2)

        for j in range(2):
            for n in range(4):
                block[slot + j, n * 64 : n * 64 + 64, :] = (pltpu.matmul_pop(acc[j][n]) * (4096 ** -0.5)).astype(BF16)

    def push(src, dst, kind, recv_sem, target):
        pltpu.make_async_remote_copy(
            src_ref=src, dst_ref=dst, send_sem=send_sem.at[kind], recv_sem=recv_sem,
            device_id=(op, target), device_id_type=MESH,
        ).start()

    def ship(slot, dy, target):
        push(block.at[slot], ren_ref.at[sec], 5, swap_sem.at[dy, core], target)

    def swapped(dy, sender_core):
        sender = turn(y, 4 - dy) * 2 + sender_core
        arrived(ren_ref.at[sender], swap_sem.at[dy, sender_core])

    far = [turn(y, 2) * 2 + j for j in range(2)]
    near = [[turn(y, dy) * 2 + j for dy in (1, 3)] for j in range(2)]
    here = [2 * y + j for j in range(2)]

    sigma_chunk(0)
    sum1(0)
    sigma_chunk(1)
    sum1(1)
    mix(far, turning=True)
    sum2(0)
    renorm(0)
    ship(0, 2, far[0])
    ship(1, 2, far[1])
    sigma_chunk(2)
    sum1(2)
    sum2(1)
    mix(near[0])
    sum3(0)
    renorm(2)
    sum2(2)
    ship(2, 1, near[0][0])
    ship(3, 3, near[0][1])
    mix(near[1])
    sum3(1)
    renorm(4)
    ship(4, 1, near[1][0])
    ship(5, 3, near[1][1])
    sum5(0)
    mix(here)
    sum3(2)
    sum5(1)
    renorm(6)
    ship(7 - core, 0, 2 * y + 1 - core)
    own = pltpu.make_async_copy(block.at[6 + core], ren_ref.at[sec], own_sem)
    own.start()
    sum5(2)
    for dy in (2, 1, 3):
        for c in range(2):
            swapped(dy, c)
    swapped(0, 1 - core)
    own.wait()
    for copy in leaves:
        copy.wait()
    all_sent = (got.at[0, pl.ds(0, 15)], got.at[1, pl.ds(0, 15)], hop1, hop2, hop3, block.at[pl.ds(0, 7)])
    for kind, ref in enumerate(all_sent):
        pltpu.make_async_copy(ref, ref, send_sem.at[kind]).wait()


def with_totals(*refs):
    totals = [pltpu.ACC(unit)((64, 256), F32) for unit in range(2) for _ in range(8)]
    pl.run_scoped(functools.partial(kernel, *refs), *totals)


def finish(sig_ref, ren_ref, sigma_ref, renorm_ref, sig, sigma, narrow, wide, in_sem, out_sem):
    come = [pltpu.make_async_copy(ren_ref.at[i], narrow.at[i], in_sem.at[i]) for i in range(8)]
    come.append(pltpu.make_async_copy(sig_ref, sig, in_sem.at[8]))
    go = [pltpu.make_async_copy(wide.at[i], renorm_ref.at[i], out_sem.at[i]) for i in range(8)]
    go.append(pltpu.make_async_copy(sigma, sigma_ref, out_sem.at[8]))
    for copy in come:
        copy.start()
    for i in range(8):
        come[i].wait()
        wide[i] = narrow[i].astype(F32)
        go[i].start()
    come[8].wait()
    sigma[...] = sig[...].astype(BF16)
    go[8].start()
    for copy in go:
        copy.wait()


def body(psi, left_env, right_env, source, coupling):
    vm = pltpu.VMEM
    sig, ren = pl.pallas_call(
        with_totals,
        out_shape=(jax.ShapeDtypeStruct((256, 256), F32), jax.ShapeDtypeStruct((8, 256, 256), BF16)),
        in_specs=[pl.BlockSpec(memory_space=pl.ANY)] * 5,
        out_specs=(pl.BlockSpec(memory_space=pl.ANY), pl.BlockSpec(memory_space=pl.ANY)),
        scratch_shapes=[
            pltpu.SMEM((8, 32), jnp.int32),
            pltpu.SMEM((8, 32), jnp.int32),
            vm((256, 256), F32),
            vm((8, 32, 128, 128), BF16),
            vm((8, 32, 128, 128), BF16),
            vm((8, 256, 256), BF16),
            vm((2, 16, 128, 256), BF16),
            vm((32, 128, 256), BF16),
            vm((16, 256, 256), BF16),
            vm((8, 32, 128, 256), BF16),
            vm((2, 16, 256, 256), BF16),
            vm((2, 4, 4, 256, 128), BF16),
            vm((8, 256, 256), BF16),
            vm((2, 2, 4, 128, 128), BF16),
            vm((2, 2, 4, 256, 128), BF16),
            vm((2, 4, 256, 128), BF16),
            vm((2, 3, 256, 128), BF16),
            pltpu.SemaphoreType.DMA((13,)),
            pltpu.SemaphoreType.DMA((6,)),
            pltpu.SemaphoreType.DMA((2, 16, 2)),
            pltpu.SemaphoreType.DMA((3, 2, 3, CHUNKS)),
            pltpu.SemaphoreType.DMA((4, 2)),
            pltpu.SemaphoreType.DMA,
            pltpu.SemaphoreType.DMA((CHUNKS,)),
        ],
        compiler_params=pltpu.CompilerParams(
            collective_id=0, has_side_effects=True, vmem_limit_bytes=60 * 1024 * 1024
        ),
        cost_estimate=pl.CostEstimate(flops=13 * 10**9, bytes_accessed=12 * 2**20, transcendentals=0),
        name="dmrg_step",
    )(psi.reshape(256, 256), left_env, right_env.reshape(8, 256, 256), source, coupling)
    sigma, renorm = pl.pallas_call(
        finish,
        out_shape=(jax.ShapeDtypeStruct((256, 256), BF16), jax.ShapeDtypeStruct((8, 256, 256), F32)),
        in_specs=[pl.BlockSpec(memory_space=pl.ANY)] * 2,
        out_specs=(pl.BlockSpec(memory_space=pl.ANY), pl.BlockSpec(memory_space=pl.ANY)),
        scratch_shapes=[
            vm((256, 256), F32),
            vm((256, 256), BF16),
            vm((8, 256, 256), BF16),
            vm((8, 256, 256), F32),
            pltpu.SemaphoreType.DMA((9,)),
            pltpu.SemaphoreType.DMA((9,)),
        ],
        compiler_params=pltpu.CompilerParams(vmem_limit_bytes=60 * 1024 * 1024),
        name="finish",
    )(sig, ren)
    return sigma.reshape(32, 8, 256), renorm[None]


def solution(mesh):
    placed = (
        P("sec", "op", None),
        P("op", "sec", None, None),
        P("op", "sec", None, None),
        P("op", "sec"),
        P("op", "sec"),
    )
    return jax.shard_map(
        body,
        mesh=mesh,
        in_specs=placed,
        out_specs=(P("sec", "op", None), P(("op", "sec"), None, None, None)),
        check_vma=False,
    )
```
